32 devices in a mesh: fsdp: 8 (over z, x), seq: 4 (over y, core).
Axes of the slice: x: 2, y: 2, z: 4, core: 2. Of those that a mesh axis runs over, the one named last changes fastest.
Arguments:
- tokens: bfloat16 [128, 200, 768], P('fsdp', 'seq'), may hold values from -6 to 6
- key_mask: int32 [128, 200], P('fsdp'), may hold values from 0 to 1, as said below
- routes: int32 [128, 200, 2], P('fsdp', 'seq'), may hold values from 0 to 3, all different within a row; in each aligned block of 50 rows (0 to 49, 50 to 99, ..., all dimensions but the last counted through in order) at most 30 rows name the same one
- out_grad: bfloat16 [128, 200, 768], P('fsdp', 'seq'), may hold values from -6 to 6
- norm1_gain: float32 [768], P('fsdp'), may hold values from 0.5 to 1.5
- norm1_bias: float32 [768], P('fsdp'), may hold values from -1.25 to 1.25
- w_qkv: float32 [768, 2304], P('fsdp'), may hold values from -0.21875 to 0.21875
- bias_q: float32 [768], P('fsdp'), may hold values from -1.25 to 1.25
- bias_v: float32 [768], P('fsdp'), may hold values from -1.25 to 1.25
- w_proj: float32 [768, 768], P('fsdp'), may hold values from -0.875 to 0.875
- bias_proj: float32 [768], P('fsdp'), may hold values from -1.25 to 1.25
- norm2_gain: float32 [768], P('fsdp'), may hold values from 0.5 to 1.5
- norm2_bias: float32 [768], P('fsdp'), may hold values from -1.25 to 1.25
- w_router: float32 [768, 4], P('fsdp'), may hold values from -0.15625 to 0.15625
- w_hidden: float32 [4, 3072, 768], P('seq', 'fsdp'), may hold values from -0.21875 to 0.21875
- bias_hidden: float32 [4, 3072], P('seq', 'fsdp'), may hold values from -1.25 to 1.25
- w_expert_out: float32 [4, 3072, 768], P('seq', 'fsdp'), may hold values from -0.625 to 0.625
- bias_expert_out: float32 [4, 768], P('seq', 'fsdp'), may hold values from -3 to 3
Outputs:
- output: bfloat16 [128, 200, 768], P('fsdp', 'seq')
- grad_tokens: bfloat16 [128, 200, 768], P('fsdp', 'seq')
- grad_norm1_gain: float32 [768], P('fsdp')
- grad_norm1_bias: float32 [768], P('fsdp')
- grad_w_qkv: float32 [768, 2304], P('fsdp')
- grad_bias_q: float32 [768], P('fsdp')
- grad_bias_v: float32 [768], P('fsdp')
- grad_w_proj: float32 [768, 768], P('fsdp')
- grad_bias_proj: float32 [768], P('fsdp')
- grad_norm2_gain: float32 [768], P('fsdp')
- grad_norm2_bias: float32 [768], P('fsdp')
- grad_w_router: float32 [768, 4], P('fsdp')
- grad_w_hidden: float32 [4, 3072, 768], P('seq', 'fsdp')
- grad_bias_hidden: float32 [4, 3072], P('seq', 'fsdp')
- grad_w_expert_out: float32 [4, 3072, 768], P('seq', 'fsdp')
- grad_bias_expert_out: float32 [4, 768], P('seq', 'fsdp')
The draws below stay inside these ranges and needn't reach their ends.
Inputs may be any that keep to these rules, and one draw needn't show every extreme that they name: `key_mask`: each image's live positions are its first ones: 1 for at least 175 and at most 199 positions, then 0. `routes`: each row names 2 different experts. In each aligned block of 50 positions of an image no expert is named in more than 30 rows, and in every draw some block has an expert named in exactly 30 rows.
All inputs are finite; a program needn't handle non-finite values.
Results may differ from the reference program's by a relative error of at most 0.02.
Values may be sent and summed in bfloat16 or wider, within the bound.
No kernel may reach another device: no remote copies, remote signals or barrier semaphores. Data moves between devices by JAX's collectives and lax.ppermute only.
A program may use at most 256 MiB of HBM per device.

```python
import math
import jax
import jax.numpy as jnp
import numpy as np
from jax import lax

D = 768
HEADS = 12
HEAD_DIM = 64
FF = 3072
SEQ_LEN = 200
TOP = 2
CAP = 30
IMG_DEV = 16
BLOCK_LEN = 50
IMAGES = 128
EXPERTS = 4
N_SEQ = 4


def draw_key_mask(key, part):
    key = jax.random.fold_in(key, 7)
    lengths = jax.random.randint(key, (IMAGES,), SEQ_LEN - SEQ_LEN // 8, SEQ_LEN)
    positions = jnp.arange(SEQ_LEN, dtype=jnp.int32)
    return (positions[None, :] < lengths[:, None]).astype(jnp.int32)


def spiked(values, rng, source, target, shards_of, factor):
    owner, partner = [(jnp.arange(values.shape[axis_at]) // (values.shape[axis_at] // shards_of)).reshape([-1 if axis == axis_at else 1 for axis in range(values.ndim)]) for axis_at in (source, target)]
    chosen = jax.random.permutation(rng, shards_of)[partner]
    strong = (owner == chosen) | (owner == (partner + shards_of // 2) % shards_of)
    return jnp.where(strong, factor * values, values)


def block_scale(stream_key, extent, shards, least, high):
    gain, own = 1.0, jax.random.fold_in(stream_key, 6)
    for dim, shards_of in shards:
        steps = jnp.exp(jax.random.uniform(jax.random.fold_in(own, dim), (shards_of,), jnp.float32, least / len(shards), high / len(shards)))
        gain = gain * jnp.repeat(steps, extent[dim] // shards_of).reshape([-1 if axis == dim else 1 for axis in range(len(extent))])
    return gain


def deal_out(rng, own, number, rows, count, top, bound, slope):
    sequence = jax.random.permutation(rng, count)
    crowded, common = load_shares(count, rows * top, bound, slope, True), load_shares(count, rows * top, bound, slope, False)
    places = jnp.arange(count)

    def named(sizes, offset_by):
        used = int((sizes > 0).sum())
        fixed = max(1, used // 4)
        passed = fixed + (places - fixed + offset_by * (used - fixed)) % max(1, count - fixed)
        return jnp.zeros((count,), jnp.int32).at[sequence[jnp.where(places < fixed, places, passed)]].set(jnp.asarray(sizes, jnp.int32))

    sizes = jnp.where(number % 4 == 0, named(crowded, number // 4), named(common, number - number // 4 - 1))
    mixed = jax.random.permutation(jax.random.fold_in(own, 3), count)
    source_of, taker = mixed[0:count // 2 * 2:2], mixed[1:count // 2 * 2:2]
    slack = jnp.minimum(sizes[source_of] - 1, bound - sizes[taker]) // 2
    slack = jnp.where((source_of == sequence[0]) | (taker == sequence[0]) | (sizes[taker] == 0), 0, jnp.maximum(slack, 0))
    passed = jax.random.randint(jax.random.fold_in(own, 4), (count // 2,), 0, 1 << 20) % (slack + 1)
    sizes = sizes.at[source_of].add(-passed).at[taker].add(passed)
    labels = jnp.searchsorted(jnp.cumsum(sizes), jnp.arange(rows * top), side="right").astype(jnp.int32)
    listing = labels.reshape(top, rows).T
    listing = listing[jax.random.permutation(jax.random.fold_in(own, 1), rows)]
    offset_by = jax.random.randint(jax.random.fold_in(own, 2), (rows, 1), 0, top)
    return jnp.take_along_axis(listing, (jnp.arange(top)[None, :] + offset_by) % top, axis=1)


def load_shares(number_of, total, reach, skew, full):
    portions = [(1 << 20) // math.isqrt(rank ** skew) + 1 for rank in range(1, number_of + 1)]
    largest = reach if full else min(reach, max(-(-total // number_of), total * portions[0] // sum(portions)))
    least = 1 if total - largest >= number_of - 1 else 0
    given, spare = [largest] + [least] * (number_of - 1), total - largest - least * (number_of - 1)
    while spare > 0:
        candidates = [i for i in range(1, number_of) if given[i] < largest] or [i for i in range(1, number_of) if given[i] < reach]
        mass, budget = sum([portions[i] for i in candidates]), spare
        for i in candidates:
            more = min(reach - given[i], max(1, budget * portions[i] // mass), spare)
            given[i] = given[i] + more
            spare = spare - more
    return np.array(given)


def gaussian(rng, shape, deviation, reach, split=(), kind=jnp.bfloat16):
    values = deviation * jax.random.normal(rng, shape, jnp.float32)
    if split:
        values = values * block_scale(rng, shape, split, -0.22, 0.18)
    return jnp.clip(values, -reach, reach).astype(kind)


def noise_with(key, extent, deviation, reach, shards, heavy, kind=jnp.bfloat16):
    entries = deviation * jax.random.normal(key, extent, jnp.float32)
    if shards:
        entries = entries * block_scale(key, extent, shards, -0.22, 0.18)
    return jnp.clip(spiked(entries, jax.random.fold_in(key, 3), *heavy), -reach, reach).astype(kind)


def setup_inputs(seed: int = 0) -> dict:
    key_list = jax.random.split(jax.random.key(seed), 19)
    tokens = gaussian(key_list[0], (IMAGES, SEQ_LEN, D), 1.0, 6.0, ((0, 8), (1, 4)))
    key_mask = draw_key_mask(jax.random.fold_in(key_list[18], 71), 0)
    routes_keys = jax.random.split(jax.random.fold_in(key_list[2], 1), IMAGES * SEQ_LEN // BLOCK_LEN)
    routes_turns = jax.random.permutation(jax.random.fold_in(key_list[2], 3), IMAGES * SEQ_LEN // BLOCK_LEN)
    routes = jax.vmap(lambda own, number: deal_out(jax.random.fold_in(key_list[2], 2), own, number, BLOCK_LEN, EXPERTS, TOP, CAP, 0))(routes_keys, routes_turns).reshape((IMAGES, SEQ_LEN, TOP))
    out_grad = noise_with(key_list[3], (IMAGES, SEQ_LEN, D), 1.0, 6.0, ((0, 8), (1, 4)), (0, 2, 8, 2.0))
    norm1_gain = jnp.clip(1.0 + 0.1 * jax.random.normal(key_list[4], (D,), jnp.float32), 0.5, 1.5)
    norm1_bias = gaussian(key_list[5], (D,), 0.2, 1.25, ((0, 8),), jnp.float32)
    w_qkv = gaussian(key_list[6], (D, 3 * D), D ** -0.5, 0.21875, ((0, 8),), jnp.float32)
    bias_q = gaussian(key_list[7], (D,), 0.2, 1.25, ((0, 8),), jnp.float32)
    bias_v = gaussian(key_list[8], (D,), 0.2, 1.25, ((0, 8),), jnp.float32)
    w_proj = gaussian(key_list[9], (D, D), (D // 16) ** -0.5, 0.875, ((0, 8),), jnp.float32)
    bias_proj = gaussian(key_list[10], (D,), 0.2, 1.25, ((0, 8),), jnp.float32)
    norm2_gain = jnp.clip(1.0 + 0.1 * jax.random.normal(key_list[11], (D,), jnp.float32), 0.5, 1.5)
    norm2_bias = gaussian(key_list[12], (D,), 0.2, 1.25, ((0, 8),), jnp.float32)
    w_router = gaussian(key_list[13], (D, EXPERTS), (2 * D) ** -0.5, 0.15625, ((0, 8),), jnp.float32)
    w_hidden = gaussian(key_list[14], (EXPERTS, FF, D), D ** -0.5, 0.21875, ((0, 4), (1, 8)), jnp.float32)
    bias_hidden = gaussian(key_list[15], (EXPERTS, FF), 0.2, 1.25, ((0, 4), (1, 8)), jnp.float32)
    w_expert_out = gaussian(key_list[16], (EXPERTS, FF, D), (FF // 32) ** -0.5, 0.625, ((0, 4), (1, 8)), jnp.float32)
    bias_expert_out = gaussian(key_list[17], (EXPERTS, D), 0.5, 3.0, ((0, 4), (1, 8)), jnp.float32)
    return {"tokens": tokens, "key_mask": key_mask, "routes": routes, "out_grad": out_grad, "norm1_gain": norm1_gain, "norm1_bias": norm1_bias, "w_qkv": w_qkv, "bias_q": bias_q, "bias_v": bias_v, "w_proj": w_proj, "bias_proj": bias_proj, "norm2_gain": norm2_gain, "norm2_bias": norm2_bias, "w_router": w_router, "w_hidden": w_hidden, "bias_hidden": bias_hidden, "w_expert_out": w_expert_out, "bias_expert_out": bias_expert_out}


@jax.custom_vjp
def low(v):
    return lax.optimization_barrier(v.astype(jnp.bfloat16)).astype(jnp.float32)

@jax.custom_vjp
def low_back(v):
    return v

def low_keep(v):
    return (low(v), None)

def low_pass(kept, grad):
    return (grad,)

def back_keep(v):
    return (v, None)

def back_low(kept, grad):
    return (low(grad),)
low.defvjp(low_keep, low_pass)
low_back.defvjp(back_keep, back_low)
norm_eps = 1e-06

def contract(form, left, right):
    return jnp.einsum(form, left, right, precision=lax.Precision.HIGHEST)

def layer_norm(values, gain_vec, shift_vec):
    center = values - lax.optimization_barrier(jnp.mean(values, axis=-1, keepdims=True))
    scaled = center * lax.rsqrt(lax.optimization_barrier(jnp.mean(center * center, axis=-1, keepdims=True)) + norm_eps)
    return scaled * gain_vec + shift_vec

def softmax_last(scores):
    shifted = jnp.exp(scores - lax.optimization_barrier(jnp.max(scores, axis=-1, keepdims=True)))
    return shifted / lax.optimization_barrier(jnp.sum(shifted, axis=-1, keepdims=True))

def group_forward(params, tokens_g, mask_g, routes_g):
    gain_one, shift_one, qkv_weight, query_bias, value_bias, proj_weight, proj_bias, gain_two, shift_two, router_weight, in_weight, in_bias, out_weight, out_bias = params
    img_count = tokens_g.shape[0]
    block_len = SEQ_LEN // N_SEQ
    normed = low(layer_norm(tokens_g, gain_one, shift_one))
    bias_all = jnp.concatenate([query_bias, jnp.zeros_like(query_bias), value_bias])
    qkv_all = low(low_back(contract('gld,de->gle', normed, qkv_weight) + bias_all))
    qkv_all = qkv_all.reshape(img_count, SEQ_LEN, 3, HEADS, HEAD_DIM)
    scores = low_back(contract('gqhe,gkhe->ghqk', qkv_all[:, :, 0], qkv_all[:, :, 1]) * HEAD_DIM ** (-0.5))
    scores = jnp.where(mask_g[:, None, None, :] > 0, scores, -1000000000.0)
    probs_low = low(softmax_last(scores))
    attended = contract('ghqk,gkhe->gqhe', probs_low, qkv_all[:, :, 2]).reshape(img_count, SEQ_LEN, D)
    attended = low(low_back(attended))
    residual = tokens_g + low_back(contract('gld,de->gle', attended, proj_weight) + proj_bias)
    z_vals = low(layer_norm(residual, gain_two, shift_two))
    router = softmax_last(low_back(contract('gld,de->gle', z_vals, router_weight)))
    choose = (routes_g[..., None] == jnp.arange(EXPERTS, dtype=jnp.int32)).astype(jnp.float32)
    gate_vals = lax.optimization_barrier(jnp.sum(router[:, :, None, :] * choose, axis=-1))
    flat_hits = choose.reshape(img_count, N_SEQ, block_len * TOP, EXPERTS)
    before = jnp.cumsum(flat_hits, axis=2) - flat_hits
    slot_rank = lax.optimization_barrier(jnp.sum(before * flat_hits, axis=-1)).astype(jnp.int32)
    slot_ids = routes_g.reshape(img_count, N_SEQ, block_len * TOP) * CAP + slot_rank
    onehot = (slot_ids[..., None] == jnp.arange(EXPERTS * CAP, dtype=jnp.int32)).astype(jnp.float32)
    onehot = onehot.reshape(img_count, N_SEQ, block_len, TOP, EXPERTS * CAP)
    z_blocks = z_vals.reshape(img_count, N_SEQ, block_len, D)
    slots_in = low_back(contract('gnbts,gnbd->gnsd', onehot, z_blocks))
    slots_in = slots_in.reshape(img_count, N_SEQ, EXPERTS, CAP, D)
    pre_act = low_back(contract('gnecd,efd->gnecf', slots_in, in_weight) + in_bias[None, None, :, None, :])
    hidden = low(jax.nn.gelu(pre_act, approximate=False))
    expert_out = low(low_back(contract('gnecf,efd->gnecd', hidden, out_weight) + out_bias[None, None, :, None, :]))
    picked = contract('gnbts,gnsd->gnbtd', onehot, expert_out.reshape(img_count, N_SEQ, EXPERTS * CAP, D))
    gates_blocks = gate_vals.reshape(img_count, N_SEQ, block_len, TOP, 1)
    mixture = lax.optimization_barrier(jnp.sum(picked * gates_blocks, axis=3)).reshape(img_count, SEQ_LEN, D)
    return (residual + mixture) * mask_g[:, :, None].astype(jnp.float32)

def reference(tokens, key_mask, routes, out_grad, norm1_gain, norm1_bias, w_qkv, bias_q, bias_v, w_proj, bias_proj, norm2_gain, norm2_bias, w_router, w_hidden, bias_hidden, w_expert_out, bias_expert_out):
    masters = (norm1_gain, norm1_bias, w_qkv, bias_q, bias_v, w_proj, bias_proj, norm2_gain, norm2_bias, w_router, w_hidden, bias_hidden, w_expert_out, bias_expert_out)
    groups = IMAGES // IMG_DEV
    mask_groups = key_mask.reshape(groups, IMG_DEV, SEQ_LEN)
    route_groups = routes.reshape(groups, IMG_DEV, SEQ_LEN, TOP)

    def forward(tokens_f, *weights):
        params = tuple((low(weight) for weight in weights))

        def run_group(packed):
            return group_forward(params, packed[0], packed[1], packed[2])
        result = lax.map(jax.checkpoint(run_group), (tokens_f.reshape(groups, IMG_DEV, SEQ_LEN, D), mask_groups, route_groups))
        return result.reshape(IMAGES, SEQ_LEN, D)
    result, pullback = jax.vjp(forward, tokens.astype(jnp.float32), *masters)
    gradients = pullback(out_grad.astype(jnp.float32))
    return (result.astype(jnp.bfloat16), gradients[0].astype(jnp.bfloat16), gradients[1], gradients[2], gradients[3], gradients[4], gradients[5], gradients[6], gradients[7], gradients[8], gradients[9], gradients[10], gradients[11], gradients[12], gradients[13], gradients[14])
```

```python
import functools

import jax
import jax.numpy as jnp
from jax import lax
from jax.experimental import pallas as pl
from jax.experimental.pallas import tpu as pltpu
from jax.sharding import PartitionSpec as P

HEAD_DIM = 64
TOP = 2
CAP = 30
TILE = 4
EPS = 1e-06
NEG = -1e30
BF = jnp.bfloat16
F32 = jnp.float32
VMEM = 60 * 1024 * 1024


def nn(a, b):
    return jnp.dot(a, b, preferred_element_type=F32)


def nt(a, b):
    return lax.dot_general(a, b, (((1,), (1,)), ((), ())), preferred_element_type=F32)


def tn(a, b):
    return lax.dot_general(a, b, (((0,), (0,)), ((), ())), preferred_element_type=F32)


def stats(v):
    center = v - jnp.mean(v, axis=-1, keepdims=True)
    r = lax.rsqrt(jnp.mean(center * center, axis=-1, keepdims=True) + EPS)
    return center * r, r


def norm_back(u, gain, vhat, r):
    ug = u * gain
    return r * (
        ug
        - jnp.mean(ug, axis=-1, keepdims=True)
        - vhat * jnp.mean(ug * vhat, axis=-1, keepdims=True)
    )


def rows_of(refs, i=0):
    return jnp.concatenate([ref[i].astype(F32) for ref in refs], axis=0)


def params(**kw):
    return pltpu.CompilerParams(vmem_limit_bytes=VMEM, **kw)


def cost(us):
    return pl.CostEstimate(flops=int(us * 1e9), bytes_accessed=int(us * 1e4), transcendentals=0)


def half_masks():
    lane = lax.broadcasted_iota(jnp.int32, (1, 2 * HEAD_DIM), 1)
    first = (lane < HEAD_DIM).astype(F32)
    return first, 1.0 - first


def fwd_kernel(parts, *refs):
    toks, refs = refs[:parts], refs[parts:]
    mask_ref, w_ref, vec_ref, qkv_ref, att_ref, lse_ref, res_ref, z_ref, normed_ref = refs[:9]
    sends = refs[9:]
    x = rows_of(toks)
    d = x.shape[1]
    vec = vec_ref[...]
    vhat, _ = stats(x)
    normed = (vhat * vec[0:1] + vec[1:2]).astype(BF)
    normed_ref[0] = normed
    qkv_ref[0, :, 0:d] = (nn(normed, w_ref[:, 0:d]) + vec[2:3]).astype(BF)
    qkv_ref[0, :, d : 2 * d] = nn(normed, w_ref[:, d : 2 * d]).astype(BF)
    qkv_ref[0, :, 2 * d : 3 * d] = (nn(normed, w_ref[:, 2 * d : 3 * d]) + vec[3:4]).astype(BF)
    bias = mask_ref[0]
    first, second = half_masks()
    scale = HEAD_DIM ** (-0.5)
    lane = lax.broadcasted_iota(jnp.int32, (x.shape[0], 128), 1)
    lse = jnp.zeros((x.shape[0], 128), F32)
    for pair in range(d // 128):
        q2 = qkv_ref[0, :, 128 * pair : 128 * pair + 128]
        k2 = qkv_ref[0, :, d + 128 * pair : d + 128 * pair + 128]
        v2 = qkv_ref[0, :, 2 * d + 128 * pair : 2 * d + 128 * pair + 128]
        outs = []
        for a, half in enumerate((first, second)):
            qa = q2 * (half * scale).astype(BF)
            s = nt(qa, k2) + bias
            top = jnp.max(s, axis=-1, keepdims=True)
            e = jnp.exp(s - top)
            total = jnp.sum(e, axis=-1, keepdims=True)
            outs.append(nn(e.astype(BF), v2) * (1.0 / total))
            lse = jnp.where(lane == 2 * pair + a, top + jnp.log(total), lse)
        att = jnp.where(first > 0, outs[0], outs[1])
        att_ref[0, :, 128 * pair : 128 * pair + 128] = att.astype(BF)
    lse_ref[0] = lse
    res = x + nn(att_ref[0], w_ref[:, 3 * d : 4 * d]) + vec[4:5]
    res_ref[0] = res
    zhat, _ = stats(res)
    z_ref[0] = (zhat * vec[5:6] + vec[6:7]).astype(BF)
    block = x.shape[0] // parts
    for j, ref in enumerate(sends):
        ref[0] = res[j * block : (j + 1) * block].astype(BF)


def spread(row, slots, values):
    length = values.shape[0]
    hot = (lax.broadcasted_iota(jnp.int32, (slots, length), 0) == row).astype(BF)
    return nn(hot, values)


def gather_grads_kernel(slots, parts, ids_ref, slot_ref, *refs):
    out = []
    for i in range(TILE):
        values = rows_of(refs[:parts], i).astype(BF)
        out.append(spread(slot_ref[i], slots, values))
    refs[parts][0] = jnp.concatenate(out, axis=0).astype(BF)


def router_probs(rows, router, experts):
    logits = nn(rows, router)
    lane = lax.broadcasted_iota(jnp.int32, logits.shape, 1)
    logits = jnp.where(lane < experts, logits, NEG)
    e = jnp.exp(logits - jnp.max(logits, axis=-1, keepdims=True))
    return e / jnp.sum(e, axis=-1, keepdims=True), lane


def gather_rows_kernel(slots, experts, ids_ref, slot_ref, z_ref, g_ref, router_ref, *refs):
    x_ref, gr_ref = refs[-2:]
    out = [spread(slot_ref[i], slots, z_ref[i]) for i in range(TILE)]
    x = jnp.concatenate(out, axis=0).astype(BF)
    probs, lane = router_probs(x, router_ref[...], experts)
    gate = jnp.sum(jnp.where(lane == ids_ref[0], probs, 0.0), axis=-1, keepdims=True)
    x_ref[0] = x
    gr_ref[0] = (gate * g_ref[0].astype(F32)).astype(BF)


def gelu_parts(v):
    e = jnp.exp(-0.5 * v * v)
    den = 1.0 + 0.23164189 * jnp.abs(v)
    t = pl.reciprocal(den, approx=True)
    t = t * (2.0 - den * t)
    poly = t * (
        0.127414796 + t * (-0.142248368 + t * (0.7107068705 + t * (-0.7265760135 + t * 0.5307027145)))
    )
    tail = poly * e
    cdf = jnp.where(v >= 0, 1.0 - tail, tail)
    return v * cdf, cdf + v * (0.3989422804 * e)


def expert_kernel(first, last, slots, experts, fs, *refs):
    e0, e1, x_ref, gr_ref = refs[:4]
    refs = list(refs[4:])
    if not first:
        acc_out_in, acc_gx_in = refs[:2]
        refs = refs[2:]
    if last:
        g_ref, bo_ref, refs = refs[0], refs[1], refs[2:]
    p0, p1, acc_out = refs[:3]
    gx_refs, refs = refs[3:-7], refs[-7:]
    wh, wo, gwh, gwo, gbh, gbo, bias = refs
    step = pl.program_id(0)

    @pl.when(step == 0)
    def _():
        wh[0:fs] = e0[0:fs]
        wh[fs : 2 * fs] = e1[0:fs]
        wo[0:fs] = e0[fs : 2 * fs]
        wo[fs : 2 * fs] = e1[fs : 2 * fs]
        both = [e[2 * fs : 2 * fs + 16, 0:fs].astype(F32)[0:8] for e in (e0, e1)]
        bias[...] = jnp.concatenate(both, axis=1)
        gwh[...] = jnp.zeros_like(gwh)
        gwo[...] = jnp.zeros_like(gwo)
        gbh[...] = jnp.zeros_like(gbh)
        gbo[...] = jnp.zeros_like(gbo)

    x = x_ref[0]
    gr = gr_ref[0]
    pre = nt(x, wh[...]) + bias[0:1]
    act, slope = gelu_parts(pre)
    hidden = act.astype(BF)
    out = nn(hidden, wo[...])
    grad_pre_f = nt(gr, wo[...]) * slope
    grad_pre = grad_pre_f.astype(BF)
    gx = nn(grad_pre, wh[...])
    gwo[...] += tn(hidden, gr)
    gwh[...] += tn(grad_pre, x)
    gbh[0:1] += jnp.sum(grad_pre_f, axis=0, keepdims=True)
    gbo[0:1] += jnp.sum(gr.astype(F32), axis=0, keepdims=True)
    if not first:
        out = out + acc_out_in[0]
        gx = gx + acc_gx_in[0]
    acc_out[0] = out
    if last:
        dots = jnp.sum((out + bo_ref[7:8]) * g_ref[0].astype(F32), axis=-1, keepdims=True)
        sub = lax.broadcasted_iota(jnp.int32, (8, x.shape[1]), 0)
        fill = jnp.zeros((128 - slots, 128), F32)
        wide_fill = jnp.zeros((8, x.shape[1] - 128), F32)
        out_rows = []
        for i in range(TILE):
            col = jnp.broadcast_to(dots[i * slots : (i + 1) * slots], (slots, 128))
            row = jnp.concatenate([col, fill], axis=0).T[0:8]
            row = jnp.concatenate([row, wide_fill], axis=1)
            high = row.astype(BF).astype(F32)
            row = jnp.where(sub == 0, high, jnp.where(sub == 1, row - high, 0.0))
            out_rows += [gx[i * slots : (i + 1) * slots], row]
        gx = jnp.concatenate(out_rows, axis=0).reshape(TILE, slots + 8, -1).astype(BF)
        for k, ref in enumerate(gx_refs):

            @pl.when(step // (pl.num_programs(0) // len(gx_refs)) == k)
            def _(ref=ref):
                ref[...] = gx
    else:
        gx_refs[0][0] = gx

    @pl.when(step == pl.num_programs(0) - 1)
    def _():
        d = gwh.shape[1]
        for i, pack in enumerate((p0, p1)):
            pack[0:fs] = gwh[i * fs : (i + 1) * fs].astype(BF)
            pack[fs : 2 * fs] = gwo[i * fs : (i + 1) * fs].astype(BF)
            row = jnp.broadcast_to(gbh[0:1, i * fs : (i + 1) * fs], (16, fs))
            row = jnp.concatenate([row, jnp.zeros((16, d - fs), F32)], axis=1)
            sub = lax.broadcasted_iota(jnp.int32, (16, d), 0)
            pack[2 * fs : 2 * fs + 16] = jnp.where(
                sub == 0, row, jnp.where(sub == 1, gbo[0:1], 0.0)
            ).astype(BF)


def weigh_kernel(slots, experts, ids_ref, out_ref, x_ref, router_ref, bo_ref, perm_ref, *mixed_refs):
    x = x_ref[0]
    out = out_ref[0] + bo_ref[7:8]
    probs, lane = router_probs(x, router_ref[...], experts)
    gate = jnp.sum(jnp.where(lane == ids_ref[0], probs, 0.0), axis=-1, keepdims=True)
    weighted = nn(perm_ref[...], (gate * out).astype(BF))
    count = weighted.shape[0] // len(mixed_refs)
    for k, ref in enumerate(mixed_refs):
        ref[0] = weighted[k * count : (k + 1) * count].astype(BF)


def combine_kernel(parts, ids_ref, meta_ref, *refs):
    res, rows, out_ref = refs[:parts], refs[parts : 2 * parts], refs[2 * parts]
    step = pl.program_id(0)
    block, length = meta_ref.shape[1], out_ref.shape[1]
    meta = meta_ref[...].reshape(TILE * block, 8)
    total = 0.0
    for k, ref in enumerate(rows):
        slot = lax.broadcasted_iota(jnp.int32, (TILE * block, ref.shape[1]), 1)
        total += nn((slot == meta[:, k : k + 1]).astype(BF), ref[0])
    live = meta[:, 4:5].astype(F32)
    for j in range(parts):

        @pl.when(step == j)
        def _(j=j):
            base = res[j][...].astype(F32).reshape(TILE * block, -1)
            out = ((base + total) * live).reshape(TILE, block, -1)
            out_ref[...] = out[:, :length].astype(BF)


def norm_part(parts, experts, slots, refs, accs, ids_ref, i):
    meta_ref, gx_refs, g_refs, att_ref, res_ref, z_ref, w_ref, vec_ref, router_ref = refs
    acc_proj, acc_small, acc_router = accs
    length, d = res_ref.shape[1:]
    meta = meta_ref[0]
    lane = lax.broadcasted_iota(jnp.int32, (length, 128), 1)
    dz = jnp.zeros((length, d), F32)
    grad_probs = jnp.zeros((length, 128), F32)
    for k in range(parts):
        hot = lane == meta[:, k : k + 1]
        dz += nn(hot.astype(BF), gx_refs[k][0])
        dots = gx_refs[k][0, slots - 8 : slots + 8, 0:128].astype(F32)
        dots = dots[8:9] + dots[9:10]
        of_token = jnp.sum(jnp.where(hot, dots, 0.0), axis=-1, keepdims=True)
        grad_probs = jnp.where(lane == (ids_ref[0] ^ k), of_token, grad_probs)
    z = z_ref[0]
    probs, _ = router_probs(z, router_ref[...], experts)
    grad_logits = probs * (grad_probs - jnp.sum(probs * grad_probs, axis=-1, keepdims=True))
    grad_logits = grad_logits.astype(BF)
    dz += nt(grad_logits, router_ref[...])
    acc_router[...] += tn(z, grad_logits)
    zhat, r2 = stats(res_ref[0])
    acc_small[5:6] += jnp.sum(dz * zhat, axis=0, keepdims=True)
    acc_small[6:7] += jnp.sum(dz, axis=0, keepdims=True)
    grad_res = rows_of(g_refs) + norm_back(dz, vec_ref[5:6], zhat, r2)
    branch = grad_res.astype(BF)
    acc_small[4:5] += jnp.sum(branch.astype(F32), axis=0, keepdims=True)
    acc_proj[...] += tn(att_ref[0], branch)
    return grad_res, nt(branch, w_ref[...]).astype(BF)


def heads_part(half, mask_ref, qkv_refs, att_ref, ga_ref, lse_ref, normed_ref, w_refs, acc, acc_small, gqkv):
    q_ref, k_ref, v_ref = qkv_refs
    width = q_ref.shape[2]
    spot = half * width
    bias = mask_ref[0]
    lse = lse_ref[0]
    first, second = half_masks()
    scale = HEAD_DIM ** (-0.5)
    for pair in range(width // 128):
        at = 128 * pair
        here = slice(spot + at, spot + at + 128)
        q2 = q_ref[0, :, at : at + 128]
        k2 = k_ref[0, :, at : at + 128]
        v2 = v_ref[0, :, at : at + 128]
        g2 = ga_ref[0, :, here]
        prod = g2.astype(F32) * att_ref[0, :, here].astype(F32)
        gq, gk, gv = [], 0.0, 0.0
        for a, mask in enumerate((first, second)):
            qa = q2 * (mask * scale).astype(BF)
            ga = g2 * mask.astype(BF)
            head = half * (width // HEAD_DIM) + 2 * pair + a
            probs = jnp.exp(nt(qa, k2) + bias - lse[:, head : head + 1])
            delta = jnp.sum(prod * mask, axis=-1, keepdims=True)
            grad_scores = (probs * (nt(ga, v2) - delta)).astype(BF)
            gq.append(nn(grad_scores, k2))
            gk += tn(grad_scores, qa)
            gv += tn(probs.astype(BF), ga)
        gqkv[:, at : at + 128] = (jnp.where(first > 0, gq[0], gq[1]) * scale).astype(BF)
        gqkv[:, width + at : width + at + 128] = gk.astype(BF)
        gqkv[:, 2 * width + at : 2 * width + at + 128] = gv.astype(BF)
    acc_small[2:3, spot : spot + width] += jnp.sum(
        gqkv[:, 0:width].astype(F32), axis=0, keepdims=True
    )
    acc_small[3:4, spot : spot + width] += jnp.sum(
        gqkv[:, 2 * width : 3 * width].astype(F32), axis=0, keepdims=True
    )
    acc[...] += tn(normed_ref[0], gqkv[...])
    return sum(
        nt(gqkv[:, n * width : (n + 1) * width], w_ref[...]) for n, w_ref in enumerate(w_refs)
    )


def split_rows(outs, accs, core):
    col = 0
    for acc in accs:
        cols = slice(col, col + acc.shape[1])
        col += acc.shape[1]
        if len(outs) == 1:
            outs[0][:, cols] = acc[...].astype(BF)
            continue
        for out, which in zip(outs, (core, 1 - core)):
            shards, sides, count = out.shape[:3]
            for n in range(shards * sides):
                row = pl.multiple_of((2 * n + which) * count, 8)
                out[n // sides, n % sides, :, cols] = acc[pl.ds(row, count)].astype(BF)


def taker(refs):
    refs = list(refs)

    def take(n):
        out = refs[:n]
        del refs[:n]
        return out

    return take


def back_first_kernel(parts, experts, slots, outs, ids_ref, *refs):
    take = taker(refs)
    (meta_ref,) = take(1)
    norm_refs = [meta_ref, take(parts), take(parts)]
    att_ref, res_ref, z_ref, wp_ref, vec_ref, router_ref = take(6)
    norm_refs += [att_ref, res_ref, z_ref, wp_ref, vec_ref, router_ref]
    (mask_ref,) = take(1)
    qkv_refs = take(3)
    lse_ref, normed_ref = take(2)
    w_refs = take(3)
    ga_ref, gres_ref, dn_ref, small_ref = take(4)
    grads_refs = take(outs)
    acc_proj, acc, acc_small, acc_router, gqkv = take(5)
    i = pl.program_id(0)

    @pl.when(i == 0)
    def _():
        for part in (acc_proj, acc, acc_small, acc_router):
            part[...] = jnp.zeros_like(part)

    accs = (acc_proj, acc_small, acc_router)
    gres_ref[0], ga_ref[0] = norm_part(parts, experts, slots, norm_refs, accs, ids_ref, i)
    dn_ref[0] = heads_part(
        0, mask_ref, qkv_refs, att_ref, ga_ref, lse_ref, normed_ref, w_refs, acc, acc_small, gqkv
    )

    @pl.when(i == pl.num_programs(0) - 1)
    def _():
        acc_small[8:16] = acc_router[...].T[0:8]
        small_ref[...] = acc_small[...]
        split_rows(grads_refs, (acc_proj, acc), ids_ref[0] % 2)


def back_second_kernel(parts, outs, ids_ref, *refs):
    take = taker(refs)
    (mask_ref,) = take(1)
    qkv_refs = take(3)
    att_ref, ga_ref, lse_ref, normed_ref = take(4)
    w_refs = take(3)
    small_in, dn_in, gres_ref, vec_ref = take(4)
    toks, gt_refs = take(parts), take(parts)
    grads_refs = take(outs)
    acc, acc_small, acc_turned, gqkv = take(4)
    i = pl.program_id(0)

    @pl.when(i == 0)
    def _():
        acc[...] = jnp.zeros_like(acc)
        acc_small[0:16] = small_in[...]
        acc_small[16:128] = jnp.zeros((112, acc_small.shape[1]), F32)

    dn = dn_in[0] + heads_part(
        1, mask_ref, qkv_refs, att_ref, ga_ref, lse_ref, normed_ref, w_refs, acc, acc_small, gqkv
    )
    x = rows_of(toks)
    vhat, r1 = stats(x)
    acc_small[0:1] += jnp.sum(dn * vhat, axis=0, keepdims=True)
    acc_small[1:2] += jnp.sum(dn, axis=0, keepdims=True)
    grad_tok = gres_ref[0] + norm_back(dn, vec_ref[0:1], vhat, r1)
    block = x.shape[0] // parts
    for j, ref in enumerate(gt_refs):
        ref[0] = grad_tok[j * block : (j + 1) * block].astype(BF)

    @pl.when(i == pl.num_programs(0) - 1)
    def _():
        acc_turned[...] = acc_small[...].T
        split_rows(grads_refs, (acc, acc_turned), ids_ref[0] % 2)


def assemble_kernel(ring_len, half, share, ids_ref, *refs):
    parts, (out_ref, vec_ref, router_ref) = refs[:-3], refs[-3:]
    ring_at, column = ids_ref[1] // 2, ids_ref[1] % 2
    core = ids_ref[0] % 2
    d = vec_ref.shape[1]
    vec = jnp.zeros((16, d), F32)
    at = 0
    for r in range(ring_len):
        for p in range(2):
            shard = lax.rem(ring_at + ring_len - r, ring_len) * 2 + (column ^ p)
            for c in range(2):
                row = pl.multiple_of((shard * 2 + (core ^ c)) * half, half)
                out_ref[pl.ds(row, half)] = parts[at][0:half]
                if c == 0:
                    few = parts[at][half : half + 8, 0:256].astype(F32)
                    few = jnp.concatenate([few[:, 0:128], few[:, 128:256]], axis=0).astype(BF)
                    source = lax.broadcasted_iota(jnp.int32, (128, d), 0)
                    target = lax.broadcasted_iota(jnp.int32, (128, d), 1) - shard * share
                    vec += nn(few, ((source == target) & (source < share)).astype(BF))
                at += 1
    vec_ref[...] = vec
    fill = jnp.zeros((120, d), F32)
    router_ref[...] = jnp.concatenate([vec[8:16], fill], axis=0).T.astype(BF)


def whole(shape):
    return pl.BlockSpec(shape, lambda *_: (0,) * len(shape))


def body(
    tokens,
    key_mask,
    routes,
    out_grad,
    norm1_gain,
    norm1_bias,
    w_qkv,
    bias_q,
    bias_v,
    w_proj,
    bias_proj,
    norm2_gain,
    norm2_bias,
    w_router,
    w_hidden,
    bias_hidden,
    w_expert_out,
    bias_expert_out,
):
    images, block_len, d = tokens.shape
    parts = lax.axis_size("seq")
    shards = lax.axis_size("fsdp")
    experts = parts
    ring_len = shards // 2
    own = images // parts
    sub = own // TILE
    tiles = parts * sub
    pad = -(-block_len // 8) * 8
    length = parts * pad
    slots = parts * CAP
    rows = TILE * slots
    fs = w_hidden.shape[1]
    share = d // shards
    half = share // 2
    me = lax.axis_index("seq")
    rank = lax.axis_index("fsdp")
    ring_at, column = rank // 2, rank % 2
    core = me % 2
    ids = jnp.stack([me, rank]).astype(jnp.int32)

    def to_seq(v, k):
        return lax.ppermute(v, "seq", [(n, n ^ k) for n in range(parts)])

    def to_column(v):
        return lax.ppermute(v, "fsdp", [(n, n ^ 1) for n in range(shards)])

    def round_ring(v):
        return lax.ppermute(v, "fsdp", [(n, (n + 2) % shards) for n in range(shards)])

    def gate(*values):
        return lax.optimization_barrier(values)

    def after(v, *others):
        return lax.optimization_barrier((v,) + others)[0]

    def index(v, at, axis=0):
        return lax.dynamic_index_in_dim(v, at, axis, keepdims=False)

    def share_seq(v):
        two = to_seq(v, 2)
        return [v, to_seq(v, 1), two, to_seq(two, 1)]

    order = jnp.arange(shards, dtype=jnp.int32)
    spot = 2 * ((ring_at - order // 2) % ring_len) + (order % 2 ^ column)

    wide = 4 * d
    masters = (
        norm1_gain,
        norm1_bias,
        bias_q,
        bias_v,
        bias_proj,
        norm2_gain,
        norm2_bias,
    )
    few = jnp.concatenate([jnp.stack(masters), bias_expert_out, w_router.T], axis=0)
    few = jnp.pad(few, ((0, 16 - few.shape[0]), (0, 128 - share))).astype(BF)
    few_row = jnp.concatenate([few[:8], few[8:]], axis=1)
    few_row = jnp.pad(few_row, ((0, 0), (0, wide - 256)))
    both = jnp.concatenate([w_qkv, w_proj], axis=1)

    def half_rows(which):
        part = lax.dynamic_slice_in_dim(both, which * half, half, 0).astype(BF)
        return jnp.concatenate([part, few_row], axis=0)

    now, now_core = half_rows(core), half_rows(1 - core)
    tokens, routes, out_grad = lax.optimization_barrier((tokens, routes, out_grad, now))[:3]

    grow = ((0, 0), (0, pad - block_len), (0, 0))
    padded = jnp.pad(tokens, grow)
    pieces = [lax.dynamic_slice_in_dim(padded, (me ^ j) * own, own, 0) for j in range(parts)]
    toks = [pieces[j] if j == 0 else to_seq(pieces[j], j) for j in range(parts)]

    spare = jnp.zeros((15, d), F32)
    def build_pack():
      return jnp.concatenate(
        [
            w_hidden[0],
            w_expert_out[0],
            jnp.pad(bias_hidden, ((0, 0), (0, d - fs))),
            spare,
        ],
        axis=0,
    ).astype(BF)
    own_live = lax.dynamic_slice_in_dim(key_mask, me * block_len, block_len, 1)

    def build_final():
        return jnp.pad(out_grad * own_live[:, :, None].astype(BF), grow)


    flat = jnp.pad(
        routes.reshape(images, block_len * TOP), ((0, 0), (0, (-block_len * TOP) % 128))
    )
    blocks = jnp.stack(share_seq(flat))[:, :, : block_len * TOP]
    blocks = blocks.reshape(parts, images, block_len, TOP)
    names = me ^ jnp.arange(parts, dtype=jnp.int32)
    hit = jnp.any(blocks[..., None] == names, axis=3)
    ahead = (
        lax.broadcasted_iota(jnp.int32, (block_len, block_len), 0)
        < lax.broadcasted_iota(jnp.int32, (block_len, block_len), 1)
    ).astype(BF)
    ranks = jnp.einsum(
        "jitk,tu->jiuk", hit.astype(BF), ahead, preferred_element_type=F32
    ).astype(jnp.int32)
    in_image = jnp.where(hit, ranks + (names * CAP)[:, None, None, None], -1)
    in_image = jnp.pad(
        in_image, ((0, 0), (0, 0), (0, pad - block_len), (0, 0)), constant_values=-1
    )
    own_meta = lax.dynamic_slice_in_dim(in_image, me * own, own, 1)
    own_meta = own_meta.transpose(1, 0, 2, 3).reshape(own, length, parts)
    expert_slot = in_image[..., 0]

    def by_image(order):
        out = jnp.concatenate([expert_slot[j] for j in order], axis=-1)
        return out.reshape(images, 1, length)

    slot_rows = [by_image([j ^ k for j in range(parts)]) for k in range(parts)]
    within = (jnp.arange(images, dtype=jnp.int32) % TILE) * CAP
    mix_slot = jnp.where(hit[0], ranks[0] + within[:, None, None], -1)
    mix_meta = jnp.concatenate([mix_slot, own_live[:, :, None]], axis=-1)
    mix_meta = jnp.pad(
        mix_meta, ((0, 0), (0, pad - block_len), (0, 8 - parts - 1)), constant_values=-1
    )
    seen = lax.dynamic_slice_in_dim(key_mask, me * own, own, 0).reshape(own, parts, block_len)
    seen = jnp.stack([index(seen, me ^ j, 1) for j in range(parts)], axis=1)
    seen = jnp.pad(seen, ((0, 0), (0, 0), (0, pad - block_len))).reshape(own, 1, length)
    mask_bias = jnp.where(seen > 0, 0.0, NEG).astype(F32)

    at = lax.broadcasted_iota(jnp.int32, (rows, rows), 0)
    image_at, rank_at = (at % (TILE * CAP)) // CAP, at % CAP
    source = image_at * slots + ((at // (TILE * CAP)) ^ me) * CAP + rank_at
    reorder = (lax.broadcasted_iota(jnp.int32, (rows, rows), 1) == source).astype(BF)

    halves, others = [], []
    for r in range(ring_len):
        if r:
            if r == 2:
                now, w_hidden, w_expert_out, out_grad, others[0] = gate(
                    now, w_hidden, w_expert_out, out_grad, others[0], *pieces
                )[:5]
                pack, final = build_pack(), build_final()
            elif r == 3:
                now, others[1], pack, final, *toks[1:] = gate(
                    now, others[1], pack, final, *toks[1:]
                )
            elif r > 3:
                now, others[r - 2] = gate(now, others[r - 2])
            now = round_ring(now)
            arrived = now
            if r == ring_len - 1:
                grads_in = [final, None, to_seq(final, 2), None]
                now, mask_bias, own_meta, mix_meta, reorder, *slot_rows = gate(
                    now, mask_bias, own_meta, mix_meta, reorder, *slot_rows
                )
            now_core = to_seq(now, 1)
        others.append(to_column(now))
        halves.append((now, now_core))
    halves = [
        part for pair, other in zip(halves, others) for part in (*pair, other, to_seq(other, 1))
    ]
    halves[0], grads_in[2] = gate(halves[0], grads_in[2])
    grads_in[1], grads_in[3] = to_seq(final, 1), to_seq(grads_in[2], 1)
    if half % 16 == 0:
        weights, vec, router = pl.pallas_call(
            functools.partial(assemble_kernel, ring_len, half, share),
            grid_spec=pltpu.PrefetchScalarGridSpec(
                num_scalar_prefetch=1,
                grid=(1,),
                in_specs=[whole((half + 8, wide))] * len(halves),
                out_specs=[whole((d, wide)), whole((16, d)), whole((d, 128))],
            ),
            out_shape=[
                jax.ShapeDtypeStruct((d, wide), BF),
                jax.ShapeDtypeStruct((16, d), F32),
                jax.ShapeDtypeStruct((d, 128), BF),
            ],
            compiler_params=params(),
            cost_estimate=cost(0.01),
            name="assemble",
        )(ids, *halves)
    else:
        place = jnp.arange(shards * 2, dtype=jnp.int32)
        place = spot[place // 2] * 2 + (place % 2 ^ core)
        weights = jnp.stack([part[:half] for part in halves])[place].reshape(d, wide)
        vec = jnp.stack([part[half:, :256] for part in halves[::2]])[spot]
        vec = vec.reshape(shards, 8, 2, 128)[..., :share].transpose(2, 1, 0, 3)
        vec = vec.reshape(16, d).astype(F32)
        router = jnp.pad(vec[8:16].T, ((0, 0), (0, 120))).astype(BF)

    pack = after(pack, arrived, *others)
    chunks = [(pack, to_column(pack)), (round_ring(pack),)]

    def tile_spec(shape, index_map):
        return pl.BlockSpec(shape, index_map)

    grad_slots = pl.pallas_call(
        functools.partial(gather_grads_kernel, slots, parts),
        grid_spec=pltpu.PrefetchScalarGridSpec(
            num_scalar_prefetch=1,
            grid=(parts, sub),
            in_specs=[
                tile_spec((TILE, 1, length), lambda k, u, ids: ((ids[0] ^ k) * sub + u, 0, 0))
            ]
            + [tile_spec((TILE, pad, d), lambda k, u, ids: ((ids[0] ^ k) * sub + u, 0, 0))]
            * parts,
            out_specs=tile_spec((1, rows, d), lambda k, u, ids: (k * sub + u, 0, 0)),
        ),
        out_shape=jax.ShapeDtypeStruct((tiles, rows, d), BF),
        compiler_params=params(),
        cost_estimate=cost(0.01),
        name="grad_slots",
    )(ids, slot_rows[0], *grads_in)

    per_image = lambda *tail: pl.BlockSpec((1,) + tail, lambda i: (i,) + (0,) * len(tail))
    made = pl.pallas_call(
        functools.partial(fwd_kernel, parts),
        grid=(own,),
        in_specs=[per_image(pad, d)] * parts
        + [per_image(1, length), whole((d, wide)), whole((16, d))],
        out_specs=[
            per_image(length, 3 * d),
            per_image(length, d),
            per_image(length, 128),
            per_image(length, d),
            per_image(length, d),
            per_image(length, d),
        ]
        + [per_image(pad, d)] * parts,
        out_shape=[
            jax.ShapeDtypeStruct((own, length, 3 * d), BF),
            jax.ShapeDtypeStruct((own, length, d), BF),
            jax.ShapeDtypeStruct((own, length, 128), F32),
            jax.ShapeDtypeStruct((own, length, d), F32),
            jax.ShapeDtypeStruct((own, length, d), BF),
            jax.ShapeDtypeStruct((own, length, d), BF),
        ]
        + [jax.ShapeDtypeStruct((own, pad, d), BF)] * parts,
        compiler_params=params(),
        cost_estimate=cost(0.01),
        name="block_forward",
    )(*toks, mask_bias, weights, vec)
    *made, first_other, second = gate(*made, chunks[0][1], chunks[1][0])
    chunks = [(chunks[0][0], first_other), (second, to_column(second))]
    qkv, attended, lse, residual, z_own, normed = made[:6]
    res_pieces = list(made[6:])

    def add(*terms):
        return sum(term.astype(F32) for term in terms)

    def ring_sum(moving, r):
        terms = (packs[r][0], crossed[r]) + (() if moving is None else (moving,))
        return add(*terms)

    z_far = to_seq(z_own, 2)
    z_rows = [z_own, to_seq(z_own, 1), z_far, None]
    if ring_len > 2:
        chunks.append((round_ring(second),))
    x_rows = gr_rows = None
    for k in range(parts):
        chain = () if k == 0 else (x_rows, gr_rows)
        if k == 2:
            z_far, x_rows, gr_rows, second_other, *rest = gate(
                z_far, x_rows, gr_rows, chunks[1][1], *[c[0] for c in chunks[2:]]
            )
            chunks[1] = (chunks[1][0], second_other)
            for r in range(2, ring_len):
                part = rest[0] if r == 2 else round_ring(part)
                chunks[r:] = [(part, to_column(part) if r < ring_len - 1 else part)]
            z_rows[2:] = [z_far, to_seq(z_far, 1)]
            chain = (x_rows, gr_rows)
        x_rows, gr_rows = pl.pallas_call(
            functools.partial(gather_rows_kernel, slots, experts),
            grid_spec=pltpu.PrefetchScalarGridSpec(
                num_scalar_prefetch=1,
                grid=(sub,),
                in_specs=[
                    tile_spec(
                        (TILE, 1, length), lambda u, ids, k=k: ((ids[0] ^ k) * sub + u, 0, 0)
                    ),
                    tile_spec((TILE, length, d), lambda u, ids: (u, 0, 0)),
                    tile_spec((1, rows, d), lambda u, ids, k=k: (k * sub + u, 0, 0)),
                    whole((d, 128)),
                ]
                + [pl.BlockSpec(memory_space=pl.ANY)] * len(chain),
                out_specs=[
                    tile_spec((1, rows, d), lambda u, ids, k=k: (k * sub + u, 0, 0)),
                    tile_spec((1, rows, d), lambda u, ids, k=k: (k * sub + u, 0, 0)),
                ],
            ),
            out_shape=[jax.ShapeDtypeStruct((tiles, rows, d), BF)] * 2,
            input_output_aliases={5: 0, 6: 1} if chain else {},
            compiler_params=params(),
            cost_estimate=cost(0.01),
            name="slot_rows",
        )(ids, slot_rows[k], z_rows[k], grad_slots, router, *chain)

    tile3 = pl.BlockSpec((1, rows, d), lambda t, *_: (t, 0, 0))
    pack_rows = 2 * fs + 16
    acc_out = acc_gx = None
    packs = []
    crossed = {}
    moving = None
    for r in range(ring_len):
        e0, e1 = chunks[r]
        is_first, is_last = r == 0, r == ring_len - 1
        operands = [e0, e1, x_rows, gr_rows]
        in_specs = [
            whole((pack_rows, d)),
            whole((pack_rows, d)),
            tile3,
            tile3,
        ]
        aliases = {}
        if not is_first:
            operands += [acc_out, acc_gx]
            in_specs += [tile3, tile3]
            aliases = {4: 2} if is_last else {4: 2, 5: 3}
        pack_shape = jax.ShapeDtypeStruct((pack_rows, d), BF)
        out_specs = [whole((pack_rows, d)), whole((pack_rows, d)), tile3, tile3]
        acc_shape = jax.ShapeDtypeStruct((tiles, rows, d), F32)
        out_shape = [pack_shape, pack_shape, acc_shape, acc_shape]
        if is_last:
            operands += [grad_slots, vec]
            in_specs += [tile3, whole((16, d))]
            out_specs[3:] = [
                pl.BlockSpec(
                    (TILE, slots + 8, d), lambda t, k=k: (jnp.clip(t - k * sub, 0, sub - 1), 0, 0)
                )
                for k in range(parts)
            ]
            out_shape[3:] = [jax.ShapeDtypeStruct((own, slots + 8, d), BF)] * parts
        made = pl.pallas_call(
            functools.partial(expert_kernel, is_first, is_last, slots, experts, fs),
            grid_spec=pltpu.PrefetchScalarGridSpec(
                num_scalar_prefetch=0,
                grid=(tiles,),
                in_specs=in_specs,
                out_specs=out_specs,
                scratch_shapes=[
                    pltpu.VMEM((2 * fs, d), BF),
                    pltpu.VMEM((2 * fs, d), BF),
                    pltpu.VMEM((2 * fs, d), F32),
                    pltpu.VMEM((2 * fs, d), F32),
                    pltpu.VMEM((8, 2 * fs), F32),
                    pltpu.VMEM((8, d), F32),
                    pltpu.VMEM((8, 2 * fs), F32),
                ],
            ),
            out_shape=out_shape,
            input_output_aliases=aliases,
            compiler_params=params(),
            cost_estimate=cost(50),
            name="expert_pair",
        )(*operands)
        ready = {}
        if r == 0:
            ready = {("in", q, p): chunks[q][p] for q in range(2, ring_len) for p in (0, 1)}
            ready.pop(("in", ring_len - 1, 1), None)
        elif r == 1:
            ready[("in", ring_len - 1, 1)] = chunks[ring_len - 1][1]
            ready.update({("piece", j): res_pieces[j] for j in range(1, parts)})
        else:
            ready[("out", r - 1, 1)] = crossed[r - 1]
            if moving is not None:
                ready["moving"] = moving
            if r == 2:
                ready.update({("res", j): res_in[j] for j in range(1, parts)})
        values = gate(*made, *ready.values())
        made, ready = values[: len(made)], dict(zip(ready, values[len(made) :]))
        for key, value in ready.items():
            if key == "moving":
                moving = value
            elif key[0] == "in":
                chunks[key[1]] = tuple(value if p == key[2] else chunks[key[1]][p] for p in (0, 1))
            elif key[0] == "out":
                crossed[key[1]] = value
            elif key[0] == "piece":
                res_pieces[key[1]] = value
            else:
                res_in[key[1]] = value
        packs.append(made[:2])
        acc_out, acc_gx = made[2:4]
        if r == 0 and ring_len > 2:
            chunks[ring_len - 1] = (chunks[ring_len - 1][0], to_column(chunks[ring_len - 1][0]))
        if r >= 1:
            crossed[r] = to_column(packs[r][1])
        if r >= 2:
            moving = round_ring(ring_sum(moving, r - 1).astype(BF))
        if r == 1:
            res_in = [res_pieces[0]] + [to_seq(res_pieces[j], j) for j in range(1, parts)]
    gx = made[3 : 3 + parts]

    gx_in = [gx[k] if k == 0 else to_seq(gx[k], k) for k in range(parts)]
    mixed = pl.pallas_call(
        functools.partial(weigh_kernel, slots, experts),
        grid_spec=pltpu.PrefetchScalarGridSpec(
            num_scalar_prefetch=1,
            grid=(tiles,),
            in_specs=[
                tile3,
                tile3,
                whole((d, 128)),
                whole((16, d)),
                whole((rows, rows)),
            ],
            out_specs=[
                *[pl.BlockSpec((1, TILE * CAP, d), lambda t, *_: (t, 0, 0))] * parts,
            ],
        ),
        out_shape=[
            *[jax.ShapeDtypeStruct((tiles, TILE * CAP, d), BF)] * parts,
        ],
        compiler_params=params(),
        cost_estimate=cost(50),
        name="weigh",
    )(ids, acc_out, x_rows, router, vec, reorder)
    last = ring_len - 1
    own_meta, moving, crossed[last], *rest = gate(
        own_meta, moving, crossed[last], *gx_in[1:], *mixed
    )
    gx_in[1:], mixed = rest[: parts - 1], rest[parts - 1 :]
    mixed_in = [mixed[0]] + [to_seq(mixed[k], k) for k in range(1, parts)]
    moving = round_ring(ring_sum(moving, last).astype(BF))
    crossed[0] = to_column(packs[0][1])

    side = me // 2
    quarter = share // 4

    def shift_ring(v, k):
        return lax.ppermute(v, "fsdp", [(n, (n + 2 * k) % shards) for n in range(shards)])

    def core_pair(made):
        if len(made) == 1:
            split = made[0].reshape(shards, 2, 2, quarter, made[0].shape[-1])
            made = index(split, core, 2), index(split, 1 - core, 2)
        return made[0], to_seq(made[1], 1)

    def over_y(keep, come=None):
        pair = [v for v in (keep, come) if v is not None]
        send = add(*[index(v, 1 - side, 1) for v in pair]).astype(BF)
        return add(*[index(v, side, 1) for v in pair], to_seq(send, 2)).astype(BF)

    def over_x(keep, come=None):
        pair = [v.reshape(ring_len, 2, *v.shape[1:]) for v in (keep, come) if v is not None]
        send = add(*[index(v, 1 - column, 1) for v in pair]).astype(BF)
        return add(*[index(v, column, 1) for v in pair], to_column(send)).astype(BF)

    def over_ring(v):
        far = [
            shift_ring(index(v, (ring_at + k) % ring_len), k) for k in range(1, ring_len)
        ]
        return add(index(v, ring_at), *far).astype(BF)

    def in_order(pieces):
        a, b, c, e = pieces
        near = [jnp.where(core == 0, a, b), jnp.where(core == 0, b, a)]
        far = [jnp.where(core == 0, c, e), jnp.where(core == 0, e, c)]
        front = [jnp.where(side == 0, u, v) for u, v in zip(near, far)]
        back = [jnp.where(side == 0, v, u) for u, v in zip(near, far)]
        return jnp.concatenate(front + back, axis=0)

    def spread_rows(v):
        return in_order([v] + [to_seq(v, k) for k in range(1, parts)]).astype(F32)

    image3 = lambda *tail: pl.BlockSpec((1,) + tail, lambda i, *_: (i,) + (0,) * len(tail))
    width = d // 2
    column3 = lambda n: pl.BlockSpec((1, length, width), lambda i, *_: (i, 0, n))
    weight3 = lambda n: pl.BlockSpec((d, width), lambda i, *_: (0, n))
    partial_shape = jax.ShapeDtypeStruct((own, length, d), F32)
    def grad_outs(cols):
        if quarter % 8:
            return [whole((d, cols))], [jax.ShapeDtypeStruct((d, cols), BF)]
        shape = (shards, 2, quarter, cols)
        return [whole(shape)] * 2, [jax.ShapeDtypeStruct(shape, BF)] * 2

    grad_specs, grad_shapes = grad_outs(d + 3 * width)
    grad_att, grad_res, after_first, small, *first = pl.pallas_call(
        functools.partial(back_first_kernel, parts, experts, slots, len(grad_specs)),
        grid_spec=pltpu.PrefetchScalarGridSpec(
            num_scalar_prefetch=1,
            grid=(own,),
            in_specs=[image3(length, parts)]
            + [image3(slots + 8, d)] * parts
            + [pl.BlockSpec((1, pad, d), lambda i, ids: (ids[0] * own + i, 0, 0))] * parts
            + [
                image3(length, d),
                image3(length, d),
                image3(length, d),
                pl.BlockSpec((d, d), lambda i, ids: (0, 3)),
                whole((16, d)),
                whole((d, 128)),
                image3(1, length),
                column3(0),
                column3(2),
                column3(4),
                image3(length, 128),
                image3(length, d),
                weight3(0),
                weight3(2),
                weight3(4),
            ],
            out_specs=[
                image3(length, d),
                image3(length, d),
                image3(length, d),
                whole((16, d)),
                *grad_specs,
            ],
            scratch_shapes=[
                pltpu.VMEM((d, d), F32),
                pltpu.VMEM((d, 3 * width), F32),
                pltpu.VMEM((16, d), F32),
                pltpu.VMEM((d, 128), F32),
                pltpu.VMEM((length, 3 * width), BF),
            ],
        ),
        out_shape=[
            jax.ShapeDtypeStruct((own, length, d), BF),
            partial_shape,
            partial_shape,
            jax.ShapeDtypeStruct((16, d), F32),
            *grad_shapes,
        ],
        compiler_params=params(),
        cost_estimate=cost(50),
        name="back_first",
    )(
        ids,
        own_meta,
        *gx_in,
        *grads_in,
        attended,
        residual,
        z_own,
        weights,
        vec,
        router,
        mask_bias,
        qkv,
        qkv,
        qkv,
        lse,
        normed,
        weights,
        weights,
        weights,
    )
    grad_att, grad_res, after_first, small, moving, crossed[0], *rest = gate(
        grad_att, grad_res, after_first, small, moving, crossed[0], *mixed_in[1:], *first
    )
    mixed_in[1:], first = rest[: parts - 1], rest[parts - 1 :]
    first = core_pair(first)
    grad_specs, grad_shapes = grad_outs(3 * width + 128)
    made = pl.pallas_call(
        functools.partial(back_second_kernel, parts, len(grad_specs)),
        grid_spec=pltpu.PrefetchScalarGridSpec(
        num_scalar_prefetch=1,
        grid=(own,),
        in_specs=[
            image3(1, length),
            column3(1),
            column3(3),
            column3(5),
            image3(length, d),
            image3(length, d),
            image3(length, 128),
            image3(length, d),
            weight3(1),
            weight3(3),
            weight3(5),
            whole((16, d)),
            image3(length, d),
            image3(length, d),
            whole((16, d)),
        ]
        + [image3(pad, d)] * parts,
        out_specs=[image3(pad, d)] * parts + grad_specs,
        scratch_shapes=[
            pltpu.VMEM((d, 3 * width), F32),
            pltpu.VMEM((128, d), F32),
            pltpu.VMEM((d, 128), F32),
            pltpu.VMEM((length, 3 * width), BF),
        ],
        ),
        out_shape=[jax.ShapeDtypeStruct((own, pad, d), BF)] * parts + grad_shapes,
        compiler_params=params(),
        cost_estimate=cost(50),
        name="back_second",
    )(
        ids,
        mask_bias,
        qkv,
        qkv,
        qkv,
        attended,
        grad_att,
        lse,
        normed,
        weights,
        weights,
        weights,
        small,
        after_first,
        grad_res,
        vec,
        *toks,
    )
    token_pieces, second = made[:parts], made[parts:]
    far_first, moving, crossed[0], *rest = gate(
        first[1], moving, crossed[0], *token_pieces, *mixed_in[1:], *second
    )
    first = (first[0], far_first)
    token_pieces, mixed_in[1:], second = (
        rest[:parts],
        rest[parts : 2 * parts - 1],
        rest[2 * parts - 1 :],
    )

    image_block = pl.BlockSpec(
        (TILE, block_len, d), lambda j, u, ids: ((ids[0] ^ j) * sub + u, 0, 0)
    )
    output = pl.pallas_call(
        functools.partial(combine_kernel, parts),
        grid_spec=pltpu.PrefetchScalarGridSpec(
            num_scalar_prefetch=1,
            grid=(parts, sub),
            in_specs=[
                pl.BlockSpec((TILE, pad, 8), lambda j, u, ids: ((ids[0] ^ j) * sub + u, 0, 0))
            ]
            + [pl.BlockSpec((TILE, pad, d), lambda j, u, ids: (u, 0, 0))] * parts
            + [
                pl.BlockSpec(
                    (1, TILE * CAP, d), lambda j, u, ids, k=k: ((j ^ k) * sub + u, 0, 0)
                )
                for k in range(parts)
            ],
            out_specs=image_block,
        ),
        out_shape=jax.ShapeDtypeStruct((images, block_len, d), BF),
        compiler_params=params(),
        cost_estimate=cost(50),
        name="combine",
    )(ids, mix_meta, *res_in, *mixed_in)

    first_x = over_x(*first)
    second = core_pair(second)
    second_y = over_y(*second)
    tokens_in = [token_pieces[j] if j == 0 else to_seq(token_pieces[j], j) for j in range(parts)]
    first_x, second_y, output, *tokens_in = gate(first_x, second_y, output, *tokens_in)
    first_own, second_x = over_y(first_x), over_x(second_y)
    grad_tokens = in_order(tokens_in)[:, :block_len]
    first_own, second_x, grad_tokens = gate(first_own, second_x, grad_tokens)
    both_x = jnp.concatenate([first_own, second_x], axis=-1)
    total = ring_sum(moving, 0)
    grad_hidden = total[None, :fs]
    grad_expert_out = total[None, fs : 2 * fs]
    grad_hidden_bias = total[2 * fs : 2 * fs + 1, :fs]
    grad_out_bias = lax.dynamic_slice(total, (2 * fs + 1, rank * share), (1, share))
    own_rows = over_ring(both_x)
    mine = spread_rows(own_rows)
    grad_proj = mine[:, :d]
    at_b, at_small = d + 3 * width, d + 6 * width
    grad_qkv = jnp.concatenate(
        [
            mine[:, start + n * width : start + (n + 1) * width]
            for n in range(3)
            for start in (d, at_b)
        ],
        axis=1,
    )
    small = mine[:, at_small : at_small + 16].T
    grad_router = mine[:, at_small + 8 : at_small + 8 + experts]

    return (
        output,
        grad_tokens,
        small[0],
        small[1],
        grad_qkv,
        small[2],
        small[3],
        grad_proj,
        small[4],
        small[5],
        small[6],
        grad_router,
        grad_hidden,
        grad_hidden_bias,
        grad_expert_out,
        grad_out_bias,
    )


def solution(mesh):
    in_specs = (
        P("fsdp", "seq", None),
        P("fsdp", None),
        P("fsdp", "seq", None),
        P("fsdp", "seq", None),
        P("fsdp"),
        P("fsdp"),
        P("fsdp", None),
        P("fsdp"),
        P("fsdp"),
        P("fsdp", None),
        P("fsdp"),
        P("fsdp"),
        P("fsdp"),
        P("fsdp", None),
        P("seq", "fsdp", None),
        P("seq", "fsdp"),
        P("seq", "fsdp", None),
        P("seq", "fsdp"),
    )
    out_specs = (
        P("fsdp", "seq", None),
        P("fsdp", "seq", None),
        P("fsdp"),
        P("fsdp"),
        P("fsdp", None),
        P("fsdp"),
        P("fsdp"),
        P("fsdp", None),
        P("fsdp"),
        P("fsdp"),
        P("fsdp"),
        P("fsdp", None),
        P("seq", "fsdp", None),
        P("seq", "fsdp"),
        P("seq", "fsdp", None),
        P("seq", "fsdp"),
    )
    return jax.shard_map(body, mesh=mesh, in_specs=in_specs, out_specs=out_specs, check_vma=False)
```

```python
import functools

import jax
import jax.numpy as jnp
from jax import lax
from jax.experimental import pallas as pl
from jax.experimental.pallas import tpu as pltpu
from jax.sharding import PartitionSpec as P

HEAD_DIM = 64
TOP = 2
CAP = 30
TILE = 4
EPS = 1e-06
NEG = -1e30
BF = jnp.bfloat16
F32 = jnp.float32
VMEM = 66_500_000


def nn(a, b):
    return jnp.dot(a, b, preferred_element_type=F32)


def nt(a, b):
    return lax.dot_general(a, b, (((1,), (1,)), ((), ())), preferred_element_type=F32)


def tn(a, b):
    return lax.dot_general(a, b, (((0,), (0,)), ((), ())), preferred_element_type=F32)


def stats(v):
    center = v - jnp.mean(v, axis=-1, keepdims=True)
    r = lax.rsqrt(jnp.mean(center * center, axis=-1, keepdims=True) + EPS)
    return center * r, r


def norm_back(u, gain, vhat, r):
    ug = u * gain
    return r * (
        ug
        - jnp.mean(ug, axis=-1, keepdims=True)
        - vhat * jnp.mean(ug * vhat, axis=-1, keepdims=True)
    )


def rows_of(refs, i=0):
    return jnp.concatenate([ref[i].astype(F32) for ref in refs], axis=0)


def params(**kw):
    return pltpu.CompilerParams(vmem_limit_bytes=VMEM, **kw)


def cost(us):
    return pl.CostEstimate(flops=int(us * 1e9), bytes_accessed=int(us * 1e4), transcendentals=0)


def half_masks():
    lane = lax.broadcasted_iota(jnp.int32, (1, 2 * HEAD_DIM), 1)
    first = (lane < HEAD_DIM).astype(F32)
    return first, 1.0 - first


def fwd_kernel(parts, *refs):
    toks, refs = refs[:parts], refs[parts:]
    mask_ref, w_ref, vec_ref, qkv_ref, att_ref, lse_ref, res_ref, z_ref, normed_ref = refs[:9]
    sends = refs[9:]
    x = rows_of(toks)
    d = x.shape[1]
    vec = vec_ref[...]
    vhat, _ = stats(x)
    normed = (vhat * vec[0:1] + vec[1:2]).astype(BF)
    normed_ref[0] = normed
    qkv_ref[0, :, 0:d] = (nn(normed, w_ref[:, 0:d]) + vec[2:3]).astype(BF)
    qkv_ref[0, :, d : 2 * d] = nn(normed, w_ref[:, d : 2 * d]).astype(BF)
    qkv_ref[0, :, 2 * d : 3 * d] = (nn(normed, w_ref[:, 2 * d : 3 * d]) + vec[3:4]).astype(BF)
    bias = mask_ref[0]
    first, second = half_masks()
    scale = HEAD_DIM ** (-0.5)
    lane = lax.broadcasted_iota(jnp.int32, (x.shape[0], 128), 1)
    lse = jnp.zeros((x.shape[0], 128), F32)
    for pair in range(d // 128):
        q2 = qkv_ref[0, :, 128 * pair : 128 * pair + 128]
        k2 = qkv_ref[0, :, d + 128 * pair : d + 128 * pair + 128]
        v2 = qkv_ref[0, :, 2 * d + 128 * pair : 2 * d + 128 * pair + 128]
        outs = []
        for a, half in enumerate((first, second)):
            qa = q2 * (half * scale).astype(BF)
            s = nt(qa, k2) + bias
            top = jnp.max(s, axis=-1, keepdims=True)
            e = jnp.exp(s - top)
            total = jnp.sum(e, axis=-1, keepdims=True)
            outs.append(nn(e.astype(BF), v2) * (1.0 / total))
            lse = jnp.where(lane == 2 * pair + a, top + jnp.log(total), lse)
        att = jnp.where(first > 0, outs[0], outs[1])
        att_ref[0, :, 128 * pair : 128 * pair + 128] = att.astype(BF)
    lse_ref[0] = lse
    res = x + nn(att_ref[0], w_ref[:, 3 * d : 4 * d]) + vec[4:5]
    res_ref[0] = res
    zhat, _ = stats(res)
    z_ref[0] = (zhat * vec[5:6] + vec[6:7]).astype(BF)
    block = x.shape[0] // parts
    for j, ref in enumerate(sends):
        ref[0] = res[j * block : (j + 1) * block].astype(BF)


def spread(row, slots, values):
    length = values.shape[0]
    hot = (lax.broadcasted_iota(jnp.int32, (slots, length), 0) == row).astype(BF)
    return nn(hot, values)


def gather_grads_kernel(slots, parts, ids_ref, slot_ref, *refs):
    out = []
    for i in range(TILE):
        values = rows_of(refs[:parts], i).astype(BF)
        out.append(spread(slot_ref[i], slots, values))
    refs[parts][0] = jnp.concatenate(out, axis=0).astype(BF)


def router_probs(rows, router, experts):
    logits = nn(rows, router)
    lane = lax.broadcasted_iota(jnp.int32, logits.shape, 1)
    logits = jnp.where(lane < experts, logits, NEG)
    e = jnp.exp(logits - jnp.max(logits, axis=-1, keepdims=True))
    return e / jnp.sum(e, axis=-1, keepdims=True), lane


def gather_rows_kernel(slots, experts, ids_ref, slot_ref, z_ref, g_ref, router_ref, *refs):
    x_ref, gr_ref = refs[-2:]
    out = [spread(slot_ref[i], slots, z_ref[i]) for i in range(TILE)]
    x = jnp.concatenate(out, axis=0).astype(BF)
    probs, lane = router_probs(x, router_ref[...], experts)
    gate = jnp.sum(jnp.where(lane == ids_ref[0], probs, 0.0), axis=-1, keepdims=True)
    x_ref[0] = x
    gr_ref[0] = (gate * g_ref[0].astype(F32)).astype(BF)


def gelu_parts(v):
    e = jnp.exp(-0.5 * v * v)
    den = 1.0 + 0.23164189 * jnp.abs(v)
    t = pl.reciprocal(den, approx=True)
    t = t * (2.0 - den * t)
    poly = t * (
        0.127414796 + t * (-0.142248368 + t * (0.7107068705 + t * (-0.7265760135 + t * 0.5307027145)))
    )
    tail = poly * e
    cdf = jnp.where(v >= 0, 1.0 - tail, tail)
    return v * cdf, cdf + v * (0.3989422804 * e)


def expert_kernel(first, last, slots, experts, fs, *refs):
    e0, e1, x_ref, gr_ref = refs[:4]
    refs = list(refs[4:])
    if not first:
        acc_out_in, acc_gx_in = refs[:2]
        refs = refs[2:]
    if last:
        g_ref, bo_ref, refs = refs[0], refs[1], refs[2:]
    p0, p1, acc_out = refs[:3]
    gx_refs, refs = refs[3:-7], refs[-7:]
    wh, wo, gwh, gwo, gbh, gbo, bias = refs
    step = pl.program_id(0)

    @pl.when(step == 0)
    def _():
        wh[0:fs] = e0[0:fs]
        wh[fs : 2 * fs] = e1[0:fs]
        wo[0:fs] = e0[fs : 2 * fs]
        wo[fs : 2 * fs] = e1[fs : 2 * fs]
        both = [e[2 * fs : 2 * fs + 16, 0:fs].astype(F32)[0:8] for e in (e0, e1)]
        bias[...] = jnp.concatenate(both, axis=1)
        gwh[...] = jnp.zeros_like(gwh)
        gwo[...] = jnp.zeros_like(gwo)
        gbh[...] = jnp.zeros_like(gbh)
        gbo[...] = jnp.zeros_like(gbo)

    x = x_ref[0]
    gr = gr_ref[0]
    pre = nt(x, wh[...]) + bias[0:1]
    act, slope = gelu_parts(pre)
    hidden = act.astype(BF)
    out = nn(hidden, wo[...])
    grad_pre_f = nt(gr, wo[...]) * slope
    grad_pre = grad_pre_f.astype(BF)
    gx = nn(grad_pre, wh[...])
    gwh[...] += tn(grad_pre, x)
    gwo[...] += tn(hidden, gr)
    gbh[0:1] += jnp.sum(grad_pre_f, axis=0, keepdims=True)
    gbo[0:1] += jnp.sum(gr.astype(F32), axis=0, keepdims=True)
    if not first:
        out = out + acc_out_in[0]
        gx = gx + acc_gx_in[0]
    acc_out[0] = out
    if last:
        dots = jnp.sum((out + bo_ref[7:8]) * g_ref[0].astype(F32), axis=-1, keepdims=True)
        sub = lax.broadcasted_iota(jnp.int32, (8, x.shape[1]), 0)
        fill = jnp.zeros((128 - slots, 128), F32)
        wide_fill = jnp.zeros((8, x.shape[1] - 128), F32)
        out_rows = []
        for i in range(TILE):
            col = jnp.broadcast_to(dots[i * slots : (i + 1) * slots], (slots, 128))
            row = jnp.concatenate([col, fill], axis=0).T[0:8]
            row = jnp.concatenate([row, wide_fill], axis=1)
            high = row.astype(BF).astype(F32)
            row = jnp.where(sub == 0, high, jnp.where(sub == 1, row - high, 0.0))
            out_rows += [gx[i * slots : (i + 1) * slots], row]
        gx = jnp.concatenate(out_rows, axis=0).reshape(TILE, slots + 8, -1).astype(BF)
        for k, ref in enumerate(gx_refs):

            @pl.when(step // (pl.num_programs(0) // len(gx_refs)) == k)
            def _(ref=ref):
                ref[...] = gx
    else:
        gx_refs[0][0] = gx

    @pl.when(step == pl.num_programs(0) - 1)
    def _():
        d = gwh.shape[1]
        for i, pack in enumerate((p0, p1)):
            pack[0:fs] = gwh[i * fs : (i + 1) * fs].astype(BF)
            pack[fs : 2 * fs] = gwo[i * fs : (i + 1) * fs].astype(BF)
            row = jnp.broadcast_to(gbh[0:1, i * fs : (i + 1) * fs], (16, fs))
            row = jnp.concatenate([row, jnp.zeros((16, d - fs), F32)], axis=1)
            sub = lax.broadcasted_iota(jnp.int32, (16, d), 0)
            pack[2 * fs : 2 * fs + 16] = jnp.where(
                sub == 0, row, jnp.where(sub == 1, gbo[0:1], 0.0)
            ).astype(BF)


def weigh_kernel(slots, experts, ids_ref, out_ref, x_ref, router_ref, bo_ref, perm_ref, *mixed_refs):
    x = x_ref[0]
    out = out_ref[0] + bo_ref[7:8]
    probs, lane = router_probs(x, router_ref[...], experts)
    gate = jnp.sum(jnp.where(lane == ids_ref[0], probs, 0.0), axis=-1, keepdims=True)
    weighted = nn(perm_ref[...], (gate * out).astype(BF))
    count = weighted.shape[0] // len(mixed_refs)
    for k, ref in enumerate(mixed_refs):
        ref[0] = weighted[k * count : (k + 1) * count].astype(BF)


def combine_kernel(parts, ids_ref, meta_ref, *refs):
    res, rows, out_ref = refs[:parts], refs[parts : 2 * parts], refs[2 * parts]
    step = pl.program_id(0)
    block, length = meta_ref.shape[1], out_ref.shape[1]
    meta = meta_ref[...].reshape(TILE * block, 8)
    total = 0.0
    for k, ref in enumerate(rows):
        slot = lax.broadcasted_iota(jnp.int32, (TILE * block, ref.shape[1]), 1)
        total += nn((slot == meta[:, k : k + 1]).astype(BF), ref[0])
    live = meta[:, 4:5].astype(F32)
    for j in range(parts):

        @pl.when(step == j)
        def _(j=j):
            base = res[j][...].astype(F32).reshape(TILE * block, -1)
            out = ((base + total) * live).reshape(TILE, block, -1)
            out_ref[...] = out[:, :length].astype(BF)


def norm_part(parts, experts, slots, refs, accs, ids_ref, i):
    meta_ref, gx_refs, g_refs, att_ref, res_ref, z_ref, w_ref, vec_ref, router_ref = refs
    acc_proj, acc_small, acc_router = accs
    length, d = res_ref.shape[1:]
    meta = meta_ref[0]
    lane = lax.broadcasted_iota(jnp.int32, (length, 128), 1)
    dz = jnp.zeros((length, d), F32)
    grad_probs = jnp.zeros((length, 128), F32)
    for k in range(parts):
        hot = lane == meta[:, k : k + 1]
        dz += nn(hot.astype(BF), gx_refs[k][0])
        dots = gx_refs[k][0, slots - 8 : slots + 8, 0:128].astype(F32)
        dots = dots[8:9] + dots[9:10]
        of_token = jnp.sum(jnp.where(hot, dots, 0.0), axis=-1, keepdims=True)
        grad_probs = jnp.where(lane == (ids_ref[0] ^ k), of_token, grad_probs)
    z = z_ref[0]
    probs, _ = router_probs(z, router_ref[...], experts)
    grad_logits = probs * (grad_probs - jnp.sum(probs * grad_probs, axis=-1, keepdims=True))
    grad_logits = grad_logits.astype(BF)
    dz += nt(grad_logits, router_ref[...])
    acc_router[...] += tn(z, grad_logits)
    zhat, r2 = stats(res_ref[0])
    acc_small[5:6] += jnp.sum(dz * zhat, axis=0, keepdims=True)
    acc_small[6:7] += jnp.sum(dz, axis=0, keepdims=True)
    grad_res = rows_of(g_refs) + norm_back(dz, vec_ref[5:6], zhat, r2)
    branch = grad_res.astype(BF)
    acc_small[4:5] += jnp.sum(branch.astype(F32), axis=0, keepdims=True)
    acc_proj[...] += tn(att_ref[0], branch)
    return grad_res, nt(branch, w_ref[...]).astype(BF)


def heads_part(half, mask_ref, qkv_refs, att_ref, ga_ref, lse_ref, normed_ref, w_refs, acc, acc_small, gqkv):
    q_ref, k_ref, v_ref = qkv_refs
    width = q_ref.shape[2]
    spot = half * width
    bias = mask_ref[0]
    lse = lse_ref[0]
    first, second = half_masks()
    scale = HEAD_DIM ** (-0.5)
    for pair in range(width // 128):
        at = 128 * pair
        here = slice(spot + at, spot + at + 128)
        q2 = q_ref[0, :, at : at + 128]
        k2 = k_ref[0, :, at : at + 128]
        v2 = v_ref[0, :, at : at + 128]
        g2 = ga_ref[0, :, here]
        prod = g2.astype(F32) * att_ref[0, :, here].astype(F32)
        gq, gk, gv = [], 0.0, 0.0
        for a, mask in enumerate((first, second)):
            qa = q2 * (mask * scale).astype(BF)
            ga = g2 * mask.astype(BF)
            head = half * (width // HEAD_DIM) + 2 * pair + a
            probs = jnp.exp(nt(qa, k2) + bias - lse[:, head : head + 1])
            delta = jnp.sum(prod * mask, axis=-1, keepdims=True)
            grad_scores = (probs * (nt(ga, v2) - delta)).astype(BF)
            gq.append(nn(grad_scores, k2))
            gk += tn(grad_scores, qa)
            gv += tn(probs.astype(BF), ga)
        gqkv[:, at : at + 128] = (jnp.where(first > 0, gq[0], gq[1]) * scale).astype(BF)
        gqkv[:, width + at : width + at + 128] = gk.astype(BF)
        gqkv[:, 2 * width + at : 2 * width + at + 128] = gv.astype(BF)
    acc_small[2:3, spot : spot + width] += jnp.sum(
        gqkv[:, 0:width].astype(F32), axis=0, keepdims=True
    )
    acc_small[3:4, spot : spot + width] += jnp.sum(
        gqkv[:, 2 * width : 3 * width].astype(F32), axis=0, keepdims=True
    )
    acc[...] += tn(normed_ref[0], gqkv[...])
    return sum(
        nt(gqkv[:, n * width : (n + 1) * width], w_ref[...]) for n, w_ref in enumerate(w_refs)
    )


def split_rows(outs, accs, core):
    col = 0
    for acc in accs:
        cols = slice(col, col + acc.shape[1])
        col += acc.shape[1]
        if len(outs) == 1:
            outs[0][:, cols] = acc[...].astype(BF)
            continue
        for out, which in zip(outs, (core, 1 - core)):
            shards, sides, count = out.shape[:3]
            for n in range(shards * sides):
                row = pl.multiple_of((2 * n + which) * count, 8)
                out[n // sides, n % sides, :, cols] = acc[pl.ds(row, count)].astype(BF)


def taker(refs):
    refs = list(refs)

    def take(n):
        out = refs[:n]
        del refs[:n]
        return out

    return take


def back_first_kernel(parts, experts, slots, outs, ids_ref, *refs):
    take = taker(refs)
    (meta_ref,) = take(1)
    norm_refs = [meta_ref, take(parts), take(parts)]
    att_ref, res_ref, z_ref, wp_ref, vec_ref, router_ref = take(6)
    norm_refs += [att_ref, res_ref, z_ref, wp_ref, vec_ref, router_ref]
    (mask_ref,) = take(1)
    qkv_refs = take(3)
    lse_ref, normed_ref = take(2)
    w_refs = take(3)
    ga_ref, gres_ref, dn_ref, small_ref = take(4)
    grads_refs = take(outs)
    acc_proj, acc, acc_small, acc_router, gqkv = take(5)
    i = pl.program_id(0)

    @pl.when(i == 0)
    def _():
        for part in (acc_proj, acc, acc_small, acc_router):
            part[...] = jnp.zeros_like(part)

    accs = (acc_proj, acc_small, acc_router)
    gres_ref[0], ga_ref[0] = norm_part(parts, experts, slots, norm_refs, accs, ids_ref, i)
    dn_ref[0] = heads_part(
        0, mask_ref, qkv_refs, att_ref, ga_ref, lse_ref, normed_ref, w_refs, acc, acc_small, gqkv
    )

    @pl.when(i == pl.num_programs(0) - 1)
    def _():
        acc_small[8:16] = acc_router[...].T[0:8]
        small_ref[...] = acc_small[...]
        split_rows(grads_refs, (acc_proj, acc), ids_ref[0] % 2)


def back_second_kernel(parts, outs, ids_ref, *refs):
    take = taker(refs)
    (mask_ref,) = take(1)
    qkv_refs = take(3)
    att_ref, ga_ref, lse_ref, normed_ref = take(4)
    w_refs = take(3)
    small_in, dn_in, gres_ref, vec_ref = take(4)
    toks, gt_refs = take(parts), take(parts)
    grads_refs = take(outs)
    acc, acc_small, acc_turned, gqkv = take(4)
    i = pl.program_id(0)

    @pl.when(i == 0)
    def _():
        acc[...] = jnp.zeros_like(acc)
        acc_small[0:16] = small_in[...]
        acc_small[16:128] = jnp.zeros((112, acc_small.shape[1]), F32)

    dn = dn_in[0] + heads_part(
        1, mask_ref, qkv_refs, att_ref, ga_ref, lse_ref, normed_ref, w_refs, acc, acc_small, gqkv
    )
    x = rows_of(toks)
    vhat, r1 = stats(x)
    acc_small[0:1] += jnp.sum(dn * vhat, axis=0, keepdims=True)
    acc_small[1:2] += jnp.sum(dn, axis=0, keepdims=True)
    grad_tok = gres_ref[0] + norm_back(dn, vec_ref[0:1], vhat, r1)
    block = x.shape[0] // parts
    for j, ref in enumerate(gt_refs):
        ref[0] = grad_tok[j * block : (j + 1) * block].astype(BF)

    @pl.when(i == pl.num_programs(0) - 1)
    def _():
        acc_turned[...] = acc_small[...].T
        split_rows(grads_refs, (acc, acc_turned), ids_ref[0] % 2)


def assemble_kernel(ring_len, half, share, ids_ref, *refs):
    parts, (out_ref, vec_ref, router_ref) = refs[:-3], refs[-3:]
    ring_at, column = ids_ref[1] // 2, ids_ref[1] % 2
    core = ids_ref[0] % 2
    d = vec_ref.shape[1]
    vec = jnp.zeros((16, d), F32)
    at = 0
    for r in range(ring_len):
        for p in range(2):
            shard = lax.rem(ring_at + ring_len - r, ring_len) * 2 + (column ^ p)
            for c in range(2):
                row = pl.multiple_of((shard * 2 + (core ^ c)) * half, half)
                out_ref[pl.ds(row, half)] = parts[at][0:half]
                if c == 0:
                    few = parts[at][half : half + 8, 0:256].astype(F32)
                    few = jnp.concatenate([few[:, 0:128], few[:, 128:256]], axis=0).astype(BF)
                    source = lax.broadcasted_iota(jnp.int32, (128, d), 0)
                    target = lax.broadcasted_iota(jnp.int32, (128, d), 1) - shard * share
                    vec += nn(few, ((source == target) & (source < share)).astype(BF))
                at += 1
    vec_ref[...] = vec
    fill = jnp.zeros((120, d), F32)
    router_ref[...] = jnp.concatenate([vec[8:16], fill], axis=0).T.astype(BF)


def whole(shape):
    return pl.BlockSpec(shape, lambda *_: (0,) * len(shape))


def body(
    tokens,
    key_mask,
    routes,
    out_grad,
    norm1_gain,
    norm1_bias,
    w_qkv,
    bias_q,
    bias_v,
    w_proj,
    bias_proj,
    norm2_gain,
    norm2_bias,
    w_router,
    w_hidden,
    bias_hidden,
    w_expert_out,
    bias_expert_out,
):
    images, block_len, d = tokens.shape
    parts = lax.axis_size("seq")
    shards = lax.axis_size("fsdp")
    experts = parts
    ring_len = shards // 2
    own = images // parts
    sub = own // TILE
    tiles = parts * sub
    pad = -(-block_len // 8) * 8
    length = parts * pad
    slots = parts * CAP
    rows = TILE * slots
    fs = w_hidden.shape[1]
    share = d // shards
    half = share // 2
    me = lax.axis_index("seq")
    rank = lax.axis_index("fsdp")
    ring_at, column = rank // 2, rank % 2
    core = me % 2
    ids = jnp.stack([me, rank]).astype(jnp.int32)

    def to_seq(v, k):
        return lax.ppermute(v, "seq", [(n, n ^ k) for n in range(parts)])

    def to_column(v):
        return lax.ppermute(v, "fsdp", [(n, n ^ 1) for n in range(shards)])

    def round_ring(v):
        return lax.ppermute(v, "fsdp", [(n, (n + 2) % shards) for n in range(shards)])

    def gate(*values):
        return lax.optimization_barrier(values)

    def after(v, *others):
        return lax.optimization_barrier((v,) + others)[0]

    def index(v, at, axis=0):
        return lax.dynamic_index_in_dim(v, at, axis, keepdims=False)

    def share_seq(v):
        two = to_seq(v, 2)
        return [v, to_seq(v, 1), two, to_seq(two, 1)]

    order = jnp.arange(shards, dtype=jnp.int32)
    spot = 2 * ((ring_at - order // 2) % ring_len) + (order % 2 ^ column)

    wide = 4 * d
    masters = (
        norm1_gain,
        norm1_bias,
        bias_q,
        bias_v,
        bias_proj,
        norm2_gain,
        norm2_bias,
    )
    few = jnp.concatenate([jnp.stack(masters), bias_expert_out, w_router.T], axis=0)
    few = jnp.pad(few, ((0, 16 - few.shape[0]), (0, 128 - share))).astype(BF)
    few_row = jnp.concatenate([few[:8], few[8:]], axis=1)
    few_row = jnp.pad(few_row, ((0, 0), (0, wide - 256)))
    both = jnp.concatenate([w_qkv, w_proj], axis=1)

    def half_rows(which):
        part = lax.dynamic_slice_in_dim(both, which * half, half, 0).astype(BF)
        return jnp.concatenate([part, few_row], axis=0)

    now, now_core = half_rows(core), half_rows(1 - core)
    tokens, routes, out_grad = lax.optimization_barrier((tokens, routes, out_grad, now))[:3]

    grow = ((0, 0), (0, pad - block_len), (0, 0))
    padded = jnp.pad(tokens, grow)
    pieces = [lax.dynamic_slice_in_dim(padded, (me ^ j) * own, own, 0) for j in range(parts)]
    toks = [pieces[j] if j == 0 else to_seq(pieces[j], j) for j in range(parts)]

    spare = jnp.zeros((15, d), F32)
    def build_pack():
      return jnp.concatenate(
        [
            w_hidden[0],
            w_expert_out[0],
            jnp.pad(bias_hidden, ((0, 0), (0, d - fs))),
            spare,
        ],
        axis=0,
    ).astype(BF)
    own_live = lax.dynamic_slice_in_dim(key_mask, me * block_len, block_len, 1)

    def build_final():
        return jnp.pad(out_grad * own_live[:, :, None].astype(BF), grow)


    flat = jnp.pad(
        routes.reshape(images, block_len * TOP), ((0, 0), (0, (-block_len * TOP) % 128))
    )
    blocks = jnp.stack(share_seq(flat))[:, :, : block_len * TOP]
    blocks = blocks.reshape(parts, images, block_len, TOP)
    names = me ^ jnp.arange(parts, dtype=jnp.int32)
    hit = jnp.any(blocks[..., None] == names, axis=3)
    ahead = (
        lax.broadcasted_iota(jnp.int32, (block_len, block_len), 0)
        < lax.broadcasted_iota(jnp.int32, (block_len, block_len), 1)
    ).astype(BF)
    ranks = jnp.einsum(
        "jitk,tu->jiuk", hit.astype(BF), ahead, preferred_element_type=F32
    ).astype(jnp.int32)
    in_image = jnp.where(hit, ranks + (names * CAP)[:, None, None, None], -1)
    in_image = jnp.pad(
        in_image, ((0, 0), (0, 0), (0, pad - block_len), (0, 0)), constant_values=-1
    )
    own_meta = lax.dynamic_slice_in_dim(in_image, me * own, own, 1)
    own_meta = own_meta.transpose(1, 0, 2, 3).reshape(own, length, parts)
    expert_slot = in_image[..., 0]

    def by_image(order):
        out = jnp.concatenate([expert_slot[j] for j in order], axis=-1)
        return out.reshape(images, 1, length)

    slot_rows = [by_image([j ^ k for j in range(parts)]) for k in range(parts)]
    within = (jnp.arange(images, dtype=jnp.int32) % TILE) * CAP
    mix_slot = jnp.where(hit[0], ranks[0] + within[:, None, None], -1)
    mix_meta = jnp.concatenate([mix_slot, own_live[:, :, None]], axis=-1)
    mix_meta = jnp.pad(
        mix_meta, ((0, 0), (0, pad - block_len), (0, 8 - parts - 1)), constant_values=-1
    )
    seen = lax.dynamic_slice_in_dim(key_mask, me * own, own, 0).reshape(own, parts, block_len)
    seen = jnp.stack([index(seen, me ^ j, 1) for j in range(parts)], axis=1)
    seen = jnp.pad(seen, ((0, 0), (0, 0), (0, pad - block_len))).reshape(own, 1, length)
    mask_bias = jnp.where(seen > 0, 0.0, NEG).astype(F32)

    at = lax.broadcasted_iota(jnp.int32, (rows, rows), 0)
    image_at, rank_at = (at % (TILE * CAP)) // CAP, at % CAP
    source = image_at * slots + ((at // (TILE * CAP)) ^ me) * CAP + rank_at
    reorder = (lax.broadcasted_iota(jnp.int32, (rows, rows), 1) == source).astype(BF)

    halves, others = [], []
    for r in range(ring_len):
        if r:
            if r == 2:
                now, w_hidden, w_expert_out, out_grad, others[0] = gate(
                    now, w_hidden, w_expert_out, out_grad, others[0], *pieces
                )[:5]
                pack, final = build_pack(), build_final()
            elif r == 3:
                now, others[1], pack, final, *toks[1:] = gate(
                    now, others[1], pack, final, *toks[1:]
                )
            elif r > 3:
                now, others[r - 2] = gate(now, others[r - 2])
            now = round_ring(now)
            arrived = now
            if r == ring_len - 1:
                grads_in = [final, None, to_seq(final, 2), None]
                now, mask_bias, own_meta, mix_meta, reorder, *slot_rows = gate(
                    now, mask_bias, own_meta, mix_meta, reorder, *slot_rows
                )
            now_core = to_seq(now, 1)
        others.append(to_column(now))
        halves.append((now, now_core))
    halves = [
        part for pair, other in zip(halves, others) for part in (*pair, other, to_seq(other, 1))
    ]
    if half % 16 == 0:
        weights, vec, router = pl.pallas_call(
            functools.partial(assemble_kernel, ring_len, half, share),
            grid_spec=pltpu.PrefetchScalarGridSpec(
                num_scalar_prefetch=1,
                grid=(1,),
                in_specs=[whole((half + 8, wide))] * len(halves),
                out_specs=[whole((d, wide)), whole((16, d)), whole((d, 128))],
            ),
            out_shape=[
                jax.ShapeDtypeStruct((d, wide), BF),
                jax.ShapeDtypeStruct((16, d), F32),
                jax.ShapeDtypeStruct((d, 128), BF),
            ],
            compiler_params=params(),
            cost_estimate=cost(0.01),
            name="assemble",
        )(ids, *halves)
    else:
        place = jnp.arange(shards * 2, dtype=jnp.int32)
        place = spot[place // 2] * 2 + (place % 2 ^ core)
        weights = jnp.stack([part[:half] for part in halves])[place].reshape(d, wide)
        vec = jnp.stack([part[half:, :256] for part in halves[::2]])[spot]
        vec = vec.reshape(shards, 8, 2, 128)[..., :share].transpose(2, 1, 0, 3)
        vec = vec.reshape(16, d).astype(F32)
        router = jnp.pad(vec[8:16].T, ((0, 0), (0, 120))).astype(BF)

    pack = after(pack, arrived, *others)
    chunks = [(pack, to_column(pack)), (round_ring(pack),)]

    per_image = lambda *tail: pl.BlockSpec((1,) + tail, lambda i: (i,) + (0,) * len(tail))
    made = pl.pallas_call(
        functools.partial(fwd_kernel, parts),
        grid=(own,),
        in_specs=[per_image(pad, d)] * parts
        + [per_image(1, length), whole((d, wide)), whole((16, d))],
        out_specs=[
            per_image(length, 3 * d),
            per_image(length, d),
            per_image(length, 128),
            per_image(length, d),
            per_image(length, d),
            per_image(length, d),
        ]
        + [per_image(pad, d)] * parts,
        out_shape=[
            jax.ShapeDtypeStruct((own, length, 3 * d), BF),
            jax.ShapeDtypeStruct((own, length, d), BF),
            jax.ShapeDtypeStruct((own, length, 128), F32),
            jax.ShapeDtypeStruct((own, length, d), F32),
            jax.ShapeDtypeStruct((own, length, d), BF),
            jax.ShapeDtypeStruct((own, length, d), BF),
        ]
        + [jax.ShapeDtypeStruct((own, pad, d), BF)] * parts,
        compiler_params=params(),
        cost_estimate=cost(0.01),
        name="block_forward",
    )(*toks, mask_bias, weights, vec)
    *made, first_other, second, grads_in[2] = gate(*made, chunks[0][1], chunks[1][0], grads_in[2])
    chunks = [(chunks[0][0], first_other), (second, to_column(second))]
    qkv, attended, lse, residual, z_own, normed = made[:6]
    res_pieces = list(made[6:])

    grads_in[1], grads_in[3] = to_seq(final, 1), to_seq(grads_in[2], 1)

    def tile_spec(shape, index_map):
        return pl.BlockSpec(shape, index_map)

    grad_slots = pl.pallas_call(
        functools.partial(gather_grads_kernel, slots, parts),
        grid_spec=pltpu.PrefetchScalarGridSpec(
            num_scalar_prefetch=1,
            grid=(parts, sub),
            in_specs=[
                tile_spec((TILE, 1, length), lambda k, u, ids: ((ids[0] ^ k) * sub + u, 0, 0))
            ]
            + [tile_spec((TILE, pad, d), lambda k, u, ids: ((ids[0] ^ k) * sub + u, 0, 0))]
            * parts,
            out_specs=tile_spec((1, rows, d), lambda k, u, ids: (k * sub + u, 0, 0)),
        ),
        out_shape=jax.ShapeDtypeStruct((tiles, rows, d), BF),
        compiler_params=params(),
        cost_estimate=cost(0.01),
        name="grad_slots",
    )(ids, slot_rows[0], *grads_in)

    def add(*terms):
        return sum(term.astype(F32) for term in terms)

    def ring_sum(moving, r):
        terms = (packs[r][0], crossed[r]) + (() if moving is None else (moving,))
        return add(*terms)

    z_far = to_seq(z_own, 2)
    z_rows = [z_own, to_seq(z_own, 1), z_far, None]
    if ring_len > 2:
        chunks.append((round_ring(second),))
    x_rows = gr_rows = None
    for k in range(parts):
        chain = () if k == 0 else (x_rows, gr_rows)
        if k == 2:
            z_far, x_rows, gr_rows, second_other, *rest = gate(
                z_far, x_rows, gr_rows, chunks[1][1], *[c[0] for c in chunks[2:]]
            )
            chunks[1] = (chunks[1][0], second_other)
            for r in range(2, ring_len):
                part = rest[0] if r == 2 else round_ring(part)
                chunks[r:] = [(part, to_column(part) if r < ring_len - 1 else part)]
            z_rows[2:] = [z_far, to_seq(z_far, 1)]
            chain = (x_rows, gr_rows)
        x_rows, gr_rows = pl.pallas_call(
            functools.partial(gather_rows_kernel, slots, experts),
            grid_spec=pltpu.PrefetchScalarGridSpec(
                num_scalar_prefetch=1,
                grid=(sub,),
                in_specs=[
                    tile_spec(
                        (TILE, 1, length), lambda u, ids, k=k: ((ids[0] ^ k) * sub + u, 0, 0)
                    ),
                    tile_spec((TILE, length, d), lambda u, ids: (u, 0, 0)),
                    tile_spec((1, rows, d), lambda u, ids, k=k: (k * sub + u, 0, 0)),
                    whole((d, 128)),
                ]
                + [pl.BlockSpec(memory_space=pl.ANY)] * len(chain),
                out_specs=[
                    tile_spec((1, rows, d), lambda u, ids, k=k: (k * sub + u, 0, 0)),
                    tile_spec((1, rows, d), lambda u, ids, k=k: (k * sub + u, 0, 0)),
                ],
            ),
            out_shape=[jax.ShapeDtypeStruct((tiles, rows, d), BF)] * 2,
            input_output_aliases={5: 0, 6: 1} if chain else {},
            compiler_params=params(),
            cost_estimate=cost(0.01),
            name="slot_rows",
        )(ids, slot_rows[k], z_rows[k], grad_slots, router, *chain)

    tile3 = pl.BlockSpec((1, rows, d), lambda t, *_: (t, 0, 0))
    pack_rows = 2 * fs + 16
    acc_out = acc_gx = None
    packs = []
    crossed = {}
    moving = None
    for r in range(ring_len):
        e0, e1 = chunks[r]
        is_first, is_last = r == 0, r == ring_len - 1
        operands = [e0, e1, x_rows, gr_rows]
        in_specs = [
            whole((pack_rows, d)),
            whole((pack_rows, d)),
            tile3,
            tile3,
        ]
        aliases = {}
        if not is_first:
            operands += [acc_out, acc_gx]
            in_specs += [tile3, tile3]
            aliases = {4: 2} if is_last else {4: 2, 5: 3}
        pack_shape = jax.ShapeDtypeStruct((pack_rows, d), BF)
        out_specs = [whole((pack_rows, d)), whole((pack_rows, d)), tile3, tile3]
        acc_shape = jax.ShapeDtypeStruct((tiles, rows, d), F32)
        out_shape = [pack_shape, pack_shape, acc_shape, acc_shape]
        if is_last:
            operands += [grad_slots, vec]
            in_specs += [tile3, whole((16, d))]
            out_specs[3:] = [
                pl.BlockSpec(
                    (TILE, slots + 8, d), lambda t, k=k: (jnp.clip(t - k * sub, 0, sub - 1), 0, 0)
                )
                for k in range(parts)
            ]
            out_shape[3:] = [jax.ShapeDtypeStruct((own, slots + 8, d), BF)] * parts
        made = pl.pallas_call(
            functools.partial(expert_kernel, is_first, is_last, slots, experts, fs),
            grid_spec=pltpu.PrefetchScalarGridSpec(
                num_scalar_prefetch=0,
                grid=(tiles,),
                in_specs=in_specs,
                out_specs=out_specs,
                scratch_shapes=[
                    pltpu.VMEM((2 * fs, d), BF),
                    pltpu.VMEM((2 * fs, d), BF),
                    pltpu.VMEM((2 * fs, d), F32),
                    pltpu.VMEM((2 * fs, d), F32),
                    pltpu.VMEM((8, 2 * fs), F32),
                    pltpu.VMEM((8, d), F32),
                    pltpu.VMEM((8, 2 * fs), F32),
                ],
            ),
            out_shape=out_shape,
            input_output_aliases=aliases,
            compiler_params=params(),
            cost_estimate=cost(50),
            name="expert_pair",
        )(*operands)
        ready = {}
        if r == 0:
            ready = {("in", q, p): chunks[q][p] for q in range(2, ring_len) for p in (0, 1)}
            ready.pop(("in", ring_len - 1, 1), None)
        elif r == 1:
            ready[("in", ring_len - 1, 1)] = chunks[ring_len - 1][1]
            ready.update({("piece", j): res_pieces[j] for j in range(1, parts)})
        else:
            ready[("out", r - 1, 1)] = crossed[r - 1]
            if moving is not None:
                ready["moving"] = moving
            if r == 2:
                ready.update({("res", j): res_in[j] for j in range(1, parts)})
        values = gate(*made, *ready.values())
        made, ready = values[: len(made)], dict(zip(ready, values[len(made) :]))
        for key, value in ready.items():
            if key == "moving":
                moving = value
            elif key[0] == "in":
                chunks[key[1]] = tuple(value if p == key[2] else chunks[key[1]][p] for p in (0, 1))
            elif key[0] == "out":
                crossed[key[1]] = value
            elif key[0] == "piece":
                res_pieces[key[1]] = value
            else:
                res_in[key[1]] = value
        packs.append(made[:2])
        acc_out, acc_gx = made[2:4]
        if r == 0 and ring_len > 2:
            chunks[ring_len - 1] = (chunks[ring_len - 1][0], to_column(chunks[ring_len - 1][0]))
        if r >= 1:
            crossed[r] = to_column(packs[r][1])
        if r >= 2:
            moving = round_ring(ring_sum(moving, r - 1).astype(BF))
        if r == 1:
            res_in = [res_pieces[0]] + [to_seq(res_pieces[j], j) for j in range(1, parts)]
    gx = made[3 : 3 + parts]

    gx_in = [gx[k] if k == 0 else to_seq(gx[k], k) for k in range(parts)]
    mixed = pl.pallas_call(
        functools.partial(weigh_kernel, slots, experts),
        grid_spec=pltpu.PrefetchScalarGridSpec(
            num_scalar_prefetch=1,
            grid=(tiles,),
            in_specs=[
                tile3,
                tile3,
                whole((d, 128)),
                whole((16, d)),
                whole((rows, rows)),
            ],
            out_specs=[
                *[pl.BlockSpec((1, TILE * CAP, d), lambda t, *_: (t, 0, 0))] * parts,
            ],
        ),
        out_shape=[
            *[jax.ShapeDtypeStruct((tiles, TILE * CAP, d), BF)] * parts,
        ],
        compiler_params=params(),
        cost_estimate=cost(50),
        name="weigh",
    )(ids, acc_out, x_rows, router, vec, reorder)
    last = ring_len - 1
    own_meta, moving, crossed[last], *rest = gate(
        own_meta, moving, crossed[last], *gx_in[1:], *mixed
    )
    gx_in[1:], mixed = rest[: parts - 1], rest[parts - 1 :]
    mixed_in = [mixed[0]] + [to_seq(mixed[k], k) for k in range(1, parts)]
    moving = round_ring(ring_sum(moving, last).astype(BF))
    crossed[0] = to_column(packs[0][1])

    side = me // 2
    quarter = share // 4

    def shift_ring(v, k):
        return lax.ppermute(v, "fsdp", [(n, (n + 2 * k) % shards) for n in range(shards)])

    def core_pair(made):
        if len(made) == 1:
            split = made[0].reshape(shards, 2, 2, quarter, made[0].shape[-1])
            made = index(split, core, 2), index(split, 1 - core, 2)
        return made[0], to_seq(made[1], 1)

    def over_y(keep, come=None):
        pair = [v for v in (keep, come) if v is not None]
        send = add(*[index(v, 1 - side, 1) for v in pair]).astype(BF)
        return add(*[index(v, side, 1) for v in pair], to_seq(send, 2)).astype(BF)

    def over_x(keep, come=None):
        pair = [v.reshape(ring_len, 2, *v.shape[1:]) for v in (keep, come) if v is not None]
        send = add(*[index(v, 1 - column, 1) for v in pair]).astype(BF)
        return add(*[index(v, column, 1) for v in pair], to_column(send)).astype(BF)

    def over_ring(v):
        far = [
            shift_ring(index(v, (ring_at + k) % ring_len), k) for k in range(1, ring_len)
        ]
        return add(index(v, ring_at), *far).astype(BF)

    def in_order(pieces):
        a, b, c, e = pieces
        near = [jnp.where(core == 0, a, b), jnp.where(core == 0, b, a)]
        far = [jnp.where(core == 0, c, e), jnp.where(core == 0, e, c)]
        front = [jnp.where(side == 0, u, v) for u, v in zip(near, far)]
        back = [jnp.where(side == 0, v, u) for u, v in zip(near, far)]
        return jnp.concatenate(front + back, axis=0)

    def spread_rows(v):
        return in_order([v] + [to_seq(v, k) for k in range(1, parts)]).astype(F32)

    image3 = lambda *tail: pl.BlockSpec((1,) + tail, lambda i, *_: (i,) + (0,) * len(tail))
    width = d // 2
    column3 = lambda n: pl.BlockSpec((1, length, width), lambda i, *_: (i, 0, n))
    weight3 = lambda n: pl.BlockSpec((d, width), lambda i, *_: (0, n))
    partial_shape = jax.ShapeDtypeStruct((own, length, d), F32)
    def grad_outs(cols):
        if quarter % 8:
            return [whole((d, cols))], [jax.ShapeDtypeStruct((d, cols), BF)]
        shape = (shards, 2, quarter, cols)
        return [whole(shape)] * 2, [jax.ShapeDtypeStruct(shape, BF)] * 2

    grad_specs, grad_shapes = grad_outs(d + 3 * width)
    grad_att, grad_res, after_first, small, *first = pl.pallas_call(
        functools.partial(back_first_kernel, parts, experts, slots, len(grad_specs)),
        grid_spec=pltpu.PrefetchScalarGridSpec(
            num_scalar_prefetch=1,
            grid=(own,),
            in_specs=[image3(length, parts)]
            + [image3(slots + 8, d)] * parts
            + [pl.BlockSpec((1, pad, d), lambda i, ids: (ids[0] * own + i, 0, 0))] * parts
            + [
                image3(length, d),
                image3(length, d),
                image3(length, d),
                pl.BlockSpec((d, d), lambda i, ids: (0, 3)),
                whole((16, d)),
                whole((d, 128)),
                image3(1, length),
                column3(0),
                column3(2),
                column3(4),
                image3(length, 128),
                image3(length, d),
                weight3(0),
                weight3(2),
                weight3(4),
            ],
            out_specs=[
                image3(length, d),
                image3(length, d),
                image3(length, d),
                whole((16, d)),
                *grad_specs,
            ],
            scratch_shapes=[
                pltpu.VMEM((d, d), F32),
                pltpu.VMEM((d, 3 * width), F32),
                pltpu.VMEM((16, d), F32),
                pltpu.VMEM((d, 128), F32),
                pltpu.VMEM((length, 3 * width), BF),
            ],
        ),
        out_shape=[
            jax.ShapeDtypeStruct((own, length, d), BF),
            partial_shape,
            partial_shape,
            jax.ShapeDtypeStruct((16, d), F32),
            *grad_shapes,
        ],
        compiler_params=params(),
        cost_estimate=cost(50),
        name="back_first",
    )(
        ids,
        own_meta,
        *gx_in,
        *grads_in,
        attended,
        residual,
        z_own,
        weights,
        vec,
        router,
        mask_bias,
        qkv,
        qkv,
        qkv,
        lse,
        normed,
        weights,
        weights,
        weights,
    )
    grad_att, grad_res, after_first, small, moving, crossed[0], *rest = gate(
        grad_att, grad_res, after_first, small, moving, crossed[0], *mixed_in[1:], *first
    )
    mixed_in[1:], first = rest[: parts - 1], rest[parts - 1 :]
    first = core_pair(first)
    grad_specs, grad_shapes = grad_outs(3 * width + 128)
    made = pl.pallas_call(
        functools.partial(back_second_kernel, parts, len(grad_specs)),
        grid_spec=pltpu.PrefetchScalarGridSpec(
        num_scalar_prefetch=1,
        grid=(own,),
        in_specs=[
            image3(1, length),
            column3(1),
            column3(3),
            column3(5),
            image3(length, d),
            image3(length, d),
            image3(length, 128),
            image3(length, d),
            weight3(1),
            weight3(3),
            weight3(5),
            whole((16, d)),
            image3(length, d),
            image3(length, d),
            whole((16, d)),
        ]
        + [image3(pad, d)] * parts,
        out_specs=[image3(pad, d)] * parts + grad_specs,
        scratch_shapes=[
            pltpu.VMEM((d, 3 * width), F32),
            pltpu.VMEM((128, d), F32),
            pltpu.VMEM((d, 128), F32),
            pltpu.VMEM((length, 3 * width), BF),
        ],
        ),
        out_shape=[jax.ShapeDtypeStruct((own, pad, d), BF)] * parts + grad_shapes,
        compiler_params=params(),
        cost_estimate=cost(50),
        name="back_second",
    )(
        ids,
        mask_bias,
        qkv,
        qkv,
        qkv,
        attended,
        grad_att,
        lse,
        normed,
        weights,
        weights,
        weights,
        small,
        after_first,
        grad_res,
        vec,
        *toks,
    )
    token_pieces, second = made[:parts], made[parts:]
    far_first, moving, crossed[0], *rest = gate(
        first[1], moving, crossed[0], *token_pieces, *mixed_in[1:], *second
    )
    first = (first[0], far_first)
    token_pieces, mixed_in[1:], second = (
        rest[:parts],
        rest[parts : 2 * parts - 1],
        rest[2 * parts - 1 :],
    )

    image_block = pl.BlockSpec(
        (TILE, block_len, d), lambda j, u, ids: ((ids[0] ^ j) * sub + u, 0, 0)
    )
    output = pl.pallas_call(
        functools.partial(combine_kernel, parts),
        grid_spec=pltpu.PrefetchScalarGridSpec(
            num_scalar_prefetch=1,
            grid=(parts, sub),
            in_specs=[
                pl.BlockSpec((TILE, pad, 8), lambda j, u, ids: ((ids[0] ^ j) * sub + u, 0, 0))
            ]
            + [pl.BlockSpec((TILE, pad, d), lambda j, u, ids: (u, 0, 0))] * parts
            + [
                pl.BlockSpec(
                    (1, TILE * CAP, d), lambda j, u, ids, k=k: ((j ^ k) * sub + u, 0, 0)
                )
                for k in range(parts)
            ],
            out_specs=image_block,
        ),
        out_shape=jax.ShapeDtypeStruct((images, block_len, d), BF),
        compiler_params=params(),
        cost_estimate=cost(50),
        name="combine",
    )(ids, mix_meta, *res_in, *mixed_in)

    first_x = over_x(*first)
    second = core_pair(second)
    second_y = over_y(*second)
    tokens_in = [token_pieces[j] if j == 0 else to_seq(token_pieces[j], j) for j in range(parts)]
    first_x, second_y, output, *tokens_in = gate(first_x, second_y, output, *tokens_in)
    first_own, second_x = over_y(first_x), over_x(second_y)
    grad_tokens = in_order(tokens_in)[:, :block_len]
    first_own, second_x, grad_tokens = gate(first_own, second_x, grad_tokens)
    both_x = jnp.concatenate([first_own, second_x], axis=-1)
    total = ring_sum(moving, 0)
    grad_hidden = total[None, :fs]
    grad_expert_out = total[None, fs : 2 * fs]
    grad_hidden_bias = total[2 * fs : 2 * fs + 1, :fs]
    grad_out_bias = lax.dynamic_slice(total, (2 * fs + 1, rank * share), (1, share))
    own_rows = over_ring(both_x)
    mine = spread_rows(own_rows)
    grad_proj = mine[:, :d]
    at_b, at_small = d + 3 * width, d + 6 * width
    grad_qkv = jnp.concatenate(
        [
            mine[:, start + n * width : start + (n + 1) * width]
            for n in range(3)
            for start in (d, at_b)
        ],
        axis=1,
    )
    small = mine[:, at_small : at_small + 16].T
    grad_router = mine[:, at_small + 8 : at_small + 8 + experts]

    return (
        output,
        grad_tokens,
        small[0],
        small[1],
        grad_qkv,
        small[2],
        small[3],
        grad_proj,
        small[4],
        small[5],
        small[6],
        grad_router,
        grad_hidden,
        grad_hidden_bias,
        grad_expert_out,
        grad_out_bias,
    )


def solution(mesh):
    in_specs = (
        P("fsdp", "seq", None),
        P("fsdp", None),
        P("fsdp", "seq", None),
        P("fsdp", "seq", None),
        P("fsdp"),
        P("fsdp"),
        P("fsdp", None),
        P("fsdp"),
        P("fsdp"),
        P("fsdp", None),
        P("fsdp"),
        P("fsdp"),
        P("fsdp"),
        P("fsdp", None),
        P("seq", "fsdp", None),
        P("seq", "fsdp"),
        P("seq", "fsdp", None),
        P("seq", "fsdp"),
    )
    out_specs = (
        P("fsdp", "seq", None),
        P("fsdp", "seq", None),
        P("fsdp"),
        P("fsdp"),
        P("fsdp", None),
        P("fsdp"),
        P("fsdp"),
        P("fsdp", None),
        P("fsdp"),
        P("fsdp"),
        P("fsdp"),
        P("fsdp", None),
        P("seq", "fsdp", None),
        P("seq", "fsdp"),
        P("seq", "fsdp", None),
        P("seq", "fsdp"),
    )
    return jax.shard_map(body, mesh=mesh, in_specs=in_specs, out_specs=out_specs, check_vma=False)
```

```python
import functools

import jax
import jax.numpy as jnp
from jax import lax
from jax.experimental import pallas as pl
from jax.experimental.pallas import tpu as pltpu
from jax.sharding import PartitionSpec as P

HEAD_DIM = 64
TOP = 2
CAP = 30
TILE = 4
EPS = 1e-06
NEG = -1e30
BF = jnp.bfloat16
F32 = jnp.float32
VMEM = 66_500_000


def nn(a, b):
    return jnp.dot(a, b, preferred_element_type=F32)


def nt(a, b):
    return lax.dot_general(a, b, (((1,), (1,)), ((), ())), preferred_element_type=F32)


def tn(a, b):
    return lax.dot_general(a, b, (((0,), (0,)), ((), ())), preferred_element_type=F32)


def stats(v):
    center = v - jnp.mean(v, axis=-1, keepdims=True)
    r = lax.rsqrt(jnp.mean(center * center, axis=-1, keepdims=True) + EPS)
    return center * r, r


def norm_back(u, gain, vhat, r):
    ug = u * gain
    return r * (
        ug
        - jnp.mean(ug, axis=-1, keepdims=True)
        - vhat * jnp.mean(ug * vhat, axis=-1, keepdims=True)
    )


def rows_of(refs, i=0):
    return jnp.concatenate([ref[i].astype(F32) for ref in refs], axis=0)


def params(**kw):
    return pltpu.CompilerParams(vmem_limit_bytes=VMEM, **kw)


def cost(us):
    return pl.CostEstimate(flops=int(us * 1e9), bytes_accessed=int(us * 1e4), transcendentals=0)


def half_masks():
    lane = lax.broadcasted_iota(jnp.int32, (1, 2 * HEAD_DIM), 1)
    first = (lane < HEAD_DIM).astype(F32)
    return first, 1.0 - first


def fwd_kernel(parts, *refs):
    toks, refs = refs[:parts], refs[parts:]
    mask_ref, w_ref, vec_ref, qkv_ref, att_ref, lse_ref, res_ref, z_ref, normed_ref = refs[:9]
    sends = refs[9:]
    x = rows_of(toks)
    d = x.shape[1]
    vec = vec_ref[...]
    vhat, _ = stats(x)
    normed = (vhat * vec[0:1] + vec[1:2]).astype(BF)
    normed_ref[0] = normed
    qkv_ref[0, :, 0:d] = (nn(normed, w_ref[:, 0:d]) + vec[2:3]).astype(BF)
    qkv_ref[0, :, d : 2 * d] = nn(normed, w_ref[:, d : 2 * d]).astype(BF)
    qkv_ref[0, :, 2 * d : 3 * d] = (nn(normed, w_ref[:, 2 * d : 3 * d]) + vec[3:4]).astype(BF)
    bias = mask_ref[0]
    first, second = half_masks()
    scale = HEAD_DIM ** (-0.5)
    lane = lax.broadcasted_iota(jnp.int32, (x.shape[0], 128), 1)
    lse = jnp.zeros((x.shape[0], 128), F32)
    for pair in range(d // 128):
        q2 = qkv_ref[0, :, 128 * pair : 128 * pair + 128]
        k2 = qkv_ref[0, :, d + 128 * pair : d + 128 * pair + 128]
        v2 = qkv_ref[0, :, 2 * d + 128 * pair : 2 * d + 128 * pair + 128]
        outs = []
        for a, half in enumerate((first, second)):
            qa = q2 * (half * scale).astype(BF)
            s = nt(qa, k2) + bias
            top = jnp.max(s, axis=-1, keepdims=True)
            e = jnp.exp(s - top)
            total = jnp.sum(e, axis=-1, keepdims=True)
            outs.append(nn(e.astype(BF), v2) * (1.0 / total))
            lse = jnp.where(lane == 2 * pair + a, top + jnp.log(total), lse)
        att = jnp.where(first > 0, outs[0], outs[1])
        att_ref[0, :, 128 * pair : 128 * pair + 128] = att.astype(BF)
    lse_ref[0] = lse
    res = x + nn(att_ref[0], w_ref[:, 3 * d : 4 * d]) + vec[4:5]
    res_ref[0] = res
    zhat, _ = stats(res)
    z_ref[0] = (zhat * vec[5:6] + vec[6:7]).astype(BF)
    block = x.shape[0] // parts
    for j, ref in enumerate(sends):
        ref[0] = res[j * block : (j + 1) * block].astype(BF)


def spread(row, slots, values):
    length = values.shape[0]
    hot = (lax.broadcasted_iota(jnp.int32, (slots, length), 0) == row).astype(BF)
    return nn(hot, values)


def gather_grads_kernel(slots, parts, ids_ref, slot_ref, *refs):
    out = []
    for i in range(TILE):
        values = rows_of(refs[:parts], i).astype(BF)
        out.append(spread(slot_ref[i], slots, values))
    refs[parts][0] = jnp.concatenate(out, axis=0).astype(BF)


def router_probs(rows, router, experts):
    logits = nn(rows, router)
    lane = lax.broadcasted_iota(jnp.int32, logits.shape, 1)
    logits = jnp.where(lane < experts, logits, NEG)
    e = jnp.exp(logits - jnp.max(logits, axis=-1, keepdims=True))
    return e / jnp.sum(e, axis=-1, keepdims=True), lane


def gather_rows_kernel(slots, experts, ids_ref, slot_ref, z_ref, g_ref, router_ref, *refs):
    x_ref, gr_ref = refs[-2:]
    out = [spread(slot_ref[i], slots, z_ref[i]) for i in range(TILE)]
    x = jnp.concatenate(out, axis=0).astype(BF)
    probs, lane = router_probs(x, router_ref[...], experts)
    gate = jnp.sum(jnp.where(lane == ids_ref[0], probs, 0.0), axis=-1, keepdims=True)
    x_ref[0] = x
    gr_ref[0] = (gate * g_ref[0].astype(F32)).astype(BF)


def gelu_parts(v):
    e = jnp.exp(-0.5 * v * v)
    den = 1.0 + 0.23164189 * jnp.abs(v)
    t = pl.reciprocal(den, approx=True)
    t = t * (2.0 - den * t)
    poly = t * (
        0.127414796 + t * (-0.142248368 + t * (0.7107068705 + t * (-0.7265760135 + t * 0.5307027145)))
    )
    tail = poly * e
    cdf = jnp.where(v >= 0, 1.0 - tail, tail)
    return v * cdf, cdf + v * (0.3989422804 * e)


def expert_kernel(first, last, slots, experts, fs, *refs):
    e0, e1, x_ref, gr_ref = refs[:4]
    refs = list(refs[4:])
    if not first:
        acc_out_in, acc_gx_in = refs[:2]
        refs = refs[2:]
    if last:
        g_ref, bo_ref, refs = refs[0], refs[1], refs[2:]
    p0, p1, acc_out = refs[:3]
    gx_refs, refs = refs[3:-7], refs[-7:]
    wh, wo, gwh, gwo, gbh, gbo, bias = refs
    step = pl.program_id(0)

    @pl.when(step == 0)
    def _():
        wh[0:fs] = e0[0:fs]
        wh[fs : 2 * fs] = e1[0:fs]
        wo[0:fs] = e0[fs : 2 * fs]
        wo[fs : 2 * fs] = e1[fs : 2 * fs]
        both = [e[2 * fs : 2 * fs + 16, 0:fs].astype(F32)[0:8] for e in (e0, e1)]
        bias[...] = jnp.concatenate(both, axis=1)
        gwh[...] = jnp.zeros_like(gwh)
        gwo[...] = jnp.zeros_like(gwo)
        gbh[...] = jnp.zeros_like(gbh)
        gbo[...] = jnp.zeros_like(gbo)

    x = x_ref[0]
    gr = gr_ref[0]
    pre = nt(x, wh[...]) + bias[0:1]
    act, slope = gelu_parts(pre)
    hidden = act.astype(BF)
    out = nn(hidden, wo[...])
    grad_pre_f = nt(gr, wo[...]) * slope
    grad_pre = grad_pre_f.astype(BF)
    gx = nn(grad_pre, wh[...])
    gwh[...] += tn(grad_pre, x)
    gwo[...] += tn(hidden, gr)
    gbh[0:1] += jnp.sum(grad_pre_f, axis=0, keepdims=True)
    gbo[0:1] += jnp.sum(gr.astype(F32), axis=0, keepdims=True)
    if not first:
        out = out + acc_out_in[0]
        gx = gx + acc_gx_in[0]
    acc_out[0] = out
    if last:
        dots = jnp.sum((out + bo_ref[7:8]) * g_ref[0].astype(F32), axis=-1, keepdims=True)
        sub = lax.broadcasted_iota(jnp.int32, (8, x.shape[1]), 0)
        fill = jnp.zeros((128 - slots, 128), F32)
        wide_fill = jnp.zeros((8, x.shape[1] - 128), F32)
        out_rows = []
        for i in range(TILE):
            col = jnp.broadcast_to(dots[i * slots : (i + 1) * slots], (slots, 128))
            row = jnp.concatenate([col, fill], axis=0).T[0:8]
            row = jnp.concatenate([row, wide_fill], axis=1)
            high = row.astype(BF).astype(F32)
            row = jnp.where(sub == 0, high, jnp.where(sub == 1, row - high, 0.0))
            out_rows += [gx[i * slots : (i + 1) * slots], row]
        gx = jnp.concatenate(out_rows, axis=0).reshape(TILE, slots + 8, -1).astype(BF)
        for k, ref in enumerate(gx_refs):

            @pl.when(step // (pl.num_programs(0) // len(gx_refs)) == k)
            def _(ref=ref):
                ref[...] = gx
    else:
        gx_refs[0][0] = gx

    @pl.when(step == pl.num_programs(0) - 1)
    def _():
        d = gwh.shape[1]
        for i, pack in enumerate((p0, p1)):
            pack[0:fs] = gwh[i * fs : (i + 1) * fs].astype(BF)
            pack[fs : 2 * fs] = gwo[i * fs : (i + 1) * fs].astype(BF)
            row = jnp.broadcast_to(gbh[0:1, i * fs : (i + 1) * fs], (16, fs))
            row = jnp.concatenate([row, jnp.zeros((16, d - fs), F32)], axis=1)
            sub = lax.broadcasted_iota(jnp.int32, (16, d), 0)
            pack[2 * fs : 2 * fs + 16] = jnp.where(
                sub == 0, row, jnp.where(sub == 1, gbo[0:1], 0.0)
            ).astype(BF)


def weigh_kernel(slots, experts, ids_ref, out_ref, x_ref, router_ref, bo_ref, perm_ref, *mixed_refs):
    x = x_ref[0]
    out = out_ref[0] + bo_ref[7:8]
    probs, lane = router_probs(x, router_ref[...], experts)
    gate = jnp.sum(jnp.where(lane == ids_ref[0], probs, 0.0), axis=-1, keepdims=True)
    weighted = nn(perm_ref[...], (gate * out).astype(BF))
    count = weighted.shape[0] // len(mixed_refs)
    for k, ref in enumerate(mixed_refs):
        ref[0] = weighted[k * count : (k + 1) * count].astype(BF)


def combine_kernel(parts, ids_ref, meta_ref, *refs):
    res, rows, out_ref = refs[:parts], refs[parts : 2 * parts], refs[2 * parts]
    step = pl.program_id(0)
    block, length = meta_ref.shape[1], out_ref.shape[1]
    meta = meta_ref[...].reshape(TILE * block, 8)
    total = 0.0
    for k, ref in enumerate(rows):
        slot = lax.broadcasted_iota(jnp.int32, (TILE * block, ref.shape[1]), 1)
        total += nn((slot == meta[:, k : k + 1]).astype(BF), ref[0])
    live = meta[:, 4:5].astype(F32)
    for j in range(parts):

        @pl.when(step == j)
        def _(j=j):
            base = res[j][...].astype(F32).reshape(TILE * block, -1)
            out = ((base + total) * live).reshape(TILE, block, -1)
            out_ref[...] = out[:, :length].astype(BF)


def norm_part(parts, experts, slots, refs, accs, ids_ref, i):
    meta_ref, gx_refs, g_refs, att_ref, res_ref, z_ref, w_ref, vec_ref, router_ref = refs
    acc_proj, acc_small, acc_router = accs
    length, d = res_ref.shape[1:]
    meta = meta_ref[0]
    lane = lax.broadcasted_iota(jnp.int32, (length, 128), 1)
    dz = jnp.zeros((length, d), F32)
    grad_probs = jnp.zeros((length, 128), F32)
    for k in range(parts):
        hot = lane == meta[:, k : k + 1]
        dz += nn(hot.astype(BF), gx_refs[k][0])
        dots = gx_refs[k][0, slots - 8 : slots + 8, 0:128].astype(F32)
        dots = dots[8:9] + dots[9:10]
        of_token = jnp.sum(jnp.where(hot, dots, 0.0), axis=-1, keepdims=True)
        grad_probs = jnp.where(lane == (ids_ref[0] ^ k), of_token, grad_probs)
    z = z_ref[0]
    probs, _ = router_probs(z, router_ref[...], experts)
    grad_logits = probs * (grad_probs - jnp.sum(probs * grad_probs, axis=-1, keepdims=True))
    grad_logits = grad_logits.astype(BF)
    dz += nt(grad_logits, router_ref[...])
    acc_router[...] += tn(z, grad_logits)
    zhat, r2 = stats(res_ref[0])
    acc_small[5:6] += jnp.sum(dz * zhat, axis=0, keepdims=True)
    acc_small[6:7] += jnp.sum(dz, axis=0, keepdims=True)
    grad_res = rows_of(g_refs) + norm_back(dz, vec_ref[5:6], zhat, r2)
    branch = grad_res.astype(BF)
    acc_small[4:5] += jnp.sum(branch.astype(F32), axis=0, keepdims=True)
    acc_proj[...] += tn(att_ref[0], branch)
    return grad_res, nt(branch, w_ref[...]).astype(BF)


def heads_part(half, mask_ref, qkv_refs, att_ref, ga_ref, lse_ref, normed_ref, w_refs, acc, acc_small, gqkv):
    q_ref, k_ref, v_ref = qkv_refs
    width = q_ref.shape[2]
    spot = half * width
    bias = mask_ref[0]
    lse = lse_ref[0]
    first, second = half_masks()
    scale = HEAD_DIM ** (-0.5)
    for pair in range(width // 128):
        at = 128 * pair
        here = slice(spot + at, spot + at + 128)
        q2 = q_ref[0, :, at : at + 128]
        k2 = k_ref[0, :, at : at + 128]
        v2 = v_ref[0, :, at : at + 128]
        g2 = ga_ref[0, :, here]
        prod = g2.astype(F32) * att_ref[0, :, here].astype(F32)
        gq, gk, gv = [], 0.0, 0.0
        for a, mask in enumerate((first, second)):
            qa = q2 * (mask * scale).astype(BF)
            ga = g2 * mask.astype(BF)
            head = half * (width // HEAD_DIM) + 2 * pair + a
            probs = jnp.exp(nt(qa, k2) + bias - lse[:, head : head + 1])
            delta = jnp.sum(prod * mask, axis=-1, keepdims=True)
            grad_scores = (probs * (nt(ga, v2) - delta)).astype(BF)
            gq.append(nn(grad_scores, k2))
            gk += tn(grad_scores, qa)
            gv += tn(probs.astype(BF), ga)
        gqkv[:, at : at + 128] = (jnp.where(first > 0, gq[0], gq[1]) * scale).astype(BF)
        gqkv[:, width + at : width + at + 128] = gk.astype(BF)
        gqkv[:, 2 * width + at : 2 * width + at + 128] = gv.astype(BF)
    acc_small[2:3, spot : spot + width] += jnp.sum(
        gqkv[:, 0:width].astype(F32), axis=0, keepdims=True
    )
    acc_small[3:4, spot : spot + width] += jnp.sum(
        gqkv[:, 2 * width : 3 * width].astype(F32), axis=0, keepdims=True
    )
    acc[...] += tn(normed_ref[0], gqkv[...])
    return sum(
        nt(gqkv[:, n * width : (n + 1) * width], w_ref[...]) for n, w_ref in enumerate(w_refs)
    )


def split_rows(outs, accs, core):
    col = 0
    for acc in accs:
        cols = slice(col, col + acc.shape[1])
        col += acc.shape[1]
        if len(outs) == 1:
            outs[0][:, cols] = acc[...].astype(BF)
            continue
        for out, which in zip(outs, (core, 1 - core)):
            shards, sides, count = out.shape[:3]
            for n in range(shards * sides):
                row = pl.multiple_of((2 * n + which) * count, 8)
                out[n // sides, n % sides, :, cols] = acc[pl.ds(row, count)].astype(BF)


def taker(refs):
    refs = list(refs)

    def take(n):
        out = refs[:n]
        del refs[:n]
        return out

    return take


def back_first_kernel(parts, experts, slots, outs, ids_ref, *refs):
    take = taker(refs)
    (meta_ref,) = take(1)
    norm_refs = [meta_ref, take(parts), take(parts)]
    att_ref, res_ref, z_ref, wp_ref, vec_ref, router_ref = take(6)
    norm_refs += [att_ref, res_ref, z_ref, wp_ref, vec_ref, router_ref]
    (mask_ref,) = take(1)
    qkv_refs = take(3)
    lse_ref, normed_ref = take(2)
    w_refs = take(3)
    ga_ref, gres_ref, dn_ref, small_ref = take(4)
    grads_refs = take(outs)
    acc_proj, acc, acc_small, acc_router, gqkv = take(5)
    i = pl.program_id(0)

    @pl.when(i == 0)
    def _():
        for part in (acc_proj, acc, acc_small, acc_router):
            part[...] = jnp.zeros_like(part)

    accs = (acc_proj, acc_small, acc_router)
    gres_ref[0], ga_ref[0] = norm_part(parts, experts, slots, norm_refs, accs, ids_ref, i)
    dn_ref[0] = heads_part(
        0, mask_ref, qkv_refs, att_ref, ga_ref, lse_ref, normed_ref, w_refs, acc, acc_small, gqkv
    )

    @pl.when(i == pl.num_programs(0) - 1)
    def _():
        acc_small[8:16] = acc_router[...].T[0:8]
        small_ref[...] = acc_small[...]
        split_rows(grads_refs, (acc_proj, acc), ids_ref[0] % 2)


def back_second_kernel(parts, outs, ids_ref, *refs):
    take = taker(refs)
    (mask_ref,) = take(1)
    qkv_refs = take(3)
    att_ref, ga_ref, lse_ref, normed_ref = take(4)
    w_refs = take(3)
    small_in, dn_in, gres_ref, vec_ref = take(4)
    toks, gt_refs = take(parts), take(parts)
    grads_refs = take(outs)
    acc, acc_small, acc_turned, gqkv = take(4)
    i = pl.program_id(0)

    @pl.when(i == 0)
    def _():
        acc[...] = jnp.zeros_like(acc)
        acc_small[0:16] = small_in[...]
        acc_small[16:128] = jnp.zeros((112, acc_small.shape[1]), F32)

    dn = dn_in[0] + heads_part(
        1, mask_ref, qkv_refs, att_ref, ga_ref, lse_ref, normed_ref, w_refs, acc, acc_small, gqkv
    )
    x = rows_of(toks)
    vhat, r1 = stats(x)
    acc_small[0:1] += jnp.sum(dn * vhat, axis=0, keepdims=True)
    acc_small[1:2] += jnp.sum(dn, axis=0, keepdims=True)
    grad_tok = gres_ref[0] + norm_back(dn, vec_ref[0:1], vhat, r1)
    block = x.shape[0] // parts
    for j, ref in enumerate(gt_refs):
        ref[0] = grad_tok[j * block : (j + 1) * block].astype(BF)

    @pl.when(i == pl.num_programs(0) - 1)
    def _():
        acc_turned[...] = acc_small[...].T
        split_rows(grads_refs, (acc, acc_turned), ids_ref[0] % 2)


def assemble_kernel(ring_len, half, share, ids_ref, *refs):
    parts, (out_ref, vec_ref, router_ref) = refs[:-3], refs[-3:]
    ring_at, column = ids_ref[1] // 2, ids_ref[1] % 2
    core = ids_ref[0] % 2
    d = vec_ref.shape[1]
    vec = jnp.zeros((16, d), F32)
    at = 0
    for r in range(ring_len):
        for p in range(2):
            shard = lax.rem(ring_at + ring_len - r, ring_len) * 2 + (column ^ p)
            for c in range(2):
                row = pl.multiple_of((shard * 2 + (core ^ c)) * half, half)
                out_ref[pl.ds(row, half)] = parts[at][0:half]
                if c == 0:
                    few = parts[at][half : half + 8, 0:256].astype(F32)
                    few = jnp.concatenate([few[:, 0:128], few[:, 128:256]], axis=0).astype(BF)
                    source = lax.broadcasted_iota(jnp.int32, (128, d), 0)
                    target = lax.broadcasted_iota(jnp.int32, (128, d), 1) - shard * share
                    vec += nn(few, ((source == target) & (source < share)).astype(BF))
                at += 1
    vec_ref[...] = vec
    fill = jnp.zeros((120, d), F32)
    router_ref[...] = jnp.concatenate([vec[8:16], fill], axis=0).T.astype(BF)


def whole(shape):
    return pl.BlockSpec(shape, lambda *_: (0,) * len(shape))


def body(
    tokens,
    key_mask,
    routes,
    out_grad,
    norm1_gain,
    norm1_bias,
    w_qkv,
    bias_q,
    bias_v,
    w_proj,
    bias_proj,
    norm2_gain,
    norm2_bias,
    w_router,
    w_hidden,
    bias_hidden,
    w_expert_out,
    bias_expert_out,
):
    images, block_len, d = tokens.shape
    parts = lax.axis_size("seq")
    shards = lax.axis_size("fsdp")
    experts = parts
    ring_len = shards // 2
    own = images // parts
    sub = own // TILE
    tiles = parts * sub
    pad = -(-block_len // 8) * 8
    length = parts * pad
    slots = parts * CAP
    rows = TILE * slots
    fs = w_hidden.shape[1]
    share = d // shards
    half = share // 2
    me = lax.axis_index("seq")
    rank = lax.axis_index("fsdp")
    ring_at, column = rank // 2, rank % 2
    core = me % 2
    ids = jnp.stack([me, rank]).astype(jnp.int32)

    def to_seq(v, k):
        return lax.ppermute(v, "seq", [(n, n ^ k) for n in range(parts)])

    def to_column(v):
        return lax.ppermute(v, "fsdp", [(n, n ^ 1) for n in range(shards)])

    def round_ring(v):
        return lax.ppermute(v, "fsdp", [(n, (n + 2) % shards) for n in range(shards)])

    def gate(*values):
        return lax.optimization_barrier(values)

    def after(v, *others):
        return lax.optimization_barrier((v,) + others)[0]

    def index(v, at, axis=0):
        return lax.dynamic_index_in_dim(v, at, axis, keepdims=False)

    def share_seq(v):
        two = to_seq(v, 2)
        return [v, to_seq(v, 1), two, to_seq(two, 1)]

    order = jnp.arange(shards, dtype=jnp.int32)
    spot = 2 * ((ring_at - order // 2) % ring_len) + (order % 2 ^ column)

    wide = 4 * d
    masters = (
        norm1_gain,
        norm1_bias,
        bias_q,
        bias_v,
        bias_proj,
        norm2_gain,
        norm2_bias,
    )
    few = jnp.concatenate([jnp.stack(masters), bias_expert_out, w_router.T], axis=0)
    few = jnp.pad(few, ((0, 16 - few.shape[0]), (0, 128 - share))).astype(BF)
    few_row = jnp.concatenate([few[:8], few[8:]], axis=1)
    few_row = jnp.pad(few_row, ((0, 0), (0, wide - 256)))
    both = jnp.concatenate([w_qkv, w_proj], axis=1)

    def half_rows(which):
        part = lax.dynamic_slice_in_dim(both, which * half, half, 0).astype(BF)
        return jnp.concatenate([part, few_row], axis=0)

    now, now_core = half_rows(core), half_rows(1 - core)
    tokens, routes, out_grad = lax.optimization_barrier((tokens, routes, out_grad, now))[:3]

    grow = ((0, 0), (0, pad - block_len), (0, 0))
    padded = jnp.pad(tokens, grow)
    pieces = [lax.dynamic_slice_in_dim(padded, (me ^ j) * own, own, 0) for j in range(parts)]
    toks = [pieces[j] if j == 0 else to_seq(pieces[j], j) for j in range(parts)]

    spare = jnp.zeros((15, d), F32)
    def build_pack():
      return jnp.concatenate(
        [
            w_hidden[0],
            w_expert_out[0],
            jnp.pad(bias_hidden, ((0, 0), (0, d - fs))),
            spare,
        ],
        axis=0,
    ).astype(BF)
    own_live = lax.dynamic_slice_in_dim(key_mask, me * block_len, block_len, 1)

    def build_final():
        return jnp.pad(out_grad * own_live[:, :, None].astype(BF), grow)


    flat = jnp.pad(
        routes.reshape(images, block_len * TOP), ((0, 0), (0, (-block_len * TOP) % 128))
    )
    blocks = jnp.stack(share_seq(flat))[:, :, : block_len * TOP]
    blocks = blocks.reshape(parts, images, block_len, TOP)
    names = me ^ jnp.arange(parts, dtype=jnp.int32)
    hit = jnp.any(blocks[..., None] == names, axis=3)
    ahead = (
        lax.broadcasted_iota(jnp.int32, (block_len, block_len), 0)
        < lax.broadcasted_iota(jnp.int32, (block_len, block_len), 1)
    ).astype(BF)
    ranks = jnp.einsum(
        "jitk,tu->jiuk", hit.astype(BF), ahead, preferred_element_type=F32
    ).astype(jnp.int32)
    in_image = jnp.where(hit, ranks + (names * CAP)[:, None, None, None], -1)
    in_image = jnp.pad(
        in_image, ((0, 0), (0, 0), (0, pad - block_len), (0, 0)), constant_values=-1
    )
    own_meta = lax.dynamic_slice_in_dim(in_image, me * own, own, 1)
    own_meta = own_meta.transpose(1, 0, 2, 3).reshape(own, length, parts)
    expert_slot = in_image[..., 0]

    def by_image(order):
        out = jnp.concatenate([expert_slot[j] for j in order], axis=-1)
        return out.reshape(images, 1, length)

    slot_rows = [by_image([j ^ k for j in range(parts)]) for k in range(parts)]
    within = (jnp.arange(images, dtype=jnp.int32) % TILE) * CAP
    mix_slot = jnp.where(hit[0], ranks[0] + within[:, None, None], -1)
    mix_meta = jnp.concatenate([mix_slot, own_live[:, :, None]], axis=-1)
    mix_meta = jnp.pad(
        mix_meta, ((0, 0), (0, pad - block_len), (0, 8 - parts - 1)), constant_values=-1
    )
    seen = lax.dynamic_slice_in_dim(key_mask, me * own, own, 0).reshape(own, parts, block_len)
    seen = jnp.stack([index(seen, me ^ j, 1) for j in range(parts)], axis=1)
    seen = jnp.pad(seen, ((0, 0), (0, 0), (0, pad - block_len))).reshape(own, 1, length)
    mask_bias = jnp.where(seen > 0, 0.0, NEG).astype(F32)

    at = lax.broadcasted_iota(jnp.int32, (rows, rows), 0)
    image_at, rank_at = (at % (TILE * CAP)) // CAP, at % CAP
    source = image_at * slots + ((at // (TILE * CAP)) ^ me) * CAP + rank_at
    reorder = (lax.broadcasted_iota(jnp.int32, (rows, rows), 1) == source).astype(BF)

    halves, others = [], []
    for r in range(ring_len):
        if r:
            if r == 2:
                now, w_hidden, w_expert_out, out_grad, others[0] = gate(
                    now, w_hidden, w_expert_out, out_grad, others[0], *pieces
                )[:5]
                pack, final = build_pack(), build_final()
            elif r == 3:
                now, others[1], pack, final, *toks[1:] = gate(
                    now, others[1], pack, final, *toks[1:]
                )
            elif r > 3:
                now, others[r - 2] = gate(now, others[r - 2])
            now = round_ring(now)
            arrived = now
            if r == ring_len - 1:
                grads_in = [final, None, to_seq(final, 2), None]
                now, mask_bias, own_meta, mix_meta, reorder, *slot_rows = gate(
                    now, mask_bias, own_meta, mix_meta, reorder, *slot_rows
                )
            now_core = to_seq(now, 1)
        others.append(to_column(now))
        halves.append((now, now_core))
    halves = [
        part for pair, other in zip(halves, others) for part in (*pair, other, to_seq(other, 1))
    ]
    if half % 16 == 0:
        weights, vec, router = pl.pallas_call(
            functools.partial(assemble_kernel, ring_len, half, share),
            grid_spec=pltpu.PrefetchScalarGridSpec(
                num_scalar_prefetch=1,
                grid=(1,),
                in_specs=[whole((half + 8, wide))] * len(halves),
                out_specs=[whole((d, wide)), whole((16, d)), whole((d, 128))],
            ),
            out_shape=[
                jax.ShapeDtypeStruct((d, wide), BF),
                jax.ShapeDtypeStruct((16, d), F32),
                jax.ShapeDtypeStruct((d, 128), BF),
            ],
            compiler_params=params(),
            cost_estimate=cost(0.01),
            name="assemble",
        )(ids, *halves)
    else:
        place = jnp.arange(shards * 2, dtype=jnp.int32)
        place = spot[place // 2] * 2 + (place % 2 ^ core)
        weights = jnp.stack([part[:half] for part in halves])[place].reshape(d, wide)
        vec = jnp.stack([part[half:, :256] for part in halves[::2]])[spot]
        vec = vec.reshape(shards, 8, 2, 128)[..., :share].transpose(2, 1, 0, 3)
        vec = vec.reshape(16, d).astype(F32)
        router = jnp.pad(vec[8:16].T, ((0, 0), (0, 120))).astype(BF)

    pack = after(pack, arrived, *others)
    chunks = [(pack, to_column(pack)), (round_ring(pack),)]

    per_image = lambda *tail: pl.BlockSpec((1,) + tail, lambda i: (i,) + (0,) * len(tail))
    made = pl.pallas_call(
        functools.partial(fwd_kernel, parts),
        grid=(own,),
        in_specs=[per_image(pad, d)] * parts
        + [per_image(1, length), whole((d, wide)), whole((16, d))],
        out_specs=[
            per_image(length, 3 * d),
            per_image(length, d),
            per_image(length, 128),
            per_image(length, d),
            per_image(length, d),
            per_image(length, d),
        ]
        + [per_image(pad, d)] * parts,
        out_shape=[
            jax.ShapeDtypeStruct((own, length, 3 * d), BF),
            jax.ShapeDtypeStruct((own, length, d), BF),
            jax.ShapeDtypeStruct((own, length, 128), F32),
            jax.ShapeDtypeStruct((own, length, d), F32),
            jax.ShapeDtypeStruct((own, length, d), BF),
            jax.ShapeDtypeStruct((own, length, d), BF),
        ]
        + [jax.ShapeDtypeStruct((own, pad, d), BF)] * parts,
        compiler_params=params(),
        cost_estimate=cost(0.01),
        name="block_forward",
    )(*toks, mask_bias, weights, vec)
    *made, first_other, second, grads_in[2] = gate(*made, chunks[0][1], chunks[1][0], grads_in[2])
    chunks = [(chunks[0][0], first_other), (second, to_column(second))]
    qkv, attended, lse, residual, z_own, normed = made[:6]
    res_pieces = list(made[6:])

    grads_in[1], grads_in[3] = to_seq(final, 1), to_seq(grads_in[2], 1)

    def tile_spec(shape, index_map):
        return pl.BlockSpec(shape, index_map)

    grad_slots = pl.pallas_call(
        functools.partial(gather_grads_kernel, slots, parts),
        grid_spec=pltpu.PrefetchScalarGridSpec(
            num_scalar_prefetch=1,
            grid=(parts, sub),
            in_specs=[
                tile_spec((TILE, 1, length), lambda k, u, ids: ((ids[0] ^ k) * sub + u, 0, 0))
            ]
            + [tile_spec((TILE, pad, d), lambda k, u, ids: ((ids[0] ^ k) * sub + u, 0, 0))]
            * parts,
            out_specs=tile_spec((1, rows, d), lambda k, u, ids: (k * sub + u, 0, 0)),
        ),
        out_shape=jax.ShapeDtypeStruct((tiles, rows, d), BF),
        compiler_params=params(),
        cost_estimate=cost(0.01),
        name="grad_slots",
    )(ids, slot_rows[0], *grads_in)

    def add(*terms):
        return sum(term.astype(F32) for term in terms)

    def ring_sum(moving, r):
        terms = (packs[r][0], crossed[r]) + (() if moving is None else (moving,))
        return add(*terms)

    z_far = to_seq(z_own, 2)
    z_rows = [z_own, to_seq(z_own, 1), z_far, None]
    if ring_len > 2:
        chunks.append((round_ring(second),))
    x_rows = gr_rows = None
    for k in range(parts):
        chain = () if k == 0 else (x_rows, gr_rows)
        if k == 2:
            z_far, x_rows, gr_rows, second_other, *rest = gate(
                z_far, x_rows, gr_rows, chunks[1][1], *[c[0] for c in chunks[2:]]
            )
            chunks[1] = (chunks[1][0], second_other)
            for r in range(2, ring_len):
                part = rest[0] if r == 2 else round_ring(part)
                chunks[r:] = [(part, to_column(part) if r < ring_len - 1 else part)]
            z_rows[2:] = [z_far, to_seq(z_far, 1)]
            chain = (x_rows, gr_rows)
        x_rows, gr_rows = pl.pallas_call(
            functools.partial(gather_rows_kernel, slots, experts),
            grid_spec=pltpu.PrefetchScalarGridSpec(
                num_scalar_prefetch=1,
                grid=(sub,),
                in_specs=[
                    tile_spec(
                        (TILE, 1, length), lambda u, ids, k=k: ((ids[0] ^ k) * sub + u, 0, 0)
                    ),
                    tile_spec((TILE, length, d), lambda u, ids: (u, 0, 0)),
                    tile_spec((1, rows, d), lambda u, ids, k=k: (k * sub + u, 0, 0)),
                    whole((d, 128)),
                ]
                + [pl.BlockSpec(memory_space=pl.ANY)] * len(chain),
                out_specs=[
                    tile_spec((1, rows, d), lambda u, ids, k=k: (k * sub + u, 0, 0)),
                    tile_spec((1, rows, d), lambda u, ids, k=k: (k * sub + u, 0, 0)),
                ],
            ),
            out_shape=[jax.ShapeDtypeStruct((tiles, rows, d), BF)] * 2,
            input_output_aliases={5: 0, 6: 1} if chain else {},
            compiler_params=params(),
            cost_estimate=cost(0.01),
            name="slot_rows",
        )(ids, slot_rows[k], z_rows[k], grad_slots, router, *chain)

    tile3 = pl.BlockSpec((1, rows, d), lambda t, *_: (t, 0, 0))
    pack_rows = 2 * fs + 16
    acc_out = acc_gx = None
    packs = []
    crossed = {}
    moving = None
    for r in range(ring_len):
        e0, e1 = chunks[r]
        is_first, is_last = r == 0, r == ring_len - 1
        operands = [e0, e1, x_rows, gr_rows]
        in_specs = [
            whole((pack_rows, d)),
            whole((pack_rows, d)),
            tile3,
            tile3,
        ]
        aliases = {}
        if not is_first:
            operands += [acc_out, acc_gx]
            in_specs += [tile3, tile3]
            aliases = {4: 2} if is_last else {4: 2, 5: 3}
        pack_shape = jax.ShapeDtypeStruct((pack_rows, d), BF)
        out_specs = [whole((pack_rows, d)), whole((pack_rows, d)), tile3, tile3]
        acc_shape = jax.ShapeDtypeStruct((tiles, rows, d), F32)
        out_shape = [pack_shape, pack_shape, acc_shape, acc_shape]
        if is_last:
            operands += [grad_slots, vec]
            in_specs += [tile3, whole((16, d))]
            out_specs[3:] = [
                pl.BlockSpec(
                    (TILE, slots + 8, d), lambda t, k=k: (jnp.clip(t - k * sub, 0, sub - 1), 0, 0)
                )
                for k in range(parts)
            ]
            out_shape[3:] = [jax.ShapeDtypeStruct((own, slots + 8, d), BF)] * parts
        made = pl.pallas_call(
            functools.partial(expert_kernel, is_first, is_last, slots, experts, fs),
            grid_spec=pltpu.PrefetchScalarGridSpec(
                num_scalar_prefetch=0,
                grid=(tiles,),
                in_specs=in_specs,
                out_specs=out_specs,
                scratch_shapes=[
                    pltpu.VMEM((2 * fs, d), BF),
                    pltpu.VMEM((2 * fs, d), BF),
                    pltpu.VMEM((2 * fs, d), F32),
                    pltpu.VMEM((2 * fs, d), F32),
                    pltpu.VMEM((8, 2 * fs), F32),
                    pltpu.VMEM((8, d), F32),
                    pltpu.VMEM((8, 2 * fs), F32),
                ],
            ),
            out_shape=out_shape,
            input_output_aliases=aliases,
            compiler_params=params(),
            cost_estimate=cost(50),
            name="expert_pair",
        )(*operands)
        ready = {}
        if r == 0:
            ready = {("in", q, p): chunks[q][p] for q in range(2, ring_len) for p in (0, 1)}
            ready.pop(("in", ring_len - 1, 1), None)
        elif r == 1:
            ready[("in", ring_len - 1, 1)] = chunks[ring_len - 1][1]
            ready.update({("piece", j): res_pieces[j] for j in range(1, parts)})
        else:
            ready[("out", r - 1, 1)] = crossed[r - 1]
            if moving is not None:
                ready["moving"] = moving
            if r == 2:
                ready.update({("res", j): res_in[j] for j in range(1, parts)})
        values = gate(*made, *ready.values())
        made, ready = values[: len(made)], dict(zip(ready, values[len(made) :]))
        for key, value in ready.items():
            if key == "moving":
                moving = value
            elif key[0] == "in":
                chunks[key[1]] = tuple(value if p == key[2] else chunks[key[1]][p] for p in (0, 1))
            elif key[0] == "out":
                crossed[key[1]] = value
            elif key[0] == "piece":
                res_pieces[key[1]] = value
            else:
                res_in[key[1]] = value
        packs.append(made[:2])
        acc_out, acc_gx = made[2:4]
        if r == 0 and ring_len > 2:
            chunks[ring_len - 1] = (chunks[ring_len - 1][0], to_column(chunks[ring_len - 1][0]))
        if r >= 1:
            crossed[r] = to_column(packs[r][1])
        if 2 <= r < ring_len - 1:
            moving = round_ring(ring_sum(moving, r - 1).astype(BF))
        if r == 1:
            res_in = [res_pieces[0]] + [to_seq(res_pieces[j], j) for j in range(1, parts)]
    gx = made[3 : 3 + parts]

    gx_in = [gx[k] if k == 0 else to_seq(gx[k], k) for k in range(parts)]
    packs[ring_len - 2] = (after(packs[ring_len - 2][0], gx_in[1]), None)
    moving = round_ring(ring_sum(moving, ring_len - 2).astype(BF))
    mixed = pl.pallas_call(
        functools.partial(weigh_kernel, slots, experts),
        grid_spec=pltpu.PrefetchScalarGridSpec(
            num_scalar_prefetch=1,
            grid=(tiles,),
            in_specs=[
                tile3,
                tile3,
                whole((d, 128)),
                whole((16, d)),
                whole((rows, rows)),
            ],
            out_specs=[
                *[pl.BlockSpec((1, TILE * CAP, d), lambda t, *_: (t, 0, 0))] * parts,
            ],
        ),
        out_shape=[
            *[jax.ShapeDtypeStruct((tiles, TILE * CAP, d), BF)] * parts,
        ],
        compiler_params=params(),
        cost_estimate=cost(50),
        name="weigh",
    )(ids, acc_out, x_rows, router, vec, reorder)
    last = ring_len - 1
    own_meta, moving, crossed[last], *rest = gate(
        own_meta, moving, crossed[last], *gx_in[1:], *mixed
    )
    gx_in[1:], mixed = rest[: parts - 1], rest[parts - 1 :]
    mixed_in = [mixed[0]] + [to_seq(mixed[k], k) for k in range(1, parts)]
    moving = round_ring(ring_sum(moving, last).astype(BF))
    crossed[0] = to_column(after(packs[0][1], own_meta))

    side = me // 2
    quarter = share // 4

    def shift_ring(v, k):
        return lax.ppermute(v, "fsdp", [(n, (n + 2 * k) % shards) for n in range(shards)])

    def core_pair(made):
        if len(made) == 1:
            split = made[0].reshape(shards, 2, 2, quarter, made[0].shape[-1])
            made = index(split, core, 2), index(split, 1 - core, 2)
        return made[0], to_seq(made[1], 1)

    def over_y(keep, come=None):
        pair = [v for v in (keep, come) if v is not None]
        send = add(*[index(v, 1 - side, 1) for v in pair]).astype(BF)
        return add(*[index(v, side, 1) for v in pair], to_seq(send, 2)).astype(BF)

    def over_x(keep, come=None):
        pair = [v.reshape(ring_len, 2, *v.shape[1:]) for v in (keep, come) if v is not None]
        send = add(*[index(v, 1 - column, 1) for v in pair]).astype(BF)
        return add(*[index(v, column, 1) for v in pair], to_column(send)).astype(BF)

    def over_ring(v):
        far = [
            shift_ring(index(v, (ring_at + k) % ring_len), k) for k in range(1, ring_len)
        ]
        return add(index(v, ring_at), *far).astype(BF)

    def in_order(pieces):
        a, b, c, e = pieces
        near = [jnp.where(core == 0, a, b), jnp.where(core == 0, b, a)]
        far = [jnp.where(core == 0, c, e), jnp.where(core == 0, e, c)]
        front = [jnp.where(side == 0, u, v) for u, v in zip(near, far)]
        back = [jnp.where(side == 0, v, u) for u, v in zip(near, far)]
        return jnp.concatenate(front + back, axis=0)

    def spread_rows(v):
        return in_order([v] + [to_seq(v, k) for k in range(1, parts)]).astype(F32)

    image3 = lambda *tail: pl.BlockSpec((1,) + tail, lambda i, *_: (i,) + (0,) * len(tail))
    width = d // 2
    column3 = lambda n: pl.BlockSpec((1, length, width), lambda i, *_: (i, 0, n))
    weight3 = lambda n: pl.BlockSpec((d, width), lambda i, *_: (0, n))
    partial_shape = jax.ShapeDtypeStruct((own, length, d), F32)
    def grad_outs(cols):
        if quarter % 8:
            return [whole((d, cols))], [jax.ShapeDtypeStruct((d, cols), BF)]
        shape = (shards, 2, quarter, cols)
        return [whole(shape)] * 2, [jax.ShapeDtypeStruct(shape, BF)] * 2

    grad_specs, grad_shapes = grad_outs(d + 3 * width)
    grad_att, grad_res, after_first, small, *first = pl.pallas_call(
        functools.partial(back_first_kernel, parts, experts, slots, len(grad_specs)),
        grid_spec=pltpu.PrefetchScalarGridSpec(
            num_scalar_prefetch=1,
            grid=(own,),
            in_specs=[image3(length, parts)]
            + [image3(slots + 8, d)] * parts
            + [pl.BlockSpec((1, pad, d), lambda i, ids: (ids[0] * own + i, 0, 0))] * parts
            + [
                image3(length, d),
                image3(length, d),
                image3(length, d),
                pl.BlockSpec((d, d), lambda i, ids: (0, 3)),
                whole((16, d)),
                whole((d, 128)),
                image3(1, length),
                column3(0),
                column3(2),
                column3(4),
                image3(length, 128),
                image3(length, d),
                weight3(0),
                weight3(2),
                weight3(4),
            ],
            out_specs=[
                image3(length, d),
                image3(length, d),
                image3(length, d),
                whole((16, d)),
                *grad_specs,
            ],
            scratch_shapes=[
                pltpu.VMEM((d, d), F32),
                pltpu.VMEM((d, 3 * width), F32),
                pltpu.VMEM((16, d), F32),
                pltpu.VMEM((d, 128), F32),
                pltpu.VMEM((length, 3 * width), BF),
            ],
        ),
        out_shape=[
            jax.ShapeDtypeStruct((own, length, d), BF),
            partial_shape,
            partial_shape,
            jax.ShapeDtypeStruct((16, d), F32),
            *grad_shapes,
        ],
        compiler_params=params(),
        cost_estimate=cost(50),
        name="back_first",
    )(
        ids,
        own_meta,
        *gx_in,
        *grads_in,
        attended,
        residual,
        z_own,
        weights,
        vec,
        router,
        mask_bias,
        qkv,
        qkv,
        qkv,
        lse,
        normed,
        weights,
        weights,
        weights,
    )
    grad_att, grad_res, after_first, small, moving, crossed[0], *rest = gate(
        grad_att, grad_res, after_first, small, moving, crossed[0], *mixed_in[1:], *first
    )
    mixed_in[1:], first = rest[: parts - 1], rest[parts - 1 :]
    first = core_pair(first)
    grad_specs, grad_shapes = grad_outs(3 * width + 128)
    made = pl.pallas_call(
        functools.partial(back_second_kernel, parts, len(grad_specs)),
        grid_spec=pltpu.PrefetchScalarGridSpec(
        num_scalar_prefetch=1,
        grid=(own,),
        in_specs=[
            image3(1, length),
            column3(1),
            column3(3),
            column3(5),
            image3(length, d),
            image3(length, d),
            image3(length, 128),
            image3(length, d),
            weight3(1),
            weight3(3),
            weight3(5),
            whole((16, d)),
            image3(length, d),
            image3(length, d),
            whole((16, d)),
        ]
        + [image3(pad, d)] * parts,
        out_specs=[image3(pad, d)] * parts + grad_specs,
        scratch_shapes=[
            pltpu.VMEM((d, 3 * width), F32),
            pltpu.VMEM((128, d), F32),
            pltpu.VMEM((d, 128), F32),
            pltpu.VMEM((length, 3 * width), BF),
        ],
        ),
        out_shape=[jax.ShapeDtypeStruct((own, pad, d), BF)] * parts + grad_shapes,
        compiler_params=params(),
        cost_estimate=cost(50),
        name="back_second",
    )(
        ids,
        mask_bias,
        qkv,
        qkv,
        qkv,
        attended,
        grad_att,
        lse,
        normed,
        weights,
        weights,
        weights,
        small,
        after_first,
        grad_res,
        vec,
        *toks,
    )
    token_pieces, second = made[:parts], made[parts:]
    far_first, moving, crossed[0], *rest = gate(
        first[1], moving, crossed[0], *token_pieces, *mixed_in[1:], *second
    )
    first = (first[0], far_first)
    token_pieces, mixed_in[1:], second = (
        rest[:parts],
        rest[parts : 2 * parts - 1],
        rest[2 * parts - 1 :],
    )

    image_block = pl.BlockSpec(
        (TILE, block_len, d), lambda j, u, ids: ((ids[0] ^ j) * sub + u, 0, 0)
    )
    output = pl.pallas_call(
        functools.partial(combine_kernel, parts),
        grid_spec=pltpu.PrefetchScalarGridSpec(
            num_scalar_prefetch=1,
            grid=(parts, sub),
            in_specs=[
                pl.BlockSpec((TILE, pad, 8), lambda j, u, ids: ((ids[0] ^ j) * sub + u, 0, 0))
            ]
            + [pl.BlockSpec((TILE, pad, d), lambda j, u, ids: (u, 0, 0))] * parts
            + [
                pl.BlockSpec(
                    (1, TILE * CAP, d), lambda j, u, ids, k=k: ((j ^ k) * sub + u, 0, 0)
                )
                for k in range(parts)
            ],
            out_specs=image_block,
        ),
        out_shape=jax.ShapeDtypeStruct((images, block_len, d), BF),
        compiler_params=params(),
        cost_estimate=cost(50),
        name="combine",
    )(ids, mix_meta, *res_in, *mixed_in)

    first_x = over_x(*first)
    second = core_pair(second)
    second_y = over_y(*second)
    tokens_in = [token_pieces[j] if j == 0 else to_seq(token_pieces[j], j) for j in range(parts)]
    first_x, second_y, output, *tokens_in = gate(first_x, second_y, output, *tokens_in)
    first_own, second_x = over_y(first_x), over_x(second_y)
    grad_tokens = in_order(tokens_in)[:, :block_len]
    first_own, second_x, grad_tokens = gate(first_own, second_x, grad_tokens)
    both_x = jnp.concatenate([first_own, second_x], axis=-1)
    total = ring_sum(moving, 0)
    grad_hidden = total[None, :fs]
    grad_expert_out = total[None, fs : 2 * fs]
    grad_hidden_bias = total[2 * fs : 2 * fs + 1, :fs]
    grad_out_bias = lax.dynamic_slice(total, (2 * fs + 1, rank * share), (1, share))
    own_rows = over_ring(both_x)
    mine = spread_rows(own_rows)
    grad_proj = mine[:, :d]
    at_b, at_small = d + 3 * width, d + 6 * width
    grad_qkv = jnp.concatenate(
        [
            mine[:, start + n * width : start + (n + 1) * width]
            for n in range(3)
            for start in (d, at_b)
        ],
        axis=1,
    )
    small = mine[:, at_small : at_small + 16].T
    grad_router = mine[:, at_small + 8 : at_small + 8 + experts]

    return (
        output,
        grad_tokens,
        small[0],
        small[1],
        grad_qkv,
        small[2],
        small[3],
        grad_proj,
        small[4],
        small[5],
        small[6],
        grad_router,
        grad_hidden,
        grad_hidden_bias,
        grad_expert_out,
        grad_out_bias,
    )


def solution(mesh):
    in_specs = (
        P("fsdp", "seq", None),
        P("fsdp", None),
        P("fsdp", "seq", None),
        P("fsdp", "seq", None),
        P("fsdp"),
        P("fsdp"),
        P("fsdp", None),
        P("fsdp"),
        P("fsdp"),
        P("fsdp", None),
        P("fsdp"),
        P("fsdp"),
        P("fsdp"),
        P("fsdp", None),
        P("seq", "fsdp", None),
        P("seq", "fsdp"),
        P("seq", "fsdp", None),
        P("seq", "fsdp"),
    )
    out_specs = (
        P("fsdp", "seq", None),
        P("fsdp", "seq", None),
        P("fsdp"),
        P("fsdp"),
        P("fsdp", None),
        P("fsdp"),
        P("fsdp"),
        P("fsdp", None),
        P("fsdp"),
        P("fsdp"),
        P("fsdp"),
        P("fsdp", None),
        P("seq", "fsdp", None),
        P("seq", "fsdp"),
        P("seq", "fsdp", None),
        P("seq", "fsdp"),
    )
    return jax.shard_map(body, mesh=mesh, in_specs=in_specs, out_specs=out_specs, check_vma=False)
```

```python
import functools

import jax
import jax.numpy as jnp
from jax import lax
from jax.experimental import pallas as pl
from jax.experimental.pallas import tpu as pltpu
from jax.sharding import PartitionSpec as P

HEAD_DIM = 64
TOP = 2
CAP = 30
TILE = 4
EPS = 1e-06
NEG = -1e30
BF = jnp.bfloat16
F32 = jnp.float32
VMEM = 66_500_000


def nn(a, b):
    return jnp.dot(a, b, preferred_element_type=F32)


def nt(a, b):
    return lax.dot_general(a, b, (((1,), (1,)), ((), ())), preferred_element_type=F32)


def tn(a, b):
    return lax.dot_general(a, b, (((0,), (0,)), ((), ())), preferred_element_type=F32)


def stats(v):
    center = v - jnp.mean(v, axis=-1, keepdims=True)
    r = lax.rsqrt(jnp.mean(center * center, axis=-1, keepdims=True) + EPS)
    return center * r, r


def norm_back(u, gain, vhat, r):
    ug = u * gain
    return r * (
        ug
        - jnp.mean(ug, axis=-1, keepdims=True)
        - vhat * jnp.mean(ug * vhat, axis=-1, keepdims=True)
    )


def rows_of(refs, i=0):
    return jnp.concatenate([ref[i].astype(F32) for ref in refs], axis=0)


def params(**kw):
    return pltpu.CompilerParams(vmem_limit_bytes=VMEM, **kw)


def cost(us):
    return pl.CostEstimate(flops=int(us * 1e9), bytes_accessed=int(us * 1e4), transcendentals=0)


def half_masks():
    lane = lax.broadcasted_iota(jnp.int32, (1, 2 * HEAD_DIM), 1)
    first = (lane < HEAD_DIM).astype(F32)
    return first, 1.0 - first


def fwd_kernel(parts, *refs):
    toks, refs = refs[:parts], refs[parts:]
    mask_ref, w_ref, vec_ref, qkv_ref, att_ref, lse_ref, res_ref, z_ref, normed_ref = refs[:9]
    sends = refs[9:]
    x = rows_of(toks)
    d = x.shape[1]
    vec = vec_ref[...]
    vhat, _ = stats(x)
    normed = (vhat * vec[0:1] + vec[1:2]).astype(BF)
    normed_ref[0] = normed
    qkv_ref[0, :, 0:d] = (nn(normed, w_ref[:, 0:d]) + vec[2:3]).astype(BF)
    qkv_ref[0, :, d : 2 * d] = nn(normed, w_ref[:, d : 2 * d]).astype(BF)
    qkv_ref[0, :, 2 * d : 3 * d] = (nn(normed, w_ref[:, 2 * d : 3 * d]) + vec[3:4]).astype(BF)
    bias = mask_ref[0]
    first, second = half_masks()
    scale = HEAD_DIM ** (-0.5)
    lane = lax.broadcasted_iota(jnp.int32, (x.shape[0], 128), 1)
    lse = jnp.zeros((x.shape[0], 128), F32)
    for pair in range(d // 128):
        q2 = qkv_ref[0, :, 128 * pair : 128 * pair + 128]
        k2 = qkv_ref[0, :, d + 128 * pair : d + 128 * pair + 128]
        v2 = qkv_ref[0, :, 2 * d + 128 * pair : 2 * d + 128 * pair + 128]
        outs = []
        for a, half in enumerate((first, second)):
            qa = q2 * (half * scale).astype(BF)
            s = nt(qa, k2) + bias
            top = jnp.max(s, axis=-1, keepdims=True)
            e = jnp.exp(s - top)
            total = jnp.sum(e, axis=-1, keepdims=True)
            outs.append(nn(e.astype(BF), v2) * (1.0 / total))
            lse = jnp.where(lane == 2 * pair + a, top + jnp.log(total), lse)
        att = jnp.where(first > 0, outs[0], outs[1])
        att_ref[0, :, 128 * pair : 128 * pair + 128] = att.astype(BF)
    lse_ref[0] = lse
    res = x + nn(att_ref[0], w_ref[:, 3 * d : 4 * d]) + vec[4:5]
    res_ref[0] = res
    zhat, _ = stats(res)
    z_ref[0] = (zhat * vec[5:6] + vec[6:7]).astype(BF)
    block = x.shape[0] // parts
    for j, ref in enumerate(sends):
        ref[0] = res[j * block : (j + 1) * block].astype(BF)


def spread(row, slots, values):
    length = values.shape[0]
    hot = (lax.broadcasted_iota(jnp.int32, (slots, length), 0) == row).astype(BF)
    return nn(hot, values)


def gather_grads_kernel(slots, parts, ids_ref, slot_ref, *refs):
    out = []
    for i in range(TILE):
        values = rows_of(refs[:parts], i).astype(BF)
        out.append(spread(slot_ref[i], slots, values))
    refs[parts][0] = jnp.concatenate(out, axis=0).astype(BF)


def router_probs(rows, router, experts):
    logits = nn(rows, router)
    lane = lax.broadcasted_iota(jnp.int32, logits.shape, 1)
    logits = jnp.where(lane < experts, logits, NEG)
    e = jnp.exp(logits - jnp.max(logits, axis=-1, keepdims=True))
    return e / jnp.sum(e, axis=-1, keepdims=True), lane


def gather_rows_kernel(slots, experts, ids_ref, slot_ref, z_ref, g_ref, router_ref, *refs):
    x_ref, gr_ref = refs[-2:]
    out = [spread(slot_ref[i], slots, z_ref[i]) for i in range(TILE)]
    x = jnp.concatenate(out, axis=0).astype(BF)
    probs, lane = router_probs(x, router_ref[...], experts)
    gate = jnp.sum(jnp.where(lane == ids_ref[0], probs, 0.0), axis=-1, keepdims=True)
    x_ref[0] = x
    gr_ref[0] = (gate * g_ref[0].astype(F32)).astype(BF)


def gelu_parts(v):
    e = jnp.exp(-0.5 * v * v)
    den = 1.0 + 0.23164189 * jnp.abs(v)
    t = pl.reciprocal(den, approx=True)
    t = t * (2.0 - den * t)
    poly = t * (
        0.127414796 + t * (-0.142248368 + t * (0.7107068705 + t * (-0.7265760135 + t * 0.5307027145)))
    )
    tail = poly * e
    cdf = jnp.where(v >= 0, 1.0 - tail, tail)
    return v * cdf, cdf + v * (0.3989422804 * e)


def expert_kernel(first, last, slots, experts, fs, *refs):
    e0, e1, x_ref, gr_ref = refs[:4]
    refs = list(refs[4:])
    if not first:
        acc_out_in, acc_gx_in = refs[:2]
        refs = refs[2:]
    if last:
        g_ref, bo_ref, refs = refs[0], refs[1], refs[2:]
    p0, p1, acc_out = refs[:3]
    gx_refs, refs = refs[3:-7], refs[-7:]
    wh, wo, gwh, gwo, gbh, gbo, bias = refs
    step = pl.program_id(0)

    @pl.when(step == 0)
    def _():
        wh[0:fs] = e0[0:fs]
        wh[fs : 2 * fs] = e1[0:fs]
        wo[0:fs] = e0[fs : 2 * fs]
        wo[fs : 2 * fs] = e1[fs : 2 * fs]
        both = [e[2 * fs : 2 * fs + 16, 0:fs].astype(F32)[0:8] for e in (e0, e1)]
        bias[...] = jnp.concatenate(both, axis=1)
        gwh[...] = jnp.zeros_like(gwh)
        gwo[...] = jnp.zeros_like(gwo)
        gbh[...] = jnp.zeros_like(gbh)
        gbo[...] = jnp.zeros_like(gbo)

    x = x_ref[0]
    gr = gr_ref[0]
    pre = nt(x, wh[...]) + bias[0:1]
    act, slope = gelu_parts(pre)
    hidden = act.astype(BF)
    out = nn(hidden, wo[...])
    grad_pre_f = nt(gr, wo[...]) * slope
    grad_pre = grad_pre_f.astype(BF)
    gx = nn(grad_pre, wh[...])
    gwh[...] += tn(grad_pre, x)
    gwo[...] += tn(hidden, gr)
    gbh[0:1] += jnp.sum(grad_pre_f, axis=0, keepdims=True)
    gbo[0:1] += jnp.sum(gr.astype(F32), axis=0, keepdims=True)
    if not first:
        out = out + acc_out_in[0]
        gx = gx + acc_gx_in[0]
    acc_out[0] = out
    if last:
        dots = jnp.sum((out + bo_ref[7:8]) * g_ref[0].astype(F32), axis=-1, keepdims=True)
        sub = lax.broadcasted_iota(jnp.int32, (8, x.shape[1]), 0)
        fill = jnp.zeros((128 - slots, 128), F32)
        wide_fill = jnp.zeros((8, x.shape[1] - 128), F32)
        out_rows = []
        for i in range(TILE):
            col = jnp.broadcast_to(dots[i * slots : (i + 1) * slots], (slots, 128))
            row = jnp.concatenate([col, fill], axis=0).T[0:8]
            row = jnp.concatenate([row, wide_fill], axis=1)
            high = row.astype(BF).astype(F32)
            row = jnp.where(sub == 0, high, jnp.where(sub == 1, row - high, 0.0))
            out_rows += [gx[i * slots : (i + 1) * slots], row]
        gx = jnp.concatenate(out_rows, axis=0).reshape(TILE, slots + 8, -1).astype(BF)
        for k, ref in enumerate(gx_refs):

            @pl.when(step // (pl.num_programs(0) // len(gx_refs)) == k)
            def _(ref=ref):
                ref[...] = gx
    else:
        gx_refs[0][0] = gx

    @pl.when(step == pl.num_programs(0) - 1)
    def _():
        d = gwh.shape[1]
        for i, pack in enumerate((p0, p1)):
            pack[0:fs] = gwh[i * fs : (i + 1) * fs].astype(BF)
            pack[fs : 2 * fs] = gwo[i * fs : (i + 1) * fs].astype(BF)
            row = jnp.broadcast_to(gbh[0:1, i * fs : (i + 1) * fs], (16, fs))
            row = jnp.concatenate([row, jnp.zeros((16, d - fs), F32)], axis=1)
            sub = lax.broadcasted_iota(jnp.int32, (16, d), 0)
            pack[2 * fs : 2 * fs + 16] = jnp.where(
                sub == 0, row, jnp.where(sub == 1, gbo[0:1], 0.0)
            ).astype(BF)


def weigh_kernel(slots, experts, ids_ref, out_ref, x_ref, router_ref, bo_ref, perm_ref, *mixed_refs):
    x = x_ref[0]
    out = out_ref[0] + bo_ref[7:8]
    probs, lane = router_probs(x, router_ref[...], experts)
    gate = jnp.sum(jnp.where(lane == ids_ref[0], probs, 0.0), axis=-1, keepdims=True)
    weighted = nn(perm_ref[...], (gate * out).astype(BF))
    count = weighted.shape[0] // len(mixed_refs)
    for k, ref in enumerate(mixed_refs):
        ref[0] = weighted[k * count : (k + 1) * count].astype(BF)


def combine_kernel(parts, ids_ref, meta_ref, *refs):
    res, rows, out_ref = refs[:parts], refs[parts : 2 * parts], refs[2 * parts]
    step = pl.program_id(0)
    block, length = meta_ref.shape[1], out_ref.shape[1]
    meta = meta_ref[...].reshape(TILE * block, 8)
    total = 0.0
    for k, ref in enumerate(rows):
        slot = lax.broadcasted_iota(jnp.int32, (TILE * block, ref.shape[1]), 1)
        total += nn((slot == meta[:, k : k + 1]).astype(BF), ref[0])
    live = meta[:, 4:5].astype(F32)
    for j in range(parts):

        @pl.when(step == j)
        def _(j=j):
            base = res[j][...].astype(F32).reshape(TILE * block, -1)
            out = ((base + total) * live).reshape(TILE, block, -1)
            out_ref[...] = out[:, :length].astype(BF)


def norm_part(parts, experts, slots, refs, accs, ids_ref, i):
    meta_ref, gx_refs, g_refs, att_ref, res_ref, z_ref, w_ref, vec_ref, router_ref = refs
    acc_proj, acc_small, acc_router = accs
    length, d = res_ref.shape[1:]
    meta = meta_ref[0]
    lane = lax.broadcasted_iota(jnp.int32, (length, 128), 1)
    dz = jnp.zeros((length, d), F32)
    grad_probs = jnp.zeros((length, 128), F32)
    for k in range(parts):
        hot = lane == meta[:, k : k + 1]
        dz += nn(hot.astype(BF), gx_refs[k][0])
        dots = gx_refs[k][0, slots - 8 : slots + 8, 0:128].astype(F32)
        dots = dots[8:9] + dots[9:10]
        of_token = jnp.sum(jnp.where(hot, dots, 0.0), axis=-1, keepdims=True)
        grad_probs = jnp.where(lane == (ids_ref[0] ^ k), of_token, grad_probs)
    z = z_ref[0]
    probs, _ = router_probs(z, router_ref[...], experts)
    grad_logits = probs * (grad_probs - jnp.sum(probs * grad_probs, axis=-1, keepdims=True))
    grad_logits = grad_logits.astype(BF)
    dz += nt(grad_logits, router_ref[...])
    acc_router[...] += tn(z, grad_logits)
    zhat, r2 = stats(res_ref[0])
    acc_small[5:6] += jnp.sum(dz * zhat, axis=0, keepdims=True)
    acc_small[6:7] += jnp.sum(dz, axis=0, keepdims=True)
    grad_res = rows_of(g_refs) + norm_back(dz, vec_ref[5:6], zhat, r2)
    branch = grad_res.astype(BF)
    acc_small[4:5] += jnp.sum(branch.astype(F32), axis=0, keepdims=True)
    acc_proj[...] += tn(att_ref[0], branch)
    return grad_res, nt(branch, w_ref[...]).astype(BF)


def heads_part(half, mask_ref, qkv_refs, att_ref, ga_ref, lse_ref, normed_ref, w_refs, acc, acc_small, gqkv):
    q_ref, k_ref, v_ref = qkv_refs
    width = q_ref.shape[2]
    spot = half * width
    bias = mask_ref[0]
    lse = lse_ref[0]
    first, second = half_masks()
    scale = HEAD_DIM ** (-0.5)
    for pair in range(width // 128):
        at = 128 * pair
        here = slice(spot + at, spot + at + 128)
        q2 = q_ref[0, :, at : at + 128]
        k2 = k_ref[0, :, at : at + 128]
        v2 = v_ref[0, :, at : at + 128]
        g2 = ga_ref[0, :, here]
        prod = g2.astype(F32) * att_ref[0, :, here].astype(F32)
        gq, gk, gv = [], 0.0, 0.0
        for a, mask in enumerate((first, second)):
            qa = q2 * (mask * scale).astype(BF)
            ga = g2 * mask.astype(BF)
            head = half * (width // HEAD_DIM) + 2 * pair + a
            probs = jnp.exp(nt(qa, k2) + bias - lse[:, head : head + 1])
            delta = jnp.sum(prod * mask, axis=-1, keepdims=True)
            grad_scores = (probs * (nt(ga, v2) - delta)).astype(BF)
            gq.append(nn(grad_scores, k2))
            gk += tn(grad_scores, qa)
            gv += tn(probs.astype(BF), ga)
        gqkv[:, at : at + 128] = (jnp.where(first > 0, gq[0], gq[1]) * scale).astype(BF)
        gqkv[:, width + at : width + at + 128] = gk.astype(BF)
        gqkv[:, 2 * width + at : 2 * width + at + 128] = gv.astype(BF)
    acc_small[2:3, spot : spot + width] += jnp.sum(
        gqkv[:, 0:width].astype(F32), axis=0, keepdims=True
    )
    acc_small[3:4, spot : spot + width] += jnp.sum(
        gqkv[:, 2 * width : 3 * width].astype(F32), axis=0, keepdims=True
    )
    acc[...] += tn(normed_ref[0], gqkv[...])
    return sum(
        nt(gqkv[:, n * width : (n + 1) * width], w_ref[...]) for n, w_ref in enumerate(w_refs)
    )


def split_rows(outs, accs, core):
    col = 0
    for acc in accs:
        cols = slice(col, col + acc.shape[1])
        col += acc.shape[1]
        if len(outs) == 1:
            outs[0][:, cols] = acc[...].astype(BF)
            continue
        for out, which in zip(outs, (core, 1 - core)):
            shards, sides, count = out.shape[:3]
            for n in range(shards * sides):
                row = pl.multiple_of((2 * n + which) * count, 8)
                out[n // sides, n % sides, :, cols] = acc[pl.ds(row, count)].astype(BF)


def taker(refs):
    refs = list(refs)

    def take(n):
        out = refs[:n]
        del refs[:n]
        return out

    return take


def back_first_kernel(parts, experts, slots, outs, ids_ref, *refs):
    take = taker(refs)
    (meta_ref,) = take(1)
    norm_refs = [meta_ref, take(parts), take(parts)]
    att_ref, res_ref, z_ref, wp_ref, vec_ref, router_ref = take(6)
    norm_refs += [att_ref, res_ref, z_ref, wp_ref, vec_ref, router_ref]
    (mask_ref,) = take(1)
    qkv_refs = take(3)
    lse_ref, normed_ref = take(2)
    w_refs = take(3)
    ga_ref, gres_ref, dn_ref, small_ref = take(4)
    grads_refs = take(outs)
    acc_proj, acc, acc_small, acc_router, gqkv = take(5)
    i = pl.program_id(0)

    @pl.when(i == 0)
    def _():
        for part in (acc_proj, acc, acc_small, acc_router):
            part[...] = jnp.zeros_like(part)

    accs = (acc_proj, acc_small, acc_router)
    gres_ref[0], ga_ref[0] = norm_part(parts, experts, slots, norm_refs, accs, ids_ref, i)
    dn_ref[0] = heads_part(
        0, mask_ref, qkv_refs, att_ref, ga_ref, lse_ref, normed_ref, w_refs, acc, acc_small, gqkv
    )

    @pl.when(i == pl.num_programs(0) - 1)
    def _():
        acc_small[8:16] = acc_router[...].T[0:8]
        small_ref[...] = acc_small[...]
        split_rows(grads_refs, (acc_proj, acc), ids_ref[0] % 2)


def back_second_kernel(parts, outs, ids_ref, *refs):
    take = taker(refs)
    (mask_ref,) = take(1)
    qkv_refs = take(3)
    att_ref, ga_ref, lse_ref, normed_ref = take(4)
    w_refs = take(3)
    small_in, dn_in, gres_ref, vec_ref = take(4)
    toks, gt_refs = take(parts), take(parts)
    grads_refs = take(outs)
    acc, acc_small, acc_turned, gqkv = take(4)
    i = pl.program_id(0)

    @pl.when(i == 0)
    def _():
        acc[...] = jnp.zeros_like(acc)
        acc_small[0:16] = small_in[...]
        acc_small[16:128] = jnp.zeros((112, acc_small.shape[1]), F32)

    dn = dn_in[0] + heads_part(
        1, mask_ref, qkv_refs, att_ref, ga_ref, lse_ref, normed_ref, w_refs, acc, acc_small, gqkv
    )
    x = rows_of(toks)
    vhat, r1 = stats(x)
    acc_small[0:1] += jnp.sum(dn * vhat, axis=0, keepdims=True)
    acc_small[1:2] += jnp.sum(dn, axis=0, keepdims=True)
    grad_tok = gres_ref[0] + norm_back(dn, vec_ref[0:1], vhat, r1)
    block = x.shape[0] // parts
    for j, ref in enumerate(gt_refs):
        ref[0] = grad_tok[j * block : (j + 1) * block].astype(BF)

    @pl.when(i == pl.num_programs(0) - 1)
    def _():
        acc_turned[...] = acc_small[...].T
        split_rows(grads_refs, (acc, acc_turned), ids_ref[0] % 2)


def assemble_kernel(ring_len, half, share, ids_ref, *refs):
    parts, (out_ref, vec_ref, router_ref) = refs[:-3], refs[-3:]
    ring_at, column = ids_ref[1] // 2, ids_ref[1] % 2
    core = ids_ref[0] % 2
    d = vec_ref.shape[1]
    vec = jnp.zeros((16, d), F32)
    at = 0
    for r in range(ring_len):
        for p in range(2):
            shard = lax.rem(ring_at + ring_len - r, ring_len) * 2 + (column ^ p)
            for c in range(2):
                row = pl.multiple_of((shard * 2 + (core ^ c)) * half, half)
                out_ref[pl.ds(row, half)] = parts[at][0:half]
                if c == 0:
                    few = parts[at][half : half + 8, 0:256].astype(F32)
                    few = jnp.concatenate([few[:, 0:128], few[:, 128:256]], axis=0).astype(BF)
                    source = lax.broadcasted_iota(jnp.int32, (128, d), 0)
                    target = lax.broadcasted_iota(jnp.int32, (128, d), 1) - shard * share
                    vec += nn(few, ((source == target) & (source < share)).astype(BF))
                at += 1
    vec_ref[...] = vec
    fill = jnp.zeros((120, d), F32)
    router_ref[...] = jnp.concatenate([vec[8:16], fill], axis=0).T.astype(BF)


def whole(shape):
    return pl.BlockSpec(shape, lambda *_: (0,) * len(shape))


def body(
    tokens,
    key_mask,
    routes,
    out_grad,
    norm1_gain,
    norm1_bias,
    w_qkv,
    bias_q,
    bias_v,
    w_proj,
    bias_proj,
    norm2_gain,
    norm2_bias,
    w_router,
    w_hidden,
    bias_hidden,
    w_expert_out,
    bias_expert_out,
):
    images, block_len, d = tokens.shape
    parts = lax.axis_size("seq")
    shards = lax.axis_size("fsdp")
    experts = parts
    ring_len = shards // 2
    own = images // parts
    sub = own // TILE
    tiles = parts * sub
    pad = -(-block_len // 8) * 8
    length = parts * pad
    slots = parts * CAP
    rows = TILE * slots
    fs = w_hidden.shape[1]
    share = d // shards
    half = share // 2
    me = lax.axis_index("seq")
    rank = lax.axis_index("fsdp")
    ring_at, column = rank // 2, rank % 2
    core = me % 2
    ids = jnp.stack([me, rank]).astype(jnp.int32)

    def to_seq(v, k):
        return lax.ppermute(v, "seq", [(n, n ^ k) for n in range(parts)])

    def to_column(v):
        return lax.ppermute(v, "fsdp", [(n, n ^ 1) for n in range(shards)])

    def round_ring(v):
        return lax.ppermute(v, "fsdp", [(n, (n + 2) % shards) for n in range(shards)])

    def gate(*values):
        return lax.optimization_barrier(values)

    def after(v, *others):
        return lax.optimization_barrier((v,) + others)[0]

    def index(v, at, axis=0):
        return lax.dynamic_index_in_dim(v, at, axis, keepdims=False)

    def share_seq(v):
        two = to_seq(v, 2)
        return [v, to_seq(v, 1), two, to_seq(two, 1)]

    order = jnp.arange(shards, dtype=jnp.int32)
    spot = 2 * ((ring_at - order // 2) % ring_len) + (order % 2 ^ column)

    wide = 4 * d
    masters = (
        norm1_gain,
        norm1_bias,
        bias_q,
        bias_v,
        bias_proj,
        norm2_gain,
        norm2_bias,
    )
    few = jnp.concatenate([jnp.stack(masters), bias_expert_out, w_router.T], axis=0)
    few = jnp.pad(few, ((0, 16 - few.shape[0]), (0, 128 - share))).astype(BF)
    few_row = jnp.concatenate([few[:8], few[8:]], axis=1)
    few_row = jnp.pad(few_row, ((0, 0), (0, wide - 256)))
    both = jnp.concatenate([w_qkv, w_proj], axis=1)

    def half_rows(which):
        part = lax.dynamic_slice_in_dim(both, which * half, half, 0).astype(BF)
        return jnp.concatenate([part, few_row], axis=0)

    now, now_core = half_rows(core), half_rows(1 - core)
    tokens, routes, out_grad = lax.optimization_barrier((tokens, routes, out_grad, now))[:3]

    grow = ((0, 0), (0, pad - block_len), (0, 0))
    padded = jnp.pad(tokens, grow)
    pieces = [lax.dynamic_slice_in_dim(padded, (me ^ j) * own, own, 0) for j in range(parts)]
    toks = [pieces[j] if j == 0 else to_seq(pieces[j], j) for j in range(parts)]

    spare = jnp.zeros((15, d), F32)
    def build_pack():
      return jnp.concatenate(
        [
            w_hidden[0],
            w_expert_out[0],
            jnp.pad(bias_hidden, ((0, 0), (0, d - fs))),
            spare,
        ],
        axis=0,
    ).astype(BF)
    own_live = lax.dynamic_slice_in_dim(key_mask, me * block_len, block_len, 1)

    def build_final():
        return jnp.pad(out_grad * own_live[:, :, None].astype(BF), grow)


    flat = jnp.pad(
        routes.reshape(images, block_len * TOP), ((0, 0), (0, (-block_len * TOP) % 128))
    )
    blocks = jnp.stack(share_seq(flat))[:, :, : block_len * TOP]
    blocks = blocks.reshape(parts, images, block_len, TOP)
    names = me ^ jnp.arange(parts, dtype=jnp.int32)
    hit = jnp.any(blocks[..., None] == names, axis=3)
    ahead = (
        lax.broadcasted_iota(jnp.int32, (block_len, block_len), 0)
        < lax.broadcasted_iota(jnp.int32, (block_len, block_len), 1)
    ).astype(BF)
    ranks = jnp.einsum(
        "jitk,tu->jiuk", hit.astype(BF), ahead, preferred_element_type=F32
    ).astype(jnp.int32)
    in_image = jnp.where(hit, ranks + (names * CAP)[:, None, None, None], -1)
    in_image = jnp.pad(
        in_image, ((0, 0), (0, 0), (0, pad - block_len), (0, 0)), constant_values=-1
    )
    own_meta = lax.dynamic_slice_in_dim(in_image, me * own, own, 1)
    own_meta = own_meta.transpose(1, 0, 2, 3).reshape(own, length, parts)
    expert_slot = in_image[..., 0]

    def by_image(order):
        out = jnp.concatenate([expert_slot[j] for j in order], axis=-1)
        return out.reshape(images, 1, length)

    slot_rows = [by_image([j ^ k for j in range(parts)]) for k in range(parts)]
    within = (jnp.arange(images, dtype=jnp.int32) % TILE) * CAP
    mix_slot = jnp.where(hit[0], ranks[0] + within[:, None, None], -1)
    mix_meta = jnp.concatenate([mix_slot, own_live[:, :, None]], axis=-1)
    mix_meta = jnp.pad(
        mix_meta, ((0, 0), (0, pad - block_len), (0, 8 - parts - 1)), constant_values=-1
    )
    seen = lax.dynamic_slice_in_dim(key_mask, me * own, own, 0).reshape(own, parts, block_len)
    seen = jnp.stack([index(seen, me ^ j, 1) for j in range(parts)], axis=1)
    seen = jnp.pad(seen, ((0, 0), (0, 0), (0, pad - block_len))).reshape(own, 1, length)
    mask_bias = jnp.where(seen > 0, 0.0, NEG).astype(F32)

    at = lax.broadcasted_iota(jnp.int32, (rows, rows), 0)
    image_at, rank_at = (at % (TILE * CAP)) // CAP, at % CAP
    source = image_at * slots + ((at // (TILE * CAP)) ^ me) * CAP + rank_at
    reorder = (lax.broadcasted_iota(jnp.int32, (rows, rows), 1) == source).astype(BF)

    halves, others = [], []
    for r in range(ring_len):
        if r:
            if r == 2:
                now, w_hidden, w_expert_out, out_grad, others[0] = gate(
                    now, w_hidden, w_expert_out, out_grad, others[0], *pieces
                )[:5]
                pack, final = build_pack(), build_final()
            elif r == 3:
                now, others[1], pack, final, *toks[1:] = gate(
                    now, others[1], pack, final, *toks[1:]
                )
            elif r > 3:
                now, others[r - 2] = gate(now, others[r - 2])
            now = round_ring(now)
            arrived = now
            if r == ring_len - 1:
                grads_in = [final, None, to_seq(final, 2), None]
                now, mask_bias, own_meta, mix_meta, reorder, *slot_rows = gate(
                    now, mask_bias, own_meta, mix_meta, reorder, *slot_rows
                )
            now_core = to_seq(now, 1)
        others.append(to_column(now))
        halves.append((now, now_core))
    halves = [
        part for pair, other in zip(halves, others) for part in (*pair, other, to_seq(other, 1))
    ]
    if half % 16 == 0:
        weights, vec, router = pl.pallas_call(
            functools.partial(assemble_kernel, ring_len, half, share),
            grid_spec=pltpu.PrefetchScalarGridSpec(
                num_scalar_prefetch=1,
                grid=(1,),
                in_specs=[whole((half + 8, wide))] * len(halves),
                out_specs=[whole((d, wide)), whole((16, d)), whole((d, 128))],
            ),
            out_shape=[
                jax.ShapeDtypeStruct((d, wide), BF),
                jax.ShapeDtypeStruct((16, d), F32),
                jax.ShapeDtypeStruct((d, 128), BF),
            ],
            compiler_params=params(),
            cost_estimate=cost(0.01),
            name="assemble",
        )(ids, *halves)
    else:
        place = jnp.arange(shards * 2, dtype=jnp.int32)
        place = spot[place // 2] * 2 + (place % 2 ^ core)
        weights = jnp.stack([part[:half] for part in halves])[place].reshape(d, wide)
        vec = jnp.stack([part[half:, :256] for part in halves[::2]])[spot]
        vec = vec.reshape(shards, 8, 2, 128)[..., :share].transpose(2, 1, 0, 3)
        vec = vec.reshape(16, d).astype(F32)
        router = jnp.pad(vec[8:16].T, ((0, 0), (0, 120))).astype(BF)

    pack = after(pack, arrived, *others)
    chunks = [(pack, to_column(pack)), (round_ring(pack),)]

    per_image = lambda *tail: pl.BlockSpec((1,) + tail, lambda i: (i,) + (0,) * len(tail))
    made = pl.pallas_call(
        functools.partial(fwd_kernel, parts),
        grid=(own,),
        in_specs=[per_image(pad, d)] * parts
        + [per_image(1, length), whole((d, wide)), whole((16, d))],
        out_specs=[
            per_image(length, 3 * d),
            per_image(length, d),
            per_image(length, 128),
            per_image(length, d),
            per_image(length, d),
            per_image(length, d),
        ]
        + [per_image(pad, d)] * parts,
        out_shape=[
            jax.ShapeDtypeStruct((own, length, 3 * d), BF),
            jax.ShapeDtypeStruct((own, length, d), BF),
            jax.ShapeDtypeStruct((own, length, 128), F32),
            jax.ShapeDtypeStruct((own, length, d), F32),
            jax.ShapeDtypeStruct((own, length, d), BF),
            jax.ShapeDtypeStruct((own, length, d), BF),
        ]
        + [jax.ShapeDtypeStruct((own, pad, d), BF)] * parts,
        compiler_params=params(),
        cost_estimate=cost(0.01),
        name="block_forward",
    )(*toks, mask_bias, weights, vec)
    *made, first_other, second, grads_in[2] = gate(*made, chunks[0][1], chunks[1][0], grads_in[2])
    chunks = [(chunks[0][0], first_other), (second, to_column(second))]
    qkv, attended, lse, residual, z_own, normed = made[:6]
    res_pieces = list(made[6:])

    grads_in[1], grads_in[3] = to_seq(final, 1), to_seq(grads_in[2], 1)

    def tile_spec(shape, index_map):
        return pl.BlockSpec(shape, index_map)

    grad_slots = pl.pallas_call(
        functools.partial(gather_grads_kernel, slots, parts),
        grid_spec=pltpu.PrefetchScalarGridSpec(
            num_scalar_prefetch=1,
            grid=(parts, sub),
            in_specs=[
                tile_spec((TILE, 1, length), lambda k, u, ids: ((ids[0] ^ k) * sub + u, 0, 0))
            ]
            + [tile_spec((TILE, pad, d), lambda k, u, ids: ((ids[0] ^ k) * sub + u, 0, 0))]
            * parts,
            out_specs=tile_spec((1, rows, d), lambda k, u, ids: (k * sub + u, 0, 0)),
        ),
        out_shape=jax.ShapeDtypeStruct((tiles, rows, d), BF),
        compiler_params=params(),
        cost_estimate=cost(0.01),
        name="grad_slots",
    )(ids, slot_rows[0], *grads_in)

    def add(*terms):
        return sum(term.astype(F32) for term in terms)

    def ring_sum(moving, r):
        terms = (packs[r][0], crossed[r]) + (() if moving is None else (moving,))
        return add(*terms)

    z_far = to_seq(z_own, 2)
    z_rows = [z_own, to_seq(z_own, 1), z_far, None]
    if ring_len > 2:
        chunks.append((round_ring(second),))
    x_rows = gr_rows = None
    for k in range(parts):
        chain = () if k == 0 else (x_rows, gr_rows)
        if k == 2:
            z_far, x_rows, gr_rows, second_other, *rest = gate(
                z_far, x_rows, gr_rows, chunks[1][1], *[c[0] for c in chunks[2:]]
            )
            chunks[1] = (chunks[1][0], second_other)
            for r in range(2, ring_len):
                part = rest[0] if r == 2 else round_ring(part)
                chunks[r:] = [(part, to_column(part) if r < ring_len - 1 else part)]
            z_rows[2:] = [z_far, to_seq(z_far, 1)]
            chain = (x_rows, gr_rows)
        x_rows, gr_rows = pl.pallas_call(
            functools.partial(gather_rows_kernel, slots, experts),
            grid_spec=pltpu.PrefetchScalarGridSpec(
                num_scalar_prefetch=1,
                grid=(sub,),
                in_specs=[
                    tile_spec(
                        (TILE, 1, length), lambda u, ids, k=k: ((ids[0] ^ k) * sub + u, 0, 0)
                    ),
                    tile_spec((TILE, length, d), lambda u, ids: (u, 0, 0)),
                    tile_spec((1, rows, d), lambda u, ids, k=k: (k * sub + u, 0, 0)),
                    whole((d, 128)),
                ]
                + [pl.BlockSpec(memory_space=pl.ANY)] * len(chain),
                out_specs=[
                    tile_spec((1, rows, d), lambda u, ids, k=k: (k * sub + u, 0, 0)),
                    tile_spec((1, rows, d), lambda u, ids, k=k: (k * sub + u, 0, 0)),
                ],
            ),
            out_shape=[jax.ShapeDtypeStruct((tiles, rows, d), BF)] * 2,
            input_output_aliases={5: 0, 6: 1} if chain else {},
            compiler_params=params(),
            cost_estimate=cost(0.01),
            name="slot_rows",
        )(ids, slot_rows[k], z_rows[k], grad_slots, router, *chain)

    tile3 = pl.BlockSpec((1, rows, d), lambda t, *_: (t, 0, 0))
    pack_rows = 2 * fs + 16
    acc_out = acc_gx = None
    packs = []
    crossed = {}
    moving = None
    for r in range(ring_len):
        e0, e1 = chunks[r]
        is_first, is_last = r == 0, r == ring_len - 1
        operands = [e0, e1, x_rows, gr_rows]
        in_specs = [
            whole((pack_rows, d)),
            whole((pack_rows, d)),
            tile3,
            tile3,
        ]
        aliases = {}
        if not is_first:
            operands += [acc_out, acc_gx]
            in_specs += [tile3, tile3]
            aliases = {4: 2} if is_last else {4: 2, 5: 3}
        pack_shape = jax.ShapeDtypeStruct((pack_rows, d), BF)
        out_specs = [whole((pack_rows, d)), whole((pack_rows, d)), tile3, tile3]
        acc_shape = jax.ShapeDtypeStruct((tiles, rows, d), F32)
        out_shape = [pack_shape, pack_shape, acc_shape, acc_shape]
        if is_last:
            operands += [grad_slots, vec]
            in_specs += [tile3, whole((16, d))]
            out_specs[3:] = [
                pl.BlockSpec(
                    (TILE, slots + 8, d), lambda t, k=k: (jnp.clip(t - k * sub, 0, sub - 1), 0, 0)
                )
                for k in range(parts)
            ]
            out_shape[3:] = [jax.ShapeDtypeStruct((own, slots + 8, d), BF)] * parts
        made = pl.pallas_call(
            functools.partial(expert_kernel, is_first, is_last, slots, experts, fs),
            grid_spec=pltpu.PrefetchScalarGridSpec(
                num_scalar_prefetch=0,
                grid=(tiles,),
                in_specs=in_specs,
                out_specs=out_specs,
                scratch_shapes=[
                    pltpu.VMEM((2 * fs, d), BF),
                    pltpu.VMEM((2 * fs, d), BF),
                    pltpu.VMEM((2 * fs, d), F32),
                    pltpu.VMEM((2 * fs, d), F32),
                    pltpu.VMEM((8, 2 * fs), F32),
                    pltpu.VMEM((8, d), F32),
                    pltpu.VMEM((8, 2 * fs), F32),
                ],
            ),
            out_shape=out_shape,
            input_output_aliases=aliases,
            compiler_params=params(),
            cost_estimate=cost(50),
            name="expert_pair",
        )(*operands)
        ready = {}
        if r == 0:
            ready = {("in", q, p): chunks[q][p] for q in range(2, ring_len) for p in (0, 1)}
            ready.pop(("in", ring_len - 1, 1), None)
        elif r == 1:
            ready[("in", ring_len - 1, 1)] = chunks[ring_len - 1][1]
            ready.update({("piece", j): res_pieces[j] for j in range(1, parts)})
        else:
            ready[("out", r - 1, 1)] = crossed[r - 1]
            if moving is not None:
                ready["moving"] = moving
            if r == 2:
                ready.update({("res", j): res_in[j] for j in range(1, parts)})
        values = gate(*made, *ready.values())
        made, ready = values[: len(made)], dict(zip(ready, values[len(made) :]))
        for key, value in ready.items():
            if key == "moving":
                moving = value
            elif key[0] == "in":
                chunks[key[1]] = tuple(value if p == key[2] else chunks[key[1]][p] for p in (0, 1))
            elif key[0] == "out":
                crossed[key[1]] = value
            elif key[0] == "piece":
                res_pieces[key[1]] = value
            else:
                res_in[key[1]] = value
        packs.append(made[:2])
        acc_out, acc_gx = made[2:4]
        if r == 0 and ring_len > 2:
            chunks[ring_len - 1] = (chunks[ring_len - 1][0], to_column(chunks[ring_len - 1][0]))
        if r >= 1:
            crossed[r] = to_column(packs[r][1])
        if 2 <= r < ring_len - 1:
            moving = round_ring(ring_sum(moving, r - 1).astype(BF))
        if r == 1:
            res_in = [res_pieces[0]] + [to_seq(res_pieces[j], j) for j in range(1, parts)]
    gx = made[3 : 3 + parts]

    gx_in = [gx[k] if k == 0 else to_seq(gx[k], k) for k in range(parts)]
    packs[ring_len - 2] = (after(packs[ring_len - 2][0], gx_in[1]), None)
    moving = round_ring(ring_sum(moving, ring_len - 2).astype(BF))
    mixed = pl.pallas_call(
        functools.partial(weigh_kernel, slots, experts),
        grid_spec=pltpu.PrefetchScalarGridSpec(
            num_scalar_prefetch=1,
            grid=(tiles,),
            in_specs=[
                tile3,
                tile3,
                whole((d, 128)),
                whole((16, d)),
                whole((rows, rows)),
            ],
            out_specs=[
                *[pl.BlockSpec((1, TILE * CAP, d), lambda t, *_: (t, 0, 0))] * parts,
            ],
        ),
        out_shape=[
            *[jax.ShapeDtypeStruct((tiles, TILE * CAP, d), BF)] * parts,
        ],
        compiler_params=params(),
        cost_estimate=cost(50),
        name="weigh",
    )(ids, acc_out, x_rows, router, vec, reorder)
    last = ring_len - 1
    own_meta, moving, crossed[last], *rest = gate(
        own_meta, moving, crossed[last], *gx_in[1:], *mixed
    )
    gx_in[1:], mixed = rest[: parts - 1], rest[parts - 1 :]
    mixed_in = [mixed[0]] + [to_seq(mixed[k], k) for k in range(1, parts)]
    packs[last] = (after(packs[last][0], mixed_in[1]), None)
    moving = round_ring(ring_sum(moving, last).astype(BF))
    crossed[0] = to_column(after(packs[0][1], own_meta))

    side = me // 2
    quarter = share // 4

    def shift_ring(v, k):
        return lax.ppermute(v, "fsdp", [(n, (n + 2 * k) % shards) for n in range(shards)])

    def core_pair(made):
        if len(made) == 1:
            split = made[0].reshape(shards, 2, 2, quarter, made[0].shape[-1])
            made = index(split, core, 2), index(split, 1 - core, 2)
        return made[0], to_seq(made[1], 1)

    def over_y(keep, come=None):
        pair = [v for v in (keep, come) if v is not None]
        send = add(*[index(v, 1 - side, 1) for v in pair]).astype(BF)
        return add(*[index(v, side, 1) for v in pair], to_seq(send, 2)).astype(BF)

    def over_x(keep, come=None):
        pair = [v.reshape(ring_len, 2, *v.shape[1:]) for v in (keep, come) if v is not None]
        send = add(*[index(v, 1 - column, 1) for v in pair]).astype(BF)
        return add(*[index(v, column, 1) for v in pair], to_column(send)).astype(BF)

    def over_ring(v):
        far = [
            shift_ring(index(v, (ring_at + k) % ring_len), k) for k in range(1, ring_len)
        ]
        return add(index(v, ring_at), *far).astype(BF)

    def in_order(pieces):
        a, b, c, e = pieces
        near = [jnp.where(core == 0, a, b), jnp.where(core == 0, b, a)]
        far = [jnp.where(core == 0, c, e), jnp.where(core == 0, e, c)]
        front = [jnp.where(side == 0, u, v) for u, v in zip(near, far)]
        back = [jnp.where(side == 0, v, u) for u, v in zip(near, far)]
        return jnp.concatenate(front + back, axis=0)

    def spread_rows(v):
        return in_order([v] + [to_seq(v, k) for k in range(1, parts)]).astype(F32)

    image3 = lambda *tail: pl.BlockSpec((1,) + tail, lambda i, *_: (i,) + (0,) * len(tail))
    width = d // 2
    column3 = lambda n: pl.BlockSpec((1, length, width), lambda i, *_: (i, 0, n))
    weight3 = lambda n: pl.BlockSpec((d, width), lambda i, *_: (0, n))
    partial_shape = jax.ShapeDtypeStruct((own, length, d), F32)
    def grad_outs(cols):
        if quarter % 8:
            return [whole((d, cols))], [jax.ShapeDtypeStruct((d, cols), BF)]
        shape = (shards, 2, quarter, cols)
        return [whole(shape)] * 2, [jax.ShapeDtypeStruct(shape, BF)] * 2

    grad_specs, grad_shapes = grad_outs(d + 3 * width)
    grad_att, grad_res, after_first, small, *first = pl.pallas_call(
        functools.partial(back_first_kernel, parts, experts, slots, len(grad_specs)),
        grid_spec=pltpu.PrefetchScalarGridSpec(
            num_scalar_prefetch=1,
            grid=(own,),
            in_specs=[image3(length, parts)]
            + [image3(slots + 8, d)] * parts
            + [pl.BlockSpec((1, pad, d), lambda i, ids: (ids[0] * own + i, 0, 0))] * parts
            + [
                image3(length, d),
                image3(length, d),
                image3(length, d),
                pl.BlockSpec((d, d), lambda i, ids: (0, 3)),
                whole((16, d)),
                whole((d, 128)),
                image3(1, length),
                column3(0),
                column3(2),
                column3(4),
                image3(length, 128),
                image3(length, d),
                weight3(0),
                weight3(2),
                weight3(4),
            ],
            out_specs=[
                image3(length, d),
                image3(length, d),
                image3(length, d),
                whole((16, d)),
                *grad_specs,
            ],
            scratch_shapes=[
                pltpu.VMEM((d, d), F32),
                pltpu.VMEM((d, 3 * width), F32),
                pltpu.VMEM((16, d), F32),
                pltpu.VMEM((d, 128), F32),
                pltpu.VMEM((length, 3 * width), BF),
            ],
        ),
        out_shape=[
            jax.ShapeDtypeStruct((own, length, d), BF),
            partial_shape,
            partial_shape,
            jax.ShapeDtypeStruct((16, d), F32),
            *grad_shapes,
        ],
        compiler_params=params(),
        cost_estimate=cost(50),
        name="back_first",
    )(
        ids,
        own_meta,
        *gx_in,
        *grads_in,
        attended,
        residual,
        z_own,
        weights,
        vec,
        router,
        mask_bias,
        qkv,
        qkv,
        qkv,
        lse,
        normed,
        weights,
        weights,
        weights,
    )
    grad_att, grad_res, after_first, small, moving, crossed[0], *rest = gate(
        grad_att, grad_res, after_first, small, moving, crossed[0], *mixed_in[1:], *first
    )
    mixed_in[1:], first = rest[: parts - 1], rest[parts - 1 :]
    first = core_pair(first)
    grad_specs, grad_shapes = grad_outs(3 * width + 128)
    made = pl.pallas_call(
        functools.partial(back_second_kernel, parts, len(grad_specs)),
        grid_spec=pltpu.PrefetchScalarGridSpec(
        num_scalar_prefetch=1,
        grid=(own,),
        in_specs=[
            image3(1, length),
            column3(1),
            column3(3),
            column3(5),
            image3(length, d),
            image3(length, d),
            image3(length, 128),
            image3(length, d),
            weight3(1),
            weight3(3),
            weight3(5),
            whole((16, d)),
            image3(length, d),
            image3(length, d),
            whole((16, d)),
        ]
        + [image3(pad, d)] * parts,
        out_specs=[image3(pad, d)] * parts + grad_specs,
        scratch_shapes=[
            pltpu.VMEM((d, 3 * width), F32),
            pltpu.VMEM((128, d), F32),
            pltpu.VMEM((d, 128), F32),
            pltpu.VMEM((length, 3 * width), BF),
        ],
        ),
        out_shape=[jax.ShapeDtypeStruct((own, pad, d), BF)] * parts + grad_shapes,
        compiler_params=params(),
        cost_estimate=cost(50),
        name="back_second",
    )(
        ids,
        mask_bias,
        qkv,
        qkv,
        qkv,
        attended,
        grad_att,
        lse,
        normed,
        weights,
        weights,
        weights,
        small,
        after_first,
        grad_res,
        vec,
        *toks,
    )
    token_pieces, second = made[:parts], made[parts:]
    far_first, moving, crossed[0], *rest = gate(
        first[1], moving, crossed[0], *token_pieces, *mixed_in[1:], *second
    )
    first = (first[0], far_first)
    token_pieces, mixed_in[1:], second = (
        rest[:parts],
        rest[parts : 2 * parts - 1],
        rest[2 * parts - 1 :],
    )

    image_block = pl.BlockSpec(
        (TILE, block_len, d), lambda j, u, ids: ((ids[0] ^ j) * sub + u, 0, 0)
    )
    output = pl.pallas_call(
        functools.partial(combine_kernel, parts),
        grid_spec=pltpu.PrefetchScalarGridSpec(
            num_scalar_prefetch=1,
            grid=(parts, sub),
            in_specs=[
                pl.BlockSpec((TILE, pad, 8), lambda j, u, ids: ((ids[0] ^ j) * sub + u, 0, 0))
            ]
            + [pl.BlockSpec((TILE, pad, d), lambda j, u, ids: (u, 0, 0))] * parts
            + [
                pl.BlockSpec(
                    (1, TILE * CAP, d), lambda j, u, ids, k=k: ((j ^ k) * sub + u, 0, 0)
                )
                for k in range(parts)
            ],
            out_specs=image_block,
        ),
        out_shape=jax.ShapeDtypeStruct((images, block_len, d), BF),
        compiler_params=params(),
        cost_estimate=cost(50),
        name="combine",
    )(ids, mix_meta, *res_in, *mixed_in)

    first_x = over_x(*first)
    second = core_pair(second)
    second_y = over_y(*second)
    tokens_in = [token_pieces[j] if j == 0 else to_seq(token_pieces[j], j) for j in range(parts)]
    first_x, second_y, output, *tokens_in = gate(first_x, second_y, output, *tokens_in)
    first_own, second_x = over_y(first_x), over_x(second_y)
    grad_tokens = in_order(tokens_in)[:, :block_len]
    first_own, second_x, grad_tokens = gate(first_own, second_x, grad_tokens)
    both_x = jnp.concatenate([first_own, second_x], axis=-1)
    total = ring_sum(moving, 0)
    grad_hidden = total[None, :fs]
    grad_expert_out = total[None, fs : 2 * fs]
    grad_hidden_bias = total[2 * fs : 2 * fs + 1, :fs]
    grad_out_bias = lax.dynamic_slice(total, (2 * fs + 1, rank * share), (1, share))
    own_rows = over_ring(both_x)
    mine = spread_rows(own_rows)
    grad_proj = mine[:, :d]
    at_b, at_small = d + 3 * width, d + 6 * width
    grad_qkv = jnp.concatenate(
        [
            mine[:, start + n * width : start + (n + 1) * width]
            for n in range(3)
            for start in (d, at_b)
        ],
        axis=1,
    )
    small = mine[:, at_small : at_small + 16].T
    grad_router = mine[:, at_small + 8 : at_small + 8 + experts]

    return (
        output,
        grad_tokens,
        small[0],
        small[1],
        grad_qkv,
        small[2],
        small[3],
        grad_proj,
        small[4],
        small[5],
        small[6],
        grad_router,
        grad_hidden,
        grad_hidden_bias,
        grad_expert_out,
        grad_out_bias,
    )


def solution(mesh):
    in_specs = (
        P("fsdp", "seq", None),
        P("fsdp", None),
        P("fsdp", "seq", None),
        P("fsdp", "seq", None),
        P("fsdp"),
        P("fsdp"),
        P("fsdp", None),
        P("fsdp"),
        P("fsdp"),
        P("fsdp", None),
        P("fsdp"),
        P("fsdp"),
        P("fsdp"),
        P("fsdp", None),
        P("seq", "fsdp", None),
        P("seq", "fsdp"),
        P("seq", "fsdp", None),
        P("seq", "fsdp"),
    )
    out_specs = (
        P("fsdp", "seq", None),
        P("fsdp", "seq", None),
        P("fsdp"),
        P("fsdp"),
        P("fsdp", None),
        P("fsdp"),
        P("fsdp"),
        P("fsdp", None),
        P("fsdp"),
        P("fsdp"),
        P("fsdp"),
        P("fsdp", None),
        P("seq", "fsdp", None),
        P("seq", "fsdp"),
        P("seq", "fsdp", None),
        P("seq", "fsdp"),
    )
    return jax.shard_map(body, mesh=mesh, in_specs=in_specs, out_specs=out_specs, check_vma=False)
```
